32 devices in a mesh: rep: 2 (over x), dp: 1, tensor: 16 (over z, y, core).
Axes of the slice: x: 2, y: 2, z: 4, core: 2. Of those that a mesh axis runs over, the one named last changes fastest.
Arguments:
- hidden: bfloat16 [1024, 8192], P(('rep', 'dp', 'tensor')), parts along dimension 0, may hold values from -6 to 6
- pre_gain: bfloat16 [8192], replicated, may hold values from 0.099609375 to 1.8984375
- in_x: bfloat16 [8192, 8192], P(('dp', 'tensor')), may hold values from -0.0625 to 0.0625
- in_z: bfloat16 [8192, 8192], P(('dp', 'tensor')), may hold values from -0.2 to 0.2
- conv_x: bfloat16 [8192, 4], P(('dp', 'tensor')), may hold values from -3 to 3
- conv_bc: bfloat16 [1024, 4], replicated, may hold values from -3 to 3
- bc_weight: bfloat16 [1024, 8192], P('tensor'), may hold values from -0.0625 to 0.0625
- dt_weight: bfloat16 [128, 8192], P(('dp', 'tensor')), may hold values from -0.0625 to 0.0625
- dt_bias: bfloat16 [128], P(('dp', 'tensor')), may hold values from -3 to 0.5
- decay_rate: bfloat16 [128], P(('dp', 'tensor')), may hold values from 0.0049743652 to 2
- skip: bfloat16 [128], P(('dp', 'tensor')), may hold values from 0.29882812 to 1.5
- norm_gain: bfloat16 [8192], P(('dp', 'tensor')), may hold values from 0.099609375 to 1.8984375
- out_weight: bfloat16 [8192, 8192], P(('dp', 'tensor')), may hold values from -0.0625 to 0.0625
- segment_ids: int32 [2, 512], P(('rep', 'dp')), parts along dimension 0, may hold values from 0 to 7, never falling along the last dimension, each value on 1 to 256 neighbouring positions
- destination: int32 [1024, 1], P(('rep', 'dp', 'tensor')), parts along dimension 0, may hold values from 0 to 15; in each aligned block of 32 rows (0 to 31, 32 to 63, ...) at most 2 rows name the same one
Outputs:
- layer_out: bfloat16 [1024, 8192], P(('rep', 'dp', 'tensor')), parts along dimension 0
- packed: bfloat16 [1024, 16384], P(('rep', 'dp', 'tensor')), parts along dimension 0
The draws below stay inside these ranges and needn't reach their ends.
There are 2 independent parts, one for each index of `rep`. The reference program is written for one: setup_inputs(seed, part) draws one part's arguments, and reference() takes and returns one part's arrays. A program takes and returns all parts, laid end to end along the dimension named above; an argument that names none is the same for every part. Nothing has to cross between parts.
Inputs may be any that keep to these rules, and one draw needn't show every extreme that they name: `destination`: among the 32 rows of one device no trainer shard is named more than 2 times, a bound that some block reaches. `segment_ids`: each row of 512 positions holds 8 sequences numbered 0 to 7 in order, each 1 to 256 positions long.
All inputs are finite; a program needn't handle non-finite values.
Results may differ from the reference program's by a relative error of at most 0.014.
Values may be sent and summed in bfloat16 or wider, within the bound.
No kernel may reach another device: no remote copies, remote signals or barrier semaphores. Data moves between devices by JAX's collectives and lax.ppermute only.
A program may use at most 128 MiB of HBM per device.

```python
import math
import jax
import jax.numpy as jnp
import numpy as np
from jax import lax

D = 8192
HEAD_DIM = 64
INNER = 8192
HEADS = 128
STATE = 128
GROUPS = 4
CONV_K = 4
BLOCK = 128
CAP = 2
TOK_DEV = 512
DP_GROUPS = 1
TOKENS = 512
ROWS_DEV = 32
SHARDS = 16
SLOTS = 512


def draw_in_z(key, part):
    key = jax.random.fold_in(key, 7)
    ramp = 1.0 + 2.0 * jnp.arange(INNER, dtype=jnp.float32)[:, None] / (INNER - 1)
    base = jnp.clip(jax.random.normal(key, (INNER, D), jnp.float32), -6.0, 6.0)
    return jnp.clip(base * ramp * D ** (-0.5), -0.199, 0.199).astype(jnp.bfloat16)


def levels(own_key, dims, split, least, high):
    loudness = 1.0
    for axis_at, shards_of in split:
        heights = jax.random.uniform(jax.random.fold_in(jax.random.fold_in(own_key, 6), axis_at), (shards_of,), jnp.float32, least / len(split), high / len(split))
        loudness = loudness * jnp.repeat(jnp.exp(heights), dims[axis_at] // shards_of).reshape((-1,) + (1,) * (len(dims) - 1 - axis_at))
    return loudness


def profile(count, total, bound, slope):
    weights = [(1 << 20) // math.isqrt(rank ** slope) + 1 for rank in range(2, count + 1)]
    rest, given = total - bound - (count - 1), [1] * (count - 1)
    while rest > 0:
        free = [i for i in range(count - 1) if given[i] < bound]
        mass, left = sum([weights[i] for i in free]), rest
        for i in free:
            more = min(bound - given[i], max(1, left * weights[i] // mass), rest)
            given[i] = given[i] + more
            rest = rest - more
    return np.array([bound] + given)


def uneven_parts(own_key, number_of, total, bound, slope):
    if number_of == 2:
        one = jax.random.randint(own_key, (), max(1, total - bound), min(bound, total - 1) + 1)
        return jnp.stack([one, total - one])
    tallies = jnp.asarray(profile(number_of, total, bound, slope), jnp.int32)
    pairs = (number_of - 1) // 2
    source_of, sink = tallies[1:1 + 2 * pairs:2], tallies[2:2 + 2 * pairs:2]
    room = jnp.minimum(source_of - 1, bound - sink)
    moved = jax.random.randint(jax.random.fold_in(own_key, 1), (pairs,), 0, 1 << 20) % (room + 1)
    tallies = tallies.at[1:1 + 2 * pairs:2].set(source_of - moved).at[2:2 + 2 * pairs:2].set(sink + moved)
    return tallies[jax.random.permutation(jax.random.fold_in(own_key, 2), number_of)]


def assign_block(own_key, own, number, rows, number_of, top, limit, skew):
    ranking = jax.random.permutation(own_key, number_of)
    crowded, common = portions_of(number_of, rows * top, limit, skew, True), portions_of(number_of, rows * top, limit, skew, False)
    places = jnp.arange(number_of)

    def named(lengths, rotation):
        used = int((lengths > 0).sum())
        fixed = max(1, used // 4)
        moved = fixed + (places - fixed + rotation * (used - fixed)) % max(1, number_of - fixed)
        return jnp.zeros((number_of,), jnp.int32).at[ranking[jnp.where(places < fixed, places, moved)]].set(jnp.asarray(lengths, jnp.int32))

    lengths = jnp.where(number % 4 == 0, named(crowded, number // 4), named(common, number - number // 4 - 1))
    mixed = jax.random.permutation(jax.random.fold_in(own, 3), number_of)
    donor, taker = mixed[0:number_of // 2 * 2:2], mixed[1:number_of // 2 * 2:2]
    room = jnp.minimum(lengths[donor] - 1, limit - lengths[taker]) // 2
    room = jnp.where((donor == ranking[0]) | (taker == ranking[0]) | (lengths[taker] == 0), 0, jnp.maximum(room, 0))
    moved = jax.random.randint(jax.random.fold_in(own, 4), (number_of // 2,), 0, 1 << 20) % (room + 1)
    lengths = lengths.at[donor].add(-moved).at[taker].add(moved)
    members = jnp.searchsorted(jnp.cumsum(lengths), jnp.arange(rows * top), side="right").astype(jnp.int32)
    grid = members.reshape(top, rows).T
    grid = grid[jax.random.permutation(jax.random.fold_in(own, 1), rows)]
    rotation = jax.random.randint(jax.random.fold_in(own, 2), (rows, 1), 0, top)
    return jnp.take_along_axis(grid, (jnp.arange(top)[None, :] + rotation) % top, axis=1)


def portions_of(number_of, total, reach, skew, full):
    loads = [(1 << 20) // math.isqrt(standing ** skew) + 1 for standing in range(1, number_of + 1)]
    largest = reach if full else min(reach, max(-(-total // number_of), total * loads[0] // sum(loads)))
    least = 1 if total - largest >= number_of - 1 else 0
    given, rest = [largest] + [least] * (number_of - 1), total - largest - least * (number_of - 1)
    while rest > 0:
        movable = [i for i in range(1, number_of) if given[i] < largest] or [i for i in range(1, number_of) if given[i] < reach]
        whole, budget = sum([loads[i] for i in movable]), rest
        for i in movable:
            extra = min(reach - given[i], max(1, budget * loads[i] // whole), rest)
            given[i] = given[i] + extra
            rest = rest - extra
    return np.array(given)


def noise(rng, shape, deviation, limit, split=(), kind=jnp.bfloat16):
    values = jax.random.normal(rng, shape, jnp.float32) * deviation
    if len(split) > 0:
        values = levels(rng, shape, split, -0.22, 0.18) * values
    return jnp.clip(values, min=-limit, max=limit).astype(kind)


def setup_inputs(seed: int = 0, part: int = 0) -> dict:
    arg_keys = jax.random.split(jax.random.key(seed), 16)
    part_splits = jax.random.split(jax.random.fold_in(arg_keys[15], part), 16)
    hidden = noise(part_splits[0], (TOKENS, D), 1.0, 6.0, ((0, 16),))
    pre_gain = jnp.clip(1.0 + 0.18 * jax.random.normal(arg_keys[1], (D,), jnp.float32), 0.099609375, 1.8984375).astype(jnp.bfloat16)
    in_x = noise(arg_keys[2], (INNER, D), D ** -0.5, 0.0625, ((0, 16),))
    in_z = draw_in_z(jax.random.fold_in(arg_keys[15], 71), part)
    conv_x = noise(arg_keys[4], (INNER, CONV_K), CONV_K ** -0.5, 3.0, ((0, 16),))
    conv_bc = noise(arg_keys[5], (2 * GROUPS * STATE, CONV_K), CONV_K ** -0.5, 3.0)
    bc_weight = noise(arg_keys[6], (2 * GROUPS * STATE, D), D ** -0.5, 0.0625, ((0, 16),))
    dt_weight = noise(arg_keys[7], (HEADS, D), D ** -0.5, 0.0625, ((0, 16),))
    dt_bias = jnp.clip(-3.0 + 3.5 * jax.random.uniform(arg_keys[8], (HEADS,), jnp.float32) ** levels(arg_keys[8], (HEADS,), ((0, 16),), -0.2, 0.2), -3.0, 0.5).astype(jnp.bfloat16)
    decay_rate = jnp.clip(jnp.exp(math.log(2.0) - 5.996605 * jax.random.uniform(arg_keys[9], (HEADS,), jnp.float32) ** levels(arg_keys[9], (HEADS,), ((0, 16),), -0.2, 0.2)), 0.0049743652, 2.0).astype(jnp.bfloat16)
    skip = jnp.clip(0.29882812 + 1.2011719 * jax.random.uniform(arg_keys[10], (HEADS,), jnp.float32) ** levels(arg_keys[10], (HEADS,), ((0, 16),), -0.2, 0.2), 0.29882812, 1.5).astype(jnp.bfloat16)
    norm_gain = jnp.clip(1.0 + 0.18 * jax.random.normal(arg_keys[11], (INNER,), jnp.float32), 0.099609375, 1.8984375).astype(jnp.bfloat16)
    out_weight = noise(arg_keys[12], (INNER, D), INNER ** -0.5, 0.0625, ((0, 16),))
    segment_ids = jax.vmap(lambda own: jnp.searchsorted(jnp.cumsum(uneven_parts(own, 8, TOK_DEV, TOK_DEV // 2, 1)), jnp.arange(TOK_DEV), side="right"))(jax.random.split(part_splits[13], DP_GROUPS)).reshape((DP_GROUPS, TOK_DEV)).astype(jnp.int32)
    destination_keys = jax.random.split(jax.random.fold_in(part_splits[14], 1), TOKENS // ROWS_DEV)
    destination_turns = jax.random.permutation(jax.random.fold_in(part_splits[14], 3), TOKENS // ROWS_DEV)
    destination = jax.vmap(lambda own, number: assign_block(jax.random.fold_in(part_splits[14], 2), own, number, ROWS_DEV, SHARDS, 1, CAP, 2))(destination_keys, destination_turns).reshape((TOKENS, 1))
    return dict(hidden=hidden, pre_gain=pre_gain, in_x=in_x, in_z=in_z, conv_x=conv_x, conv_bc=conv_bc, bc_weight=bc_weight, dt_weight=dt_weight, dt_bias=dt_bias, decay_rate=decay_rate, skip=skip, norm_gain=norm_gain, out_weight=out_weight, segment_ids=segment_ids, destination=destination)


highest = lax.Precision.HIGHEST

def dot_rows(left, right):
    return lax.dot_general(left, right, (((1,), (1,)), ((), ())), preferred_element_type=jnp.float32)

def rms_rows(values, scale):
    wide = values.astype(jnp.float32)
    meansq = lax.optimization_barrier(jnp.mean(wide * wide, axis=-1, keepdims=True))
    return (wide * lax.rsqrt(meansq + 1e-05) * scale.astype(jnp.float32)).astype(jnp.bfloat16)

def causal_conv(signal, kernel, segment):
    length = signal.shape[0]
    taps_count = kernel.shape[1]
    result = jnp.zeros(signal.shape, jnp.float32)
    for offset in range(taps_count):
        steps_back = taps_count - 1 - offset
        shifted = jnp.pad(signal, ((steps_back, 0), (0, 0)))[:length]
        shifted_seg = jnp.pad(segment, (steps_back, 0), constant_values=-1)[:length]
        same = (shifted_seg == segment).astype(jnp.float32)
        result = result + shifted * kernel[:, offset][None, :] * same[:, None]
    return result

def state_scan(inputs, deltas, rates, keys_b, queries_c, skips, segment):
    total, heads_n, dim_p = inputs.shape
    count = total // BLOCK
    order = jnp.arange(BLOCK)

    def advance(carry, block):
        state, previous = carry
        block_x, block_dt, block_b, block_c, block_seg = block
        cumul = jnp.cumsum(-rates[None, :] * block_dt, axis=0)
        allowed = (block_seg[:, None] == block_seg[None, :]) & (order[:, None] >= order[None, :])
        gaps = cumul[:, None, :] - cumul[None, :, :]
        decays = jnp.where(allowed[:, :, None], jnp.exp(jnp.where(allowed[:, :, None], gaps, 0.0)), 0.0)
        scores = jnp.einsum('ihn,jhn->ijh', block_c, block_b, precision=highest)
        mixing = scores * decays * block_dt[None, :, :]
        output = jnp.einsum('ijh,jhp->ihp', mixing, block_x, precision=highest)
        carried = (block_seg == previous).astype(jnp.float32)
        from_state = jnp.einsum('ihn,hpn->ihp', block_c, state, precision=highest)
        output = output + (carried[:, None] * jnp.exp(cumul))[:, :, None] * from_state
        output = output + skips[None, :, None] * block_x
        final_seg = block_seg[BLOCK - 1]
        ending = (block_seg == final_seg).astype(jnp.float32)
        weights_end = jnp.exp(cumul[BLOCK - 1][None, :] - cumul) * block_dt * ending[:, None]
        keeping = (previous == final_seg).astype(jnp.float32)
        fresh = jnp.einsum('jh,jhp,jhn->hpn', weights_end, block_x, block_b, precision=highest)
        state = keeping * jnp.exp(cumul[BLOCK - 1])[:, None, None] * state + fresh
        return ((state, final_seg), output)
    blocks = (inputs.reshape(count, BLOCK, heads_n, dim_p), deltas.reshape(count, BLOCK, heads_n), keys_b.reshape(count, BLOCK, heads_n, -1), queries_c.reshape(count, BLOCK, heads_n, -1), segment.reshape(count, BLOCK))
    start = (jnp.zeros((heads_n, dim_p, keys_b.shape[-1]), jnp.float32), jnp.array(-1, jnp.int32))
    carry_end, outputs = lax.scan(advance, start, blocks)
    return outputs.reshape(total, heads_n, dim_p)

def reference(hidden, pre_gain, in_x, in_z, conv_x, conv_bc, bc_weight, dt_weight, dt_bias, decay_rate, skip, norm_gain, out_weight, segment_ids, destination):
    per_group = HEADS // GROUPS
    width_bc = GROUPS * STATE
    layers = []
    for group_index in range(DP_GROUPS):
        rows_in = hidden[group_index * TOK_DEV:(group_index + 1) * TOK_DEV]
        segment = segment_ids[group_index].astype(jnp.int32)
        normed = rms_rows(rows_in, pre_gain)
        x_raw = dot_rows(normed, in_x).astype(jnp.bfloat16)
        z_raw = dot_rows(normed, in_z).astype(jnp.bfloat16)
        ssm_raw = dot_rows(normed, bc_weight).astype(jnp.bfloat16)
        dt_raw = dot_rows(normed, dt_weight).astype(jnp.bfloat16)
        x_act = jax.nn.silu(causal_conv(x_raw.astype(jnp.float32), conv_x.astype(jnp.float32), segment))
        ssm_act = jax.nn.silu(causal_conv(ssm_raw.astype(jnp.float32), conv_bc.astype(jnp.float32), segment))
        b_groups = ssm_act[:, :width_bc].reshape(TOK_DEV, GROUPS, STATE)
        c_groups = ssm_act[:, width_bc:].reshape(TOK_DEV, GROUPS, STATE)
        b_heads = jnp.repeat(b_groups, per_group, axis=1)
        c_heads = jnp.repeat(c_groups, per_group, axis=1)
        delta = jax.nn.softplus(dt_raw.astype(jnp.float32) + dt_bias.astype(jnp.float32)[None, :])
        scanned = state_scan(x_act.reshape(TOK_DEV, HEADS, HEAD_DIM), delta, decay_rate.astype(jnp.float32), b_heads, c_heads, skip.astype(jnp.float32), segment)
        gated = scanned.reshape(TOK_DEV, INNER) * jax.nn.silu(z_raw.astype(jnp.float32))
        grouped = gated.reshape(TOK_DEV, GROUPS, INNER // GROUPS)
        meansq = lax.optimization_barrier(jnp.mean(grouped * grouped, axis=-1, keepdims=True))
        scaled = (grouped * lax.rsqrt(meansq + 1e-05)).reshape(TOK_DEV, INNER)
        inner = (scaled * norm_gain.astype(jnp.float32)[None, :]).astype(jnp.bfloat16)
        mixer = jnp.dot(inner, out_weight, preferred_element_type=jnp.float32)
        layers.append((rows_in.astype(jnp.float32) + mixer).astype(jnp.bfloat16))
    layer_out = jnp.concatenate(layers, axis=0)
    taps = jnp.concatenate([hidden, layer_out], axis=1)
    target = destination[:, 0].astype(jnp.int32)
    onehot = (target[:, None] == jnp.arange(SHARDS, dtype=jnp.int32)[None, :]).astype(jnp.int32)
    blocked = onehot.reshape(SHARDS, ROWS_DEV, SHARDS)
    before = jnp.cumsum(blocked, axis=1) - blocked
    ranks = lax.optimization_barrier(jnp.sum(before * blocked, axis=2)).reshape(TOKENS)
    source = jnp.arange(TOKENS, dtype=jnp.int32) // ROWS_DEV
    places = target * (SHARDS * CAP) + source * CAP + ranks
    packed = jnp.zeros((SLOTS, 2 * D), jnp.bfloat16).at[places].set(taps)
    return (layer_out, packed)
```

```python
import functools

import jax
import jax.numpy as jnp
from jax import lax
from jax.experimental import pallas as pl
from jax.experimental.pallas import tpu as pltpu
from jax.sharding import PartitionSpec as P

HEAD_DIM = 64
INNER = 8192
HEADS = 128
STATE = 128
GROUPS = 4
BLOCK = 128
CAP = 2


highest = lax.Precision.HIGHEST


def dot_rows(left, right):
    return lax.dot_general(
        left, right, (((1,), (1,)), ((), ())), preferred_element_type=jnp.float32
    )


def rms_rows(values, scale):
    wide = values.astype(jnp.float32)
    meansq = jnp.mean(wide * wide, axis=-1, keepdims=True)
    return (wide * lax.rsqrt(meansq + 1e-05) * scale.astype(jnp.float32)).astype(jnp.bfloat16)


def causal_conv(signal, kernel, segment):
    length = signal.shape[0]
    taps_count = kernel.shape[1]
    result = jnp.zeros(signal.shape, jnp.float32)
    for offset in range(taps_count):
        steps_back = taps_count - 1 - offset
        shifted = jnp.pad(signal, ((steps_back, 0), (0, 0)))[:length]
        shifted_seg = jnp.pad(segment, (steps_back, 0), constant_values=-1)[:length]
        same = (shifted_seg == segment).astype(jnp.float32)
        result = result + shifted * kernel[:, offset][None, :] * same[:, None]
    return result


def state_scan(inputs, deltas, rates, keys_b, queries_c, skips, segment):
    total, heads_n, dim_p = inputs.shape
    count = total // BLOCK
    order = jnp.arange(BLOCK)

    def advance(carry, block):
        state, previous = carry
        block_x, block_dt, block_b, block_c, block_seg = block
        cumul = jnp.cumsum(-rates[None, :] * block_dt, axis=0)
        allowed = (block_seg[:, None] == block_seg[None, :]) & (order[:, None] >= order[None, :])
        gaps = cumul[:, None, :] - cumul[None, :, :]
        decays = jnp.where(
            allowed[:, :, None], jnp.exp(jnp.where(allowed[:, :, None], gaps, 0.0)), 0.0
        )
        scores = jnp.einsum("ihn,jhn->ijh", block_c, block_b, precision=highest)
        mixing = scores * decays * block_dt[None, :, :]
        output = jnp.einsum("ijh,jhp->ihp", mixing, block_x, precision=highest)
        carried = (block_seg == previous).astype(jnp.float32)
        from_state = jnp.einsum("ihn,hpn->ihp", block_c, state, precision=highest)
        output = output + (carried[:, None] * jnp.exp(cumul))[:, :, None] * from_state
        output = output + skips[None, :, None] * block_x
        final_seg = block_seg[BLOCK - 1]
        ending = (block_seg == final_seg).astype(jnp.float32)
        weights_end = jnp.exp(cumul[BLOCK - 1][None, :] - cumul) * block_dt * ending[:, None]
        keeping = (previous == final_seg).astype(jnp.float32)
        fresh = jnp.einsum("jh,jhp,jhn->hpn", weights_end, block_x, block_b, precision=highest)
        state = keeping * jnp.exp(cumul[BLOCK - 1])[:, None, None] * state + fresh
        return ((state, final_seg), output)

    blocks = (
        inputs.reshape(count, BLOCK, heads_n, dim_p),
        deltas.reshape(count, BLOCK, heads_n),
        keys_b.reshape(count, BLOCK, heads_n, -1),
        queries_c.reshape(count, BLOCK, heads_n, -1),
        segment.reshape(count, BLOCK),
    )
    start = (jnp.zeros((heads_n, dim_p, keys_b.shape[-1]), jnp.float32), jnp.array(-1, jnp.int32))
    carry_end, outputs = lax.scan(advance, start, blocks)
    return outputs.reshape(total, heads_n, dim_p)


def mixer_core(tokens, segment, params, head_ids, ssm_raw, conv_bc):
    proj_x, proj_z, taps_x, proj_dt, bias_dt, rates, skips = params
    row_total = tokens.shape[0]
    heads_here = head_ids.shape[0]
    width_bc = GROUPS * STATE
    x_raw = dot_rows(tokens, proj_x).astype(jnp.bfloat16)
    z_raw = dot_rows(tokens, proj_z).astype(jnp.bfloat16)
    dt_raw = dot_rows(tokens, proj_dt).astype(jnp.bfloat16)
    x_act = jax.nn.silu(causal_conv(x_raw.astype(jnp.float32), taps_x.astype(jnp.float32), segment))
    ssm_act = jax.nn.silu(
        causal_conv(ssm_raw.astype(jnp.float32), conv_bc.astype(jnp.float32), segment)
    )
    b_groups = ssm_act[:, :width_bc].reshape(row_total, GROUPS, STATE)
    c_groups = ssm_act[:, width_bc:].reshape(row_total, GROUPS, STATE)
    select = (head_ids[:, None] // (HEADS // GROUPS) == jnp.arange(GROUPS)[None, :]).astype(
        jnp.float32
    )
    b_heads = jnp.einsum("tgn,hg->thn", b_groups, select, precision=highest)
    c_heads = jnp.einsum("tgn,hg->thn", c_groups, select, precision=highest)
    delta = jax.nn.softplus(dt_raw.astype(jnp.float32) + bias_dt.astype(jnp.float32)[None, :])
    scanned = state_scan(
        x_act.reshape(row_total, heads_here, HEAD_DIM),
        delta,
        rates.astype(jnp.float32),
        b_heads,
        c_heads,
        skips.astype(jnp.float32),
        segment,
    )
    return scanned.reshape(row_total, -1) * jax.nn.silu(z_raw.astype(jnp.float32))


def on_device(
    hidden,
    pre_gain,
    in_x,
    in_z,
    conv_x,
    conv_bc,
    bc_weight,
    dt_weight,
    dt_bias,
    decay_rate,
    skip,
    norm_gain,
    out_weight,
    segment_ids,
    destination,
):
    tensor_count = lax.axis_size("tensor")
    group_count = lax.axis_size("dp")
    shard_count = tensor_count * group_count
    tensor_pos = lax.axis_index("tensor")
    heads_each = in_x.shape[0] // HEAD_DIM
    target = destination[:, 0]
    onehot = (target[:, None] == jnp.arange(shard_count, dtype=jnp.int32)[None, :]).astype(
        jnp.int32
    )
    ranks = jnp.sum((jnp.cumsum(onehot, axis=0) - onehot) * onehot, axis=1)
    slot_ids = target * CAP + ranks
    normed = rms_rows(hidden, pre_gain)
    tokens = lax.all_gather(normed, "tensor", axis=0, tiled=True)
    segment = segment_ids.reshape(-1)
    gathered = (
        lax.all_gather(in_x, "dp", axis=0, tiled=True),
        lax.all_gather(in_z, "dp", axis=0, tiled=True),
        lax.all_gather(conv_x, "dp", axis=0, tiled=True),
        lax.all_gather(dt_weight, "dp", axis=0, tiled=True),
        lax.all_gather(dt_bias, "dp", axis=0, tiled=True),
        lax.all_gather(decay_rate, "dp", axis=0, tiled=True),
        lax.all_gather(skip, "dp", axis=0, tiled=True),
        lax.all_gather(norm_gain, "dp", axis=0, tiled=True),
        lax.all_gather(out_weight, "dp", axis=0, tiled=True),
    )
    params = gathered[:7]
    gain_here = gathered[7]
    proj_out = gathered[8]
    head_ids = jnp.concatenate(
        [
            (member * tensor_count + tensor_pos) * heads_each + jnp.arange(heads_each)
            for member in range(group_count)
        ]
    )
    ssm_part = dot_rows(tokens, bc_weight).astype(jnp.bfloat16)
    ssm_raw = lax.all_gather(ssm_part, "tensor", axis=1, tiled=True)
    gated = mixer_core(tokens, segment, params, head_ids, ssm_raw, conv_bc)
    row_total = gated.shape[0]
    heads_here = head_ids.shape[0]
    group_sel = (head_ids[:, None] // (HEADS // GROUPS) == jnp.arange(GROUPS)[None, :]).astype(
        jnp.float32
    )
    by_head = gated.reshape(row_total, heads_here, HEAD_DIM)
    head_sq = jnp.sum(by_head * by_head, axis=2)
    partial_sq = jnp.dot(head_sq, group_sel, precision=highest)
    total_sq = lax.psum(partial_sq, "tensor")
    head_total = jnp.dot(total_sq, group_sel.T, precision=highest)
    head_scale = lax.rsqrt(head_total / (INNER // GROUPS) + 1e-05)
    scaled = (by_head * head_scale[:, :, None]).reshape(row_total, -1)
    inner = (scaled * gain_here.astype(jnp.float32)[None, :]).astype(jnp.bfloat16)
    mixer = lax.psum_scatter(
        jnp.dot(inner, proj_out, preferred_element_type=jnp.float32),
        "tensor",
        scatter_dimension=0,
        tiled=True,
    )
    layer_out = (hidden.astype(jnp.float32) + mixer).astype(jnp.bfloat16)
    joined = jnp.concatenate([hidden, layer_out], axis=1)
    filled = jnp.zeros((shard_count * CAP, joined.shape[1]), jnp.bfloat16).at[slot_ids].set(joined)
    received = lax.all_to_all(
        filled.reshape(shard_count, CAP, joined.shape[1]),
        ("dp", "tensor"),
        split_axis=0,
        concat_axis=0,
        tiled=True,
    )
    packed = received.reshape(shard_count * CAP, -1)
    return (layer_out, packed)


PLANE = 4
VMEM_LIMIT = 56 * 1024 * 1024
NEG = -1e30


def vmem():
    return pl.BlockSpec(memory_space=pltpu.VMEM)


def smem():
    return pl.BlockSpec(memory_space=pltpu.SMEM)


def dot_nt(left, right, precision=None):
    return lax.dot_general(
        left, right, (((1,), (1,)), ((), ())), precision=precision, preferred_element_type=jnp.float32
    )


def norm_kernel(spot_ref, b0, b1, b2, b3, gain_ref, small_ref, normed_ref, bc_ref, dt_ref):
    rows, width = b0.shape[0], gain_ref.shape[1]
    step = 1024
    for index, block in enumerate((b0, b1, b2, b3)):
        start = pl.multiple_of((spot_ref[0] ^ index) * rows, rows)
        total = jnp.zeros((rows, 128), jnp.float32)
        for col in range(0, width, step):
            wide = block[:, col : col + step].astype(jnp.float32)
            square = wide * wide
            for lane in range(0, step, 128):
                total = total + square[:, lane : lane + 128]
        scale = lax.rsqrt(jnp.sum(total, axis=1, keepdims=True) / width + 1e-05)
        for col in range(0, width, step):
            wide = block[:, col : col + step].astype(jnp.float32)
            normed_ref[pl.ds(start, rows), col : col + step] = (
                wide * scale * gain_ref[:, col : col + step].astype(jnp.float32)
            ).astype(jnp.bfloat16)
    result = dot_nt(normed_ref[...], small_ref[...]).astype(jnp.bfloat16)
    half = bc_ref.shape[1]
    bc_ref[...] = result[:, :half]
    dt_ref[...] = result[:, half:].astype(jnp.float32)


def norm_plane(spot, blocks, gain, small):
    rows, width = blocks[0].shape[0] * PLANE, gain.shape[1]
    return pl.pallas_call(
        norm_kernel,
        out_shape=(
            jax.ShapeDtypeStruct((rows, width), jnp.bfloat16),
            jax.ShapeDtypeStruct((rows, small.shape[0] - 128), jnp.bfloat16),
            jax.ShapeDtypeStruct((rows, 128), jnp.float32),
        ),
        in_specs=[smem()] + [vmem()] * 6,
        out_specs=(vmem(), vmem(), vmem()),
        compiler_params=pltpu.CompilerParams(vmem_limit_bytes=VMEM_LIMIT),
        cost_estimate=pl.CostEstimate(
            flops=2 * rows * width * small.shape[0], bytes_accessed=8 << 20, transcendentals=0
        ),
        name="norm_plane",
    )(spot, *blocks, gain, small)


def project_kernel(normed_ref, wx_ref, wz_ref, x_ref, z_ref):
    x_ref[...] = dot_nt(normed_ref[...], wx_ref[...]).astype(jnp.bfloat16)
    z_ref[...] = dot_nt(normed_ref[...], wz_ref[...]).astype(jnp.bfloat16)


def project_plane(normed, in_x, in_z):
    rows, width = normed.shape
    cols = in_x.shape[0]
    tile = 128
    return pl.pallas_call(
        project_kernel,
        grid=(cols // tile,),
        out_shape=(jax.ShapeDtypeStruct((rows, cols), jnp.bfloat16),) * 2,
        in_specs=[
            pl.BlockSpec((rows, width), lambda i: (0, 0)),
            pl.BlockSpec((tile, width), lambda i: (i, 0)),
            pl.BlockSpec((tile, width), lambda i: (i, 0)),
        ],
        out_specs=(pl.BlockSpec((rows, tile), lambda i: (0, i)),) * 2,
        compiler_params=pltpu.CompilerParams(vmem_limit_bytes=VMEM_LIMIT),
        cost_estimate=pl.CostEstimate(
            flops=4 * rows * width * cols, bytes_accessed=20 << 20, transcendentals=0
        ),
        name="project_plane",
    )(normed, in_x, in_z)


def silu(value):
    return value / (1.0 + jnp.exp(-value))


def scan_kernel(
    spot_ref,
    *refs,
    heads,
    planes,
):
    xs, zs, dts = refs[:planes], refs[planes : 2 * planes], refs[2 * planes : 3 * planes]
    refs = refs[3 * planes :]
    early, late = refs[:4], refs[4:8]
    (taps_x, taps_bc, masks, bias, marks, keep, head_rows, expand, skip_ref, gain_ref) = refs[8:18]
    gated_ref, square_ref = refs[18:20]
    x_all, z_all, dt_all, bc_all = refs[20:]
    z_pos, spot = spot_ref[0], spot_ref[1]
    rows = xs[0].shape[0]
    chans = xs[0].shape[1]
    highest_ = lax.Precision.HIGHEST
    bit0, bit1 = (spot & 1) == 1, (spot & 2) == 2
    x_all[0:8, :] = jnp.zeros((8, chans), jnp.float32)
    bc_all[0:8, :] = jnp.zeros((8, 2 * STATE), jnp.float32)
    for s in range(planes):
        at = pl.multiple_of(lax.rem(z_pos - s + planes, planes) * rows, rows)
        x_all[pl.ds(at + 8, rows), :] = xs[s][...].astype(jnp.float32)
        z_all[pl.ds(at, rows), :] = zs[s][...]
        dt_all[pl.ds(at, rows), :] = dts[s][...]
        if s < planes - 1:
            got = [ref[s * rows : (s + 1) * rows, :].astype(jnp.float32) for ref in early]
        else:
            got = [ref[...].astype(jnp.float32) for ref in late]
        a0, a1 = jnp.where(bit0, got[1], got[0]), jnp.where(bit0, got[0], got[1])
        a2, a3 = jnp.where(bit0, got[3], got[2]), jnp.where(bit0, got[2], got[3])
        p0, p2 = jnp.where(bit1, a2, a0), jnp.where(bit1, a0, a2)
        p1, p3 = jnp.where(bit1, a3, a1), jnp.where(bit1, a1, a3)
        for chip, first, pair in ((z_pos, 0, (p0, p1)), (z_pos + GROUPS, STATE, (p2, p3))):
            row = lax.rem(lax.div(chip, PLANE // 2) - s + planes, planes) * rows
            row = pl.multiple_of(row, rows)
            bc_all[pl.ds(row + 8, rows), first : first + STATE] = jnp.concatenate(pair, axis=1)
    order_i = lax.broadcasted_iota(jnp.int32, (rows, rows), 0)
    order_j = lax.broadcasted_iota(jnp.int32, (rows, rows), 1)
    tri = (order_i >= order_j).astype(jnp.float32)
    lane = lax.broadcasted_iota(jnp.int32, (rows, 128), 1)
    real = lane < heads
    low = lane < HEAD_DIM
    bias_dt, rates = head_rows[0:1, :], head_rows[1:2, :]
    lanes_x, lanes_bc = chans // 128, 2 * STATE // 128

    def conv(source, taps, base, count):
        last = taps.shape[0] - 1
        total = source[base + 8 : base + 8 + rows, :] * taps[last : last + 1, :]
        for back in range(1, last + 1):
            same = jnp.concatenate([masks[back - 1, base : base + rows, :]] * count, axis=1)
            total = total + (
                source[base + 8 - back : base + 8 - back + rows, :]
                * taps[last - back : last - back + 1, :]
                * same
            )
        return silu(total)

    state = jnp.zeros((STATE, chans), jnp.float32)
    for p in range(planes):
        base = p * rows
        span = slice(base, base + rows)
        x_act = conv(x_all, taps_x, base, lanes_x)
        bc_act = conv(bc_all, taps_bc, base, lanes_bc).astype(jnp.bfloat16)
        keys, queries = bc_act[:, :STATE], bc_act[:, STATE:]
        raw = dt_all[span, :] + bias_dt
        delta = jnp.maximum(raw, 0.0) + jnp.log1p(jnp.exp(-jnp.abs(raw)))
        delta = jnp.where(real, delta, 0.0)
        cum = jnp.dot(tri, -rates * delta, precision=highest_, preferred_element_type=jnp.float32)
        cum_t = cum.T
        last = cum[rows - 1 : rows, :]
        carried = jnp.where(real, jnp.exp(cum) * marks[0, span, :], 0.0)
        ending = jnp.where(real, jnp.exp(last - cum) * marks[1, span, :] * delta, 0.0)
        decay_end = jnp.where(real[0:8], jnp.exp(jnp.broadcast_to(last, (8, 128))) * keep[p : p + 1, :], 0.0)
        spread = jnp.dot(
            jnp.concatenate([delta, carried, ending, decay_end], axis=0),
            expand[...],
            precision=highest_,
            preferred_element_type=jnp.float32,
        )
        delta_x = (spread[:rows] * x_act).astype(jnp.bfloat16)
        end_x = (spread[2 * rows : 3 * rows] * x_act).astype(jnp.bfloat16)
        scores = dot_nt(queries, keys)
        from_state = jnp.dot(queries, state.astype(jnp.bfloat16), preferred_element_type=jnp.float32)
        block_bias = bias[span, :]
        outs = []
        for pair in range(heads // 2):
            both = delta_x[:, pair * 128 : (pair + 1) * 128]
            part = []
            for h in (2 * pair, 2 * pair + 1):
                gap = cum[:, h : h + 1] - cum_t[h : h + 1, :]
                mixing = (jnp.exp(gap + block_bias) * scores).astype(jnp.bfloat16)
                part.append(jnp.dot(mixing, both, preferred_element_type=jnp.float32))
            outs.append(jnp.where(low, part[0], part[1]))
        y = jnp.concatenate(outs, axis=1)
        y = y + spread[rows : 2 * rows] * from_state + skip_ref[...] * x_act
        gated = y * silu(z_all[span, :].astype(jnp.float32))
        square_ref[p : p + 1, :] = dot_nt(
            jnp.ones((8, chans), jnp.float32), gated * gated, precision=highest_
        )[0:1, :]
        gated_ref[span, :] = (gated * gain_ref[...]).astype(jnp.bfloat16)
        if p + 1 < planes:
            fresh = lax.dot_general(
                keys, end_x, (((0,), (0,)), ((), ())), preferred_element_type=jnp.float32
            )
            state = spread[3 * rows : 3 * rows + 1] * state + fresh


def scan_all(spots, xs, zs, dts, early, late, consts, heads):
    planes = len(xs)
    rows, chans = xs[0].shape
    return pl.pallas_call(
        functools.partial(scan_kernel, heads=heads, planes=planes),
        out_shape=(
            jax.ShapeDtypeStruct((planes * rows, chans), jnp.bfloat16),
            jax.ShapeDtypeStruct((8, rows), jnp.float32),
        ),
        in_specs=[smem()] + [vmem()] * (3 * planes + 8 + len(consts)),
        out_specs=(vmem(), vmem()),
        scratch_shapes=[
            pltpu.VMEM((planes * rows + 8, chans), jnp.float32),
            pltpu.VMEM((planes * rows, chans), jnp.bfloat16),
            pltpu.VMEM((planes * rows, 128), jnp.float32),
            pltpu.VMEM((planes * rows + 8, 2 * STATE), jnp.float32),
        ],
        compiler_params=pltpu.CompilerParams(vmem_limit_bytes=VMEM_LIMIT),
        cost_estimate=pl.CostEstimate(flops=1 << 30, bytes_accessed=8 << 20, transcendentals=0),
        name="scan_all",
    )(spots, *xs, *zs, *dts, *early, *late, *consts)


def away_kernel(at_ref, gated_ref, weight_ref, away_ref):
    rows = away_ref.shape[0] // 2
    left = jnp.concatenate(
        [gated_ref[pl.ds(pl.multiple_of(at_ref[i], rows), rows), :] for i in range(2)], axis=0
    )
    away_ref[...] = jnp.dot(left, weight_ref[...], preferred_element_type=jnp.float32).astype(
        jnp.bfloat16
    )


def home_kernel(at_ref, gated_ref, weight_ref, got_ref, send_ref, keep_ref):
    rows = send_ref.shape[0]
    left = jnp.concatenate(
        [gated_ref[pl.ds(pl.multiple_of(at_ref[i], rows), rows), :] for i in range(2)], axis=0
    )
    total = jnp.dot(left, weight_ref[...], preferred_element_type=jnp.float32)
    total = total + got_ref[...].astype(jnp.float32)
    send_ref[...] = total[:rows].astype(jnp.bfloat16)
    keep_ref[...] = total[rows:]


def out_part(at, gated, weight, got, rows):
    chans, width = weight.shape
    tile = 2048
    column = lambda i: (0, i)
    specs = [
        smem(),
        pl.BlockSpec(gated.shape, lambda i: (0, 0)),
        pl.BlockSpec((chans, tile), column),
    ]
    common = dict(
        grid=(width // tile,),
        compiler_params=pltpu.CompilerParams(vmem_limit_bytes=VMEM_LIMIT),
        cost_estimate=pl.CostEstimate(
            flops=4 * rows * width * chans, bytes_accessed=10 << 20, transcendentals=0
        ),
    )
    if got is None:
        return pl.pallas_call(
            away_kernel,
            out_shape=jax.ShapeDtypeStruct((2 * rows, width), jnp.bfloat16),
            in_specs=specs,
            out_specs=pl.BlockSpec((2 * rows, tile), column),
            name="out_away",
            **common,
        )(at, gated, weight)
    return pl.pallas_call(
        home_kernel,
        out_shape=(
            jax.ShapeDtypeStruct((rows, width), jnp.bfloat16),
            jax.ShapeDtypeStruct((rows, width), jnp.float32),
        ),
        in_specs=specs + [pl.BlockSpec((2 * rows, tile), column)],
        out_specs=(pl.BlockSpec((rows, tile), column),) * 2,
        name="out_home",
        **common,
    )(at, gated, weight, got)


def pick_kernel(select_ref, *refs):
    rows = jnp.concatenate([ref[...] for ref in refs[:-1]], axis=0)
    refs[-1][...] = jnp.dot(
        select_ref[...], rows, preferred_element_type=jnp.float32
    ).astype(jnp.bfloat16)


def pick_rows(select, blocks, width):
    tile = 1024
    rows = blocks[0].shape[0]
    return pl.pallas_call(
        pick_kernel,
        grid=(width // tile,),
        out_shape=jax.ShapeDtypeStruct((select.shape[0], width), jnp.bfloat16),
        in_specs=[pl.BlockSpec(select.shape, lambda i: (0, 0))]
        + [pl.BlockSpec((rows, tile), lambda i: (0, i))] * len(blocks),
        out_specs=pl.BlockSpec((select.shape[0], tile), lambda i: (0, i)),
        compiler_params=pltpu.CompilerParams(vmem_limit_bytes=VMEM_LIMIT),
        cost_estimate=pl.CostEstimate(
            flops=2 * select.shape[0] * select.shape[1] * width,
            bytes_accessed=9 << 20,
            transcendentals=0,
        ),
        name="pick_rows",
    )(select, *blocks)


def scan_constants(
    segment_ids, conv_x, conv_bc, dt_bias, decay_rate, skip, norm_gain, z_pos, planes
):
    f32 = jnp.float32
    heads = dt_bias.shape[0]
    segment = segment_ids.reshape(-1)
    total_rows = segment.shape[0]
    plane_rows = total_rows // planes
    position = jnp.arange(total_rows)
    masks = jnp.stack(
        [
            jnp.broadcast_to(
                ((jnp.roll(segment, back) == segment) & (position >= back)).astype(f32)[:, None],
                (total_rows, 128),
            )
            for back in range(1, conv_x.shape[1])
        ]
    )
    by_plane = segment.reshape(planes, plane_rows)
    inner_order = jnp.arange(plane_rows)
    allowed = (by_plane[:, :, None] == by_plane[:, None, :]) & (
        inner_order[:, None] >= inner_order[None, :]
    )
    bias = jnp.where(allowed, 0.0, NEG).astype(f32).reshape(total_rows, plane_rows)
    final = by_plane[:, -1]
    previous = jnp.concatenate([jnp.full((1,), -1, final.dtype), final[:-1]])
    marks = jnp.stack(
        [
            jnp.broadcast_to(value.astype(f32).reshape(-1, 1), (total_rows, 128))
            for value in (by_plane == previous[:, None], by_plane == final[:, None])
        ]
    )
    keep = jnp.broadcast_to((previous == final).astype(f32)[:, None], (planes, 128))
    keep = jnp.pad(keep, ((0, 8 - planes), (0, 0)))
    head_rows = jnp.pad(
        jnp.stack([dt_bias.astype(f32), decay_rate.astype(f32)]), ((0, 6), (0, 128 - heads))
    )
    expand = (jnp.arange(128)[:, None] == jnp.arange(heads * HEAD_DIM)[None, :] // HEAD_DIM).astype(f32)
    skip_row = jnp.repeat(skip.astype(f32), HEAD_DIM)[None, :]
    out_gain = norm_gain.astype(f32)[None, :]
    taps_x = conv_x.astype(f32).T
    width_bc = GROUPS * STATE
    taps_bc = jnp.concatenate(
        [
            lax.dynamic_slice_in_dim(conv_bc, z_pos * STATE + start, STATE, axis=0)
            for start in (0, width_bc)
        ],
        axis=0,
    ).astype(f32).T
    return (taps_x, taps_bc, masks, bias, marks, keep, head_rows, expand, skip_row, out_gain)


def on_device_planes(
    hidden,
    pre_gain,
    in_x,
    in_z,
    conv_x,
    conv_bc,
    bc_weight,
    dt_weight,
    dt_bias,
    decay_rate,
    skip,
    norm_gain,
    out_weight,
    segment_ids,
    destination,
):
    count = lax.axis_size("tensor")
    planes = count // PLANE
    me = lax.axis_index("tensor")
    z_pos, spot = me // PLANE, me % PLANE
    rows, width = hidden.shape
    plane_rows = rows * PLANE
    heads = dt_weight.shape[0]
    every = range(count)
    ring = [(t, (t + PLANE) % count) for t in every]
    over_y = [(t, t ^ 2) for t in every]
    over_core = [(t, t ^ 1) for t in every]

    def permute(value, pairs):
        return lax.ppermute(value, "tensor", pairs)

    f32 = jnp.float32
    small = jnp.concatenate(
        [bc_weight, jnp.zeros((0, width), bc_weight.dtype)]
        + [dt_weight, jnp.zeros((128 - heads, width), dt_weight.dtype)],
        axis=0,
    )
    gain_row = pre_gain[None, :]
    consts = scan_constants(
        segment_ids, conv_x, conv_bc, dt_bias, decay_rate, skip, norm_gain, z_pos, planes
    )
    spot_only = spot.astype(jnp.int32)[None]
    spots = jnp.stack([z_pos, spot]).astype(jnp.int32)

    target = destination[:, 0]
    own = jnp.concatenate(
        [hidden, jnp.broadcast_to(destination.astype(jnp.bfloat16), (rows, 128))], axis=1
    )
    straight, crossed = [own], []
    straight_core, crossed_core = [], []
    for step in range(planes):
        moved = [permute(straight[step], over_y), permute(straight[step], over_core)]
        if step + 1 < planes:
            moved.append(permute(straight[step], ring))
        if step:
            moved.append(permute(crossed[step - 1], over_core))
        moved = list(lax.optimization_barrier(tuple(moved)))
        crossed.append(moved[0])
        straight_core.append(moved[1])
        if step + 1 < planes:
            straight.append(moved[2])
        if step:
            crossed_core.append(moved[-1])
    crossed_core.append(permute(crossed[-1], over_core))

    def exchange(piece):
        result = []
        for turn in range(PLANE):
            pairs = []
            for t in every:
                chip, side = t // 2, t % 2
                have = (chip // GROUPS) * 2 + side
                pairs.append((t, (chip % GROUPS) * PLANE + (have ^ turn)))
            result.append(permute(piece, pairs))
        return result

    normed, pieces, dts = [], [], []
    for step in range(planes):
        blocks = [straight[step], straight_core[step], crossed[step], crossed_core[step]]
        n, b, d = norm_plane(spot_only, blocks, gain_row, small)
        normed.append(n)
        pieces.append(b)
        dts.append(d)
    early = exchange(jnp.concatenate(pieces[:-1], axis=0))
    late = exchange(pieces[-1])
    xs, zs = [], []
    for step in range(planes):
        x, z = project_plane(normed[step], in_x, in_z)
        xs.append(x)
        zs.append(z)
    gated, squares = scan_all(spots, xs, zs, dts, early, late, consts, heads)

    squares = squares + permute(squares, over_core)
    squares = squares + permute(squares, over_y)
    scale = lax.rsqrt(squares[:planes].reshape(-1) / (INNER // GROUPS) + 1e-05)

    travelling = None
    for step in range(planes):
        plane = (z_pos - 1 - step) % planes
        side, level = spot % 2, spot // 2

        def rows_at(level_, side_):
            return ((plane * 2 + level_) * 2 + side_) * rows

        away_at = jnp.stack([rows_at(1 - level, 1 - side), rows_at(level, 1 - side)]).astype(jnp.int32)
        home_at = jnp.stack([rows_at(1 - level, side), rows_at(level, side)]).astype(jnp.int32)
        away = out_part(away_at, gated, out_weight, None, rows)
        got = permute(away, over_core)
        send, hold = out_part(home_at, gated, out_weight, got, rows)
        got_y = permute(send, over_y)
        mine = lax.dynamic_slice_in_dim(scale, rows_at(level, side), rows)[:, None]
        total = (hold + got_y.astype(f32)) * mine
        if travelling is not None:
            total = total + travelling.astype(f32)
        if step + 1 < planes:
            travelling = permute(total.astype(jnp.bfloat16), ring)
    layer_out = (hidden.astype(f32) + total).astype(jnp.bfloat16)

    blocks, sources = [], []
    for step in range(planes):
        for index, block in enumerate(
            (straight[step], straight_core[step], crossed[step], crossed_core[step])
        ):
            blocks.append(block)
            sources.append(((z_pos - step) % planes) * PLANE + (spot ^ index))
    sources = jnp.stack(sources)
    targets = jnp.stack([block[:, width] for block in blocks]).astype(jnp.int32)
    match = (targets == me).astype(jnp.int32)
    ranks = jnp.cumsum(match, axis=1) - match
    slots = jnp.where(match == 1, sources[:, None] * CAP + ranks, -1).reshape(-1)
    select = (slots[None, :] == jnp.arange(count * CAP)[:, None]).astype(jnp.bfloat16)
    picked = pick_rows(select, blocks, width)

    onehot = (target[:, None] == jnp.arange(count, dtype=jnp.int32)[None, :]).astype(jnp.int32)
    own_ranks = jnp.sum((jnp.cumsum(onehot, axis=0) - onehot) * onehot, axis=1)
    own_slots = target * CAP + own_ranks
    place = (own_slots[None, :] == jnp.arange(count * CAP)[:, None]).astype(jnp.bfloat16)
    filled = jnp.dot(place, layer_out, preferred_element_type=f32).astype(jnp.bfloat16)
    received = lax.all_to_all(
        filled.reshape(count, CAP, width), "tensor", split_axis=0, concat_axis=0, tiled=True
    )
    packed = jnp.concatenate([picked, received.reshape(count * CAP, width)], axis=1)
    return (layer_out, packed)


def solution(mesh):
    planar = mesh.shape["dp"] == 1 and mesh.shape["tensor"] == PLANE * GROUPS
    return jax.shard_map(
        on_device_planes if planar else on_device,
        mesh=mesh,
        in_specs=(
            P(("rep", "dp", "tensor"), None),
            P(),
            P(("dp", "tensor"), None),
            P(("dp", "tensor"), None),
            P(("dp", "tensor"), None),
            P(),
            P("tensor", None),
            P(("dp", "tensor"), None),
            P(("dp", "tensor")),
            P(("dp", "tensor")),
            P(("dp", "tensor")),
            P(("dp", "tensor")),
            P(("dp", "tensor"), None),
            P(("rep", "dp"), None),
            P(("rep", "dp", "tensor"), None),
        ),
        out_specs=(P(("rep", "dp", "tensor"), None), P(("rep", "dp", "tensor"), None)),
        check_vma=False,
    )
```

```python
import functools

import jax
import jax.numpy as jnp
from jax import lax
from jax.experimental import pallas as pl
from jax.experimental.pallas import tpu as pltpu
from jax.sharding import PartitionSpec as P

HEAD_DIM = 64
INNER = 8192
HEADS = 128
STATE = 128
GROUPS = 4
BLOCK = 128
CAP = 2


highest = lax.Precision.HIGHEST


def dot_rows(left, right):
    return lax.dot_general(
        left, right, (((1,), (1,)), ((), ())), preferred_element_type=jnp.float32
    )


def rms_rows(values, scale):
    wide = values.astype(jnp.float32)
    meansq = jnp.mean(wide * wide, axis=-1, keepdims=True)
    return (wide * lax.rsqrt(meansq + 1e-05) * scale.astype(jnp.float32)).astype(jnp.bfloat16)


def causal_conv(signal, kernel, segment):
    length = signal.shape[0]
    taps_count = kernel.shape[1]
    result = jnp.zeros(signal.shape, jnp.float32)
    for offset in range(taps_count):
        steps_back = taps_count - 1 - offset
        shifted = jnp.pad(signal, ((steps_back, 0), (0, 0)))[:length]
        shifted_seg = jnp.pad(segment, (steps_back, 0), constant_values=-1)[:length]
        same = (shifted_seg == segment).astype(jnp.float32)
        result = result + shifted * kernel[:, offset][None, :] * same[:, None]
    return result


def state_scan(inputs, deltas, rates, keys_b, queries_c, skips, segment):
    total, heads_n, dim_p = inputs.shape
    count = total // BLOCK
    order = jnp.arange(BLOCK)

    def advance(carry, block):
        state, previous = carry
        block_x, block_dt, block_b, block_c, block_seg = block
        cumul = jnp.cumsum(-rates[None, :] * block_dt, axis=0)
        allowed = (block_seg[:, None] == block_seg[None, :]) & (order[:, None] >= order[None, :])
        gaps = cumul[:, None, :] - cumul[None, :, :]
        decays = jnp.where(
            allowed[:, :, None], jnp.exp(jnp.where(allowed[:, :, None], gaps, 0.0)), 0.0
        )
        scores = jnp.einsum("ihn,jhn->ijh", block_c, block_b, precision=highest)
        mixing = scores * decays * block_dt[None, :, :]
        output = jnp.einsum("ijh,jhp->ihp", mixing, block_x, precision=highest)
        carried = (block_seg == previous).astype(jnp.float32)
        from_state = jnp.einsum("ihn,hpn->ihp", block_c, state, precision=highest)
        output = output + (carried[:, None] * jnp.exp(cumul))[:, :, None] * from_state
        output = output + skips[None, :, None] * block_x
        final_seg = block_seg[BLOCK - 1]
        ending = (block_seg == final_seg).astype(jnp.float32)
        weights_end = jnp.exp(cumul[BLOCK - 1][None, :] - cumul) * block_dt * ending[:, None]
        keeping = (previous == final_seg).astype(jnp.float32)
        fresh = jnp.einsum("jh,jhp,jhn->hpn", weights_end, block_x, block_b, precision=highest)
        state = keeping * jnp.exp(cumul[BLOCK - 1])[:, None, None] * state + fresh
        return ((state, final_seg), output)

    blocks = (
        inputs.reshape(count, BLOCK, heads_n, dim_p),
        deltas.reshape(count, BLOCK, heads_n),
        keys_b.reshape(count, BLOCK, heads_n, -1),
        queries_c.reshape(count, BLOCK, heads_n, -1),
        segment.reshape(count, BLOCK),
    )
    start = (jnp.zeros((heads_n, dim_p, keys_b.shape[-1]), jnp.float32), jnp.array(-1, jnp.int32))
    carry_end, outputs = lax.scan(advance, start, blocks)
    return outputs.reshape(total, heads_n, dim_p)


def mixer_core(tokens, segment, params, head_ids, ssm_raw, conv_bc):
    proj_x, proj_z, taps_x, proj_dt, bias_dt, rates, skips = params
    row_total = tokens.shape[0]
    heads_here = head_ids.shape[0]
    width_bc = GROUPS * STATE
    x_raw = dot_rows(tokens, proj_x).astype(jnp.bfloat16)
    z_raw = dot_rows(tokens, proj_z).astype(jnp.bfloat16)
    dt_raw = dot_rows(tokens, proj_dt).astype(jnp.bfloat16)
    x_act = jax.nn.silu(causal_conv(x_raw.astype(jnp.float32), taps_x.astype(jnp.float32), segment))
    ssm_act = jax.nn.silu(
        causal_conv(ssm_raw.astype(jnp.float32), conv_bc.astype(jnp.float32), segment)
    )
    b_groups = ssm_act[:, :width_bc].reshape(row_total, GROUPS, STATE)
    c_groups = ssm_act[:, width_bc:].reshape(row_total, GROUPS, STATE)
    select = (head_ids[:, None] // (HEADS // GROUPS) == jnp.arange(GROUPS)[None, :]).astype(
        jnp.float32
    )
    b_heads = jnp.einsum("tgn,hg->thn", b_groups, select, precision=highest)
    c_heads = jnp.einsum("tgn,hg->thn", c_groups, select, precision=highest)
    delta = jax.nn.softplus(dt_raw.astype(jnp.float32) + bias_dt.astype(jnp.float32)[None, :])
    scanned = state_scan(
        x_act.reshape(row_total, heads_here, HEAD_DIM),
        delta,
        rates.astype(jnp.float32),
        b_heads,
        c_heads,
        skips.astype(jnp.float32),
        segment,
    )
    return scanned.reshape(row_total, -1) * jax.nn.silu(z_raw.astype(jnp.float32))


def on_device(
    hidden,
    pre_gain,
    in_x,
    in_z,
    conv_x,
    conv_bc,
    bc_weight,
    dt_weight,
    dt_bias,
    decay_rate,
    skip,
    norm_gain,
    out_weight,
    segment_ids,
    destination,
):
    tensor_count = lax.axis_size("tensor")
    group_count = lax.axis_size("dp")
    shard_count = tensor_count * group_count
    tensor_pos = lax.axis_index("tensor")
    heads_each = in_x.shape[0] // HEAD_DIM
    target = destination[:, 0]
    onehot = (target[:, None] == jnp.arange(shard_count, dtype=jnp.int32)[None, :]).astype(
        jnp.int32
    )
    ranks = jnp.sum((jnp.cumsum(onehot, axis=0) - onehot) * onehot, axis=1)
    slot_ids = target * CAP + ranks
    normed = rms_rows(hidden, pre_gain)
    tokens = lax.all_gather(normed, "tensor", axis=0, tiled=True)
    segment = segment_ids.reshape(-1)
    gathered = (
        lax.all_gather(in_x, "dp", axis=0, tiled=True),
        lax.all_gather(in_z, "dp", axis=0, tiled=True),
        lax.all_gather(conv_x, "dp", axis=0, tiled=True),
        lax.all_gather(dt_weight, "dp", axis=0, tiled=True),
        lax.all_gather(dt_bias, "dp", axis=0, tiled=True),
        lax.all_gather(decay_rate, "dp", axis=0, tiled=True),
        lax.all_gather(skip, "dp", axis=0, tiled=True),
        lax.all_gather(norm_gain, "dp", axis=0, tiled=True),
        lax.all_gather(out_weight, "dp", axis=0, tiled=True),
    )
    params = gathered[:7]
    gain_here = gathered[7]
    proj_out = gathered[8]
    head_ids = jnp.concatenate(
        [
            (member * tensor_count + tensor_pos) * heads_each + jnp.arange(heads_each)
            for member in range(group_count)
        ]
    )
    ssm_part = dot_rows(tokens, bc_weight).astype(jnp.bfloat16)
    ssm_raw = lax.all_gather(ssm_part, "tensor", axis=1, tiled=True)
    gated = mixer_core(tokens, segment, params, head_ids, ssm_raw, conv_bc)
    row_total = gated.shape[0]
    heads_here = head_ids.shape[0]
    group_sel = (head_ids[:, None] // (HEADS // GROUPS) == jnp.arange(GROUPS)[None, :]).astype(
        jnp.float32
    )
    by_head = gated.reshape(row_total, heads_here, HEAD_DIM)
    head_sq = jnp.sum(by_head * by_head, axis=2)
    partial_sq = jnp.dot(head_sq, group_sel, precision=highest)
    total_sq = lax.psum(partial_sq, "tensor")
    head_total = jnp.dot(total_sq, group_sel.T, precision=highest)
    head_scale = lax.rsqrt(head_total / (INNER // GROUPS) + 1e-05)
    scaled = (by_head * head_scale[:, :, None]).reshape(row_total, -1)
    inner = (scaled * gain_here.astype(jnp.float32)[None, :]).astype(jnp.bfloat16)
    mixer = lax.psum_scatter(
        jnp.dot(inner, proj_out, preferred_element_type=jnp.float32),
        "tensor",
        scatter_dimension=0,
        tiled=True,
    )
    layer_out = (hidden.astype(jnp.float32) + mixer).astype(jnp.bfloat16)
    joined = jnp.concatenate([hidden, layer_out], axis=1)
    filled = jnp.zeros((shard_count * CAP, joined.shape[1]), jnp.bfloat16).at[slot_ids].set(joined)
    received = lax.all_to_all(
        filled.reshape(shard_count, CAP, joined.shape[1]),
        ("dp", "tensor"),
        split_axis=0,
        concat_axis=0,
        tiled=True,
    )
    packed = received.reshape(shard_count * CAP, -1)
    return (layer_out, packed)


PLANE = 4
VMEM_LIMIT = 16 * 1024 * 1024
WEIGHT_LIMIT = 28 * 1024 * 1024
NEG = -1e30


def vmem():
    return pl.BlockSpec(memory_space=pltpu.VMEM)


def smem():
    return pl.BlockSpec(memory_space=pltpu.SMEM)


def near(value):
    return pltpu.with_memory_space_constraint(value, pltpu.VMEM)


def far(value):
    return pltpu.with_memory_space_constraint(value, pltpu.MemorySpace.HBM)


def dot_nt(left, right, precision=None):
    return lax.dot_general(
        left, right, (((1,), (1,)), ((), ())), precision=precision, preferred_element_type=jnp.float32
    )


def norm_kernel(spot_ref, *refs, pieces):
    gain_ref, small_ref, normed_ref, bc_ref, dt_ref = refs[sum(pieces) :]
    width = gain_ref.shape[1]
    step = 1024
    taken = 0
    rows = sum(ref.shape[0] for ref in refs[: pieces[0]])
    for index, parts in enumerate(pieces):
        below = 0
        for ref in refs[taken : taken + parts]:
            high = ref.shape[0]
            start = pl.multiple_of((spot_ref[1] ^ index) * rows + below, high)
            total = jnp.zeros((high, 128), jnp.float32)
            for col in range(0, width, step):
                wide = ref[:, col : col + step].astype(jnp.float32)
                square = wide * wide
                for lane in range(0, step, 128):
                    total = total + square[:, lane : lane + 128]
            scale = lax.rsqrt(jnp.sum(total, axis=1, keepdims=True) / width + 1e-05)
            for col in range(0, width, step):
                wide = ref[:, col : col + step].astype(jnp.float32)
                normed_ref[pl.ds(start, high), col : col + step] = (
                    wide * scale * gain_ref[:, col : col + step].astype(jnp.float32)
                ).astype(jnp.bfloat16)
            below += high
        taken += parts
    result = dot_nt(normed_ref[...], small_ref[...]).astype(jnp.bfloat16)
    half = bc_ref.shape[1]
    bc_ref[...] = result[:, :half]
    dt_ref[...] = result[:, half:].astype(jnp.float32)


def norm_plane(spots, blocks, gain, small):
    rows, width = blocks[0][0].shape[0] * PLANE, gain.shape[1]
    flat = [near(part) for block in blocks for part in block]
    return pl.pallas_call(
        functools.partial(norm_kernel, pieces=tuple(len(block) for block in blocks)),
        out_shape=(
            jax.ShapeDtypeStruct((rows, width), jnp.bfloat16),
            jax.ShapeDtypeStruct((rows, small.shape[0] - 128), jnp.bfloat16),
            jax.ShapeDtypeStruct((rows, 128), jnp.float32),
        ),
        in_specs=[smem()] + [vmem()] * (len(flat) + 2),
        out_specs=(vmem(), vmem(), vmem()),
        compiler_params=pltpu.CompilerParams(vmem_limit_bytes=VMEM_LIMIT),
        cost_estimate=pl.CostEstimate(
            flops=1 << 31, bytes_accessed=6 << 20, transcendentals=0
        ),
        name="norm_plane",
    )(spots, *flat, near(gain), near(small))


def flow(sources, held, sems, ahead):
    copies = [
        pltpu.make_async_copy(source, held.at[i], sems.at[i]) for i, source in enumerate(sources)
    ]
    for copy in copies[:ahead]:
        copy.start()

    def take(i):
        copies[i].wait()
        if i + ahead < len(copies):
            copies[i + ahead].start()

    return take


def project_kernel(*refs, planes):
    normed, (wx_ref, wz_ref) = refs[:planes], refs[planes : planes + 2]
    outs, (left, held, sems) = refs[planes + 2 : -3], refs[-3:]
    tile = held.shape[1]
    count = wx_ref.shape[0] // tile
    take = flow(
        [ref.at[pl.ds(i * tile, tile)] for ref in (wx_ref, wz_ref) for i in range(count)], held, sems, 3
    )
    rows = normed[0].shape[0]
    for index, ref in enumerate(normed):
        left[index * rows : (index + 1) * rows, :] = ref[...]
    for i in range(0, 2 * count, 2):
        take(i)
        take(i + 1)
        weight = jnp.concatenate([held[i], held[i + 1]], axis=0)
        result = dot_nt(left[...], weight).astype(jnp.bfloat16)
        col = i % count * tile
        for index in range(planes):
            outs[2 * index + i // count][:, col : col + 2 * tile] = result[
                index * rows : (index + 1) * rows
            ]


def project_planes(normed, in_x, in_z):
    rows, width = normed[0].shape
    cols = in_x.shape[0]
    tile = 128
    pieces = 2 * cols // tile
    count = len(normed)
    far_space = pl.BlockSpec(memory_space=pltpu.MemorySpace.HBM)
    outs = pl.pallas_call(
        functools.partial(project_kernel, planes=count),
        out_shape=(jax.ShapeDtypeStruct((rows, cols), jnp.bfloat16),) * (2 * count),
        in_specs=[vmem()] * count + [far_space, far_space],
        out_specs=(vmem(),) * (2 * count),
        scratch_shapes=[
            pltpu.VMEM((count * rows, width), jnp.bfloat16),
            pltpu.VMEM((pieces, tile, width), jnp.bfloat16),
            pltpu.SemaphoreType.DMA((pieces,)),
        ],
        compiler_params=pltpu.CompilerParams(vmem_limit_bytes=WEIGHT_LIMIT),
        cost_estimate=pl.CostEstimate(
            flops=6 << 30, bytes_accessed=16 << 20, transcendentals=0
        ),
        name="project_planes",
    )(*[near(value) for value in normed], far(in_x), far(in_z))
    return outs[0::2], outs[1::2]


def silu(value):
    return value / (1.0 + jnp.exp(-value))


def scan_kernel(
    spot_ref,
    *refs,
    heads,
    planes,
):
    xs, zs, dts = refs[:planes], refs[planes : 2 * planes], refs[2 * planes : 3 * planes]
    refs = refs[3 * planes :]
    early, late = refs[:2], refs[2:4]
    (taps_x, taps_bc, masks, bias, marks, keep, head_rows, gain_ref) = refs[4:12]
    gated_ref, square_ref = refs[12:14]
    x_all, z_all, dt_all, bc_all = refs[14:]
    z_pos, spot = spot_ref[0], spot_ref[1]
    rows = xs[0].shape[0]
    chans = xs[0].shape[1]
    highest_ = lax.Precision.HIGHEST
    upper = spot >= 2
    ahead = early[0].shape[0] // rows
    x_all[0:8, :] = jnp.zeros((8, chans), jnp.float32)
    bc_all[0:8, :] = jnp.zeros((8, 2 * STATE), jnp.float32)
    for s in range(planes):
        at = pl.multiple_of(lax.rem(z_pos - s + planes, planes) * rows, rows)
        x_all[pl.ds(at + 8, rows), :] = xs[s][...].astype(jnp.float32)
        z_all[pl.ds(at, rows), :] = zs[s][...]
        dt_all[pl.ds(at, rows), :] = dts[s][...]
        part = early if s < ahead else late
        first = (s if s < ahead else s - ahead) * rows
        one, two = [ref[first : first + rows, :].astype(jnp.float32) for ref in part]
        for chip, left, value in (
            (z_pos, 0, jnp.where(upper, two, one)),
            (z_pos + GROUPS, STATE, jnp.where(upper, one, two)),
        ):
            row = lax.rem(lax.div(chip, PLANE // 2) - s + planes, planes) * rows
            row = pl.multiple_of(row, rows)
            bc_all[pl.ds(row + 8, rows), left : left + STATE] = value
    order_i = lax.broadcasted_iota(jnp.int32, (rows, rows), 0)
    order_j = lax.broadcasted_iota(jnp.int32, (rows, rows), 1)
    tri = (order_i >= order_j).astype(jnp.float32)
    lane = lax.broadcasted_iota(jnp.int32, (rows, 128), 1)
    real = lane < heads
    low = lane < HEAD_DIM
    bias_dt, rates = head_rows[0:1, :], head_rows[1:2, :]
    expand = (
        lax.broadcasted_iota(jnp.int32, (128, chans), 0)
        == lax.broadcasted_iota(jnp.int32, (128, chans), 1) // HEAD_DIM
    ).astype(jnp.float32)
    pick_row = lax.broadcasted_iota(jnp.int32, (8, 128), 0)
    lanes_x, lanes_bc = chans // 128, 2 * STATE // 128

    def conv(source, taps, base, count):
        last = taps.shape[0] - 1
        total = source[base + 8 : base + 8 + rows, :] * taps[last : last + 1, :]
        for back in range(1, last + 1):
            same = jnp.concatenate([masks[back - 1, base : base + rows, :]] * count, axis=1)
            total = total + (
                source[base + 8 - back : base + 8 - back + rows, :]
                * taps[last - back : last - back + 1, :]
                * same
            )
        return silu(total)

    state = jnp.zeros((STATE, chans), jnp.float32)
    for p in range(planes):
        base = p * rows
        span = slice(base, base + rows)
        x_act = conv(x_all, taps_x, base, lanes_x)
        bc_act = conv(bc_all, taps_bc, base, lanes_bc).astype(jnp.bfloat16)
        keys, queries = bc_act[:, :STATE], bc_act[:, STATE:]
        raw = dt_all[span, :] + bias_dt
        delta = jnp.maximum(raw, 0.0) + jnp.log1p(jnp.exp(-jnp.abs(raw)))
        delta = jnp.where(real, delta, 0.0)
        cum = jnp.dot(tri, -rates * delta, precision=highest_, preferred_element_type=jnp.float32)
        cum_t = cum.T
        last = cum[rows - 1 : rows, :]
        carried = jnp.where(real, jnp.exp(cum) * marks[0, span, :], 0.0)
        ending = jnp.where(real, jnp.exp(last - cum) * marks[1, span, :] * delta, 0.0)
        decay_end = jnp.where(pick_row == 0, jnp.exp(last) * keep[p : p + 1, :], head_rows[2:3, :])
        decay_end = jnp.where(real[0:8], decay_end, 0.0)
        spread = jnp.dot(
            jnp.concatenate([delta, carried, ending, decay_end], axis=0),
            expand,
            precision=highest_,
            preferred_element_type=jnp.float32,
        )
        delta_x = (spread[:rows] * x_act).astype(jnp.bfloat16)
        end_x = (spread[2 * rows : 3 * rows] * x_act).astype(jnp.bfloat16)
        scores = dot_nt(queries, keys)
        from_state = jnp.dot(queries, state.astype(jnp.bfloat16), preferred_element_type=jnp.float32)
        block_bias = bias[span, :]
        outs = []
        for pair in range(heads // 2):
            both = delta_x[:, pair * 128 : (pair + 1) * 128]
            part = []
            for h in (2 * pair, 2 * pair + 1):
                gap = cum[:, h : h + 1] - cum_t[h : h + 1, :]
                mixing = (jnp.exp(gap + block_bias) * scores).astype(jnp.bfloat16)
                part.append(jnp.dot(mixing, both, preferred_element_type=jnp.float32))
            outs.append(jnp.where(low, part[0], part[1]))
        y = jnp.concatenate(outs, axis=1)
        y = y + spread[rows : 2 * rows] * from_state + spread[3 * rows + 1 : 3 * rows + 2] * x_act
        gated = y * silu(z_all[span, :].astype(jnp.float32))
        square_ref[p : p + 1, :] = dot_nt(
            jnp.ones((8, chans), jnp.float32), gated * gated, precision=highest_
        )[0:1, :]
        gated_ref[span, :] = (gated * gain_ref[...].astype(jnp.float32)).astype(jnp.bfloat16)
        if p + 1 < planes:
            fresh = lax.dot_general(
                keys, end_x, (((0,), (0,)), ((), ())), preferred_element_type=jnp.float32
            )
            state = spread[3 * rows : 3 * rows + 1] * state + fresh


def scan_all(spots, xs, zs, dts, early, late, consts, heads):
    planes = len(xs)
    rows, chans = xs[0].shape
    return pl.pallas_call(
        functools.partial(scan_kernel, heads=heads, planes=planes),
        out_shape=(
            jax.ShapeDtypeStruct((planes * rows, chans), jnp.bfloat16),
            jax.ShapeDtypeStruct((8, rows), jnp.float32),
        ),
        in_specs=[smem()] + [vmem()] * (3 * planes + 4 + len(consts)),
        out_specs=(vmem(), vmem()),
        scratch_shapes=[
            pltpu.VMEM((planes * rows + 8, chans), jnp.float32),
            pltpu.VMEM((planes * rows, chans), jnp.bfloat16),
            pltpu.VMEM((planes * rows, 128), jnp.float32),
            pltpu.VMEM((planes * rows + 8, 2 * STATE), jnp.float32),
        ],
        compiler_params=pltpu.CompilerParams(vmem_limit_bytes=VMEM_LIMIT),
        cost_estimate=pl.CostEstimate(flops=1 << 30, bytes_accessed=8 << 20, transcendentals=0),
        name="scan_all",
    )(spots, *[near(v) for v in (*xs, *zs, *dts, *early, *late, *consts)])


def out_kernel(spots, gated_ref, weight_ref, *refs, planes, first):
    outs, (held, sems) = refs[:-2], refs[-2:]
    tile = held.shape[2]
    take = flow(
        [weight_ref.at[:, pl.ds(first + i * tile, tile)] for i in range(held.shape[0])], held, sems, 3
    )
    rows = gated_ref.shape[0] // planes // PLANE
    level, side = lax.div(spots[1], 2), lax.rem(spots[1], 2)
    parts = []
    for at_side in (1 - side, side):
        for step in range(planes):
            plane = lax.rem(spots[0] - 1 - step + planes, planes)
            for at_level in (1 - level, level):
                at = pl.multiple_of(((plane * 2 + at_level) * 2 + at_side) * rows, rows)
                parts.append(gated_ref[pl.ds(at, rows), :])
    left = jnp.concatenate(parts, axis=0)
    for i in range(held.shape[0]):
        take(i)
        result = jnp.dot(left, held[i], preferred_element_type=jnp.float32).astype(jnp.bfloat16)
        at = 0
        for out in outs:
            out[:, i * tile : (i + 1) * tile] = result[at : at + out.shape[0]]
            at += out.shape[0]


def out_part(spots, gated, weight, planes, first, width):
    chans = weight.shape[0]
    rows = gated.shape[0] // planes // PLANE
    tile = 1024
    shapes = [2 * rows] * planes + [rows] * (2 * planes)
    outs = pl.pallas_call(
        functools.partial(out_kernel, planes=planes, first=first),
        out_shape=tuple(jax.ShapeDtypeStruct((high, width), jnp.bfloat16) for high in shapes),
        in_specs=[smem(), vmem(), pl.BlockSpec(memory_space=pltpu.MemorySpace.HBM)],
        out_specs=(vmem(),) * len(shapes),
        scratch_shapes=[
            pltpu.VMEM((width // tile, chans, tile), jnp.bfloat16),
            pltpu.SemaphoreType.DMA((width // tile,)),
        ],
        compiler_params=pltpu.CompilerParams(vmem_limit_bytes=VMEM_LIMIT),
        cost_estimate=pl.CostEstimate(flops=3 << 30, bytes_accessed=8 << 20, transcendentals=0),
        name="out_part",
    )(spots, near(gated), far(weight))
    return outs[:planes], outs[planes::2], outs[planes + 1 :: 2]


def pick_kernel(spots, *refs, pieces, step, planes, chained):
    parts, out_ref = refs[: sum(pieces)], refs[-1]
    width = out_ref.shape[1]
    code = jnp.concatenate([ref[:, width:] for ref in parts], axis=0).astype(jnp.float32)
    total = code.shape[0]
    rows = total // PLANE
    me = spots[0] * PLANE + spots[1]
    match = code == me.astype(jnp.float32)
    row = lax.broadcasted_iota(jnp.int32, (total, total), 0)
    col = lax.broadcasted_iota(jnp.int32, (total, total), 1)
    before = (row > col) & (row // rows == col // rows)
    rank = jnp.dot(
        before.astype(jnp.bfloat16), match.astype(jnp.bfloat16), preferred_element_type=jnp.float32
    )
    plane = lax.rem(spots[0] - step + planes, planes)
    slot = ((plane * PLANE + (spots[1] ^ (row // rows))) * CAP).astype(jnp.float32) + rank
    select = (match & (slot == col.astype(jnp.float32))).astype(jnp.float32)
    select = select.T[: out_ref.shape[0]].astype(jnp.bfloat16)
    tile = 1024
    for at in range(0, width, tile):
        raw = jnp.concatenate([ref[:, at : at + tile] for ref in parts], axis=0)
        result = jnp.dot(select, raw, preferred_element_type=jnp.float32)
        if chained:
            result = result + refs[-2][:, at : at + tile].astype(jnp.float32)
        out_ref[:, at : at + tile] = result.astype(jnp.bfloat16)


def pick_plane(spots, blocks, earlier, slots, width, step, planes):
    flat = [near(part) for block in blocks for part in block]
    chain = [] if earlier is None else [near(earlier)]
    return pl.pallas_call(
        functools.partial(
            pick_kernel,
            pieces=tuple(len(block) for block in blocks),
            step=step,
            planes=planes,
            chained=bool(chain),
        ),
        out_shape=jax.ShapeDtypeStruct((slots, width), jnp.bfloat16),
        in_specs=[smem()] + [vmem()] * (len(flat) + len(chain)),
        out_specs=vmem(),
        compiler_params=pltpu.CompilerParams(vmem_limit_bytes=VMEM_LIMIT),
        cost_estimate=pl.CostEstimate(flops=1 << 30, bytes_accessed=3 << 20, transcendentals=0),
        name="pick_plane",
    )(spots, *flat, *chain)


def marks_kernel(col_ref, row_ref, masks_ref, bias_ref, marks_ref, keep_ref, padded, *, planes):
    total = col_ref.shape[0]
    rows = total // planes
    col = col_ref[...]
    padded[0:8, :] = jnp.full((8, 128), -1.0, jnp.float32)
    padded[8:, :] = col
    for back in range(1, masks_ref.shape[0] + 1):
        masks_ref[back - 1] = (padded[8 - back : 8 - back + total, :] == col).astype(jnp.float32)
    order = lax.broadcasted_iota(jnp.int32, (rows, rows), 0) >= lax.broadcasted_iota(
        jnp.int32, (rows, rows), 1
    )
    keep_ref[...] = jnp.zeros(keep_ref.shape, jnp.float32)
    for p in range(planes):
        span = slice(p * rows, (p + 1) * rows)
        block = col[span]
        bias_ref[span, :] = jnp.where((block == row_ref[p : p + 1, :]) & order, 0.0, NEG)
        previous = padded[p * rows + 7 : p * rows + 8, :]
        final = block[rows - 1 : rows]
        marks_ref[0, span, :] = (block == previous).astype(jnp.float32)
        marks_ref[1, span, :] = (block == final).astype(jnp.float32)
        keep_ref[p : p + 1, :] = (previous == final).astype(jnp.float32)


def scan_constants(
    segment_ids, conv_x, conv_bc, dt_bias, decay_rate, skip, norm_gain, z_pos, planes
):
    f32 = jnp.float32
    heads = dt_bias.shape[0]
    segment = segment_ids.reshape(-1).astype(f32)
    total = segment.shape[0]
    rows = total // planes
    column = jnp.broadcast_to(segment[:, None], (total, 128))
    lines = jnp.pad(segment.reshape(planes, rows), ((0, 8 - planes), (0, 0)))
    back = conv_x.shape[1] - 1
    masks, bias, marks, keep = pl.pallas_call(
        functools.partial(marks_kernel, planes=planes),
        out_shape=(
            jax.ShapeDtypeStruct((back, total, 128), f32),
            jax.ShapeDtypeStruct((total, rows), f32),
            jax.ShapeDtypeStruct((2, total, 128), f32),
            jax.ShapeDtypeStruct((8, 128), f32),
        ),
        in_specs=[vmem(), vmem()],
        out_specs=(vmem(),) * 4,
        scratch_shapes=[pltpu.VMEM((total + 8, 128), f32)],
        compiler_params=pltpu.CompilerParams(vmem_limit_bytes=VMEM_LIMIT),
        cost_estimate=pl.CostEstimate(flops=1 << 20, bytes_accessed=2 << 20, transcendentals=0),
        name="scan_marks",
    )(column, lines)
    head_rows = jnp.pad(
        jnp.stack([dt_bias, decay_rate, skip]).astype(f32), ((0, 5), (0, 128 - heads))
    )
    width_bc = GROUPS * STATE
    taps_bc = jnp.concatenate(
        [
            lax.dynamic_slice_in_dim(conv_bc, z_pos * STATE + start, STATE, axis=0)
            for start in (0, width_bc)
        ],
        axis=0,
    )
    return (
        conv_x.astype(f32).T,
        taps_bc.astype(f32).T,
        masks,
        bias,
        marks,
        keep,
        head_rows,
        norm_gain[None, :],
    )


def on_device_planes(
    hidden,
    pre_gain,
    in_x,
    in_z,
    conv_x,
    conv_bc,
    bc_weight,
    dt_weight,
    dt_bias,
    decay_rate,
    skip,
    norm_gain,
    out_weight,
    segment_ids,
    destination,
):
    count = lax.axis_size("tensor")
    planes = count // PLANE
    me = lax.axis_index("tensor")
    z_pos, spot = me // PLANE, me % PLANE
    rows, width = hidden.shape
    heads = dt_weight.shape[0]
    every = range(count)
    ring = [(t, (t + PLANE) % count) for t in every]
    over_y = [(t, t ^ 2) for t in every]
    over_core = [(t, t ^ 1) for t in every]

    def permute(value, pairs):
        return lax.ppermute(value, "tensor", pairs)

    f32 = jnp.float32
    small = jnp.concatenate(
        [bc_weight, dt_weight, jnp.zeros((128 - heads, width), dt_weight.dtype)], axis=0
    )
    gain_row = pre_gain[None, :]
    spots = jnp.stack([z_pos, spot]).astype(jnp.int32)

    own = jnp.concatenate(
        [hidden, jnp.broadcast_to(destination.astype(jnp.bfloat16), (rows, 128))], axis=1
    )
    half = rows // 2
    straight, crossed = [[own]], []
    straight_core, crossed_core = [], []
    results = []
    early = picked = None
    spec = (segment_ids, conv_x, conv_bc, dt_bias, decay_rate, skip, norm_gain)

    def exchange(piece):
        other = permute(piece, over_core)
        own_first = jnp.concatenate([piece, other], axis=1)
        both = jnp.where(me % 2 == 0, own_first, jnp.concatenate([other, piece], axis=1))
        result = []
        for turn in range(2):
            pairs = []
            for t in every:
                chip, side = t // 2, t % 2
                kind, plane = chip // GROUPS, chip % GROUPS
                pairs.append((t, plane * PLANE + (kind ^ turn) * 2 + side))
            result.append(permute(both, pairs))
        return result

    def over(parts, pairs):
        return [permute(part, pairs) for part in parts]

    def blocks_of(step):
        return [straight[step], straight_core[step], crossed[step], crossed_core[step]]

    def compute(step):
        return norm_plane(spots, blocks_of(step), gain_row, small)

    def pick(step, earlier):
        return pick_plane(spots, blocks_of(step), earlier, count * CAP, width, step, planes)

    def own_slots(dest):
        target = dest[:, 0]
        onehot = (target[:, None] == jnp.arange(count, dtype=jnp.int32)[None, :]).astype(jnp.int32)
        ranks = jnp.sum((jnp.cumsum(onehot, axis=0) - onehot) * onehot, axis=1)
        slots = target * CAP + ranks
        return (slots[None, :] == jnp.arange(count * CAP)[:, None]).astype(jnp.bfloat16)

    for step in range(planes):
        last = step + 1 == planes
        group = [over(straight[step], over_core)]
        if last:
            group.append(
                [permute(straight[step][0][:half], over_y), permute(crossed[step - 1][0][half:], ring)]
            )
        else:
            group.append(over(straight[step], over_y))
            group.append(over(straight[step], ring))
        if step:
            crossed_core.append(over(crossed[step - 1], over_core))
        extra = {}
        if step == 0:
            extra["spec"] = (spec, destination)
        else:
            extra["result"] = compute(step - 1)
            picked = pick(step - 1, picked)
        if step == 1:
            extra["consts"] = scan_constants(*spec, z_pos, planes)
            extra["place"] = own_slots(own_dest)
        if step == 2:
            extra["first"] = project_planes([results[0][0], extra["result"][0]], in_x, in_z)
        if last:
            extra["early"] = exchange(
                jnp.concatenate([result[1] for result in results[:2]], axis=0)
            )
        group, extra, picked = lax.optimization_barrier((group, extra, picked))
        straight_core.append(group[0])
        crossed.append(group[1])
        if not last:
            straight.append(group[2])
        if step:
            results.append(extra["result"])
        else:
            spec, own_dest = extra["spec"]
        if step == 1:
            consts, place = extra["consts"], extra["place"]
        if step == 2:
            first = extra["first"]
        if last:
            early = extra["early"]
    crossed_core.append(over(crossed[-1], over_core))
    results.append(compute(planes - 1))

    normed, pieces, dts = zip(*results)
    late = exchange(jnp.concatenate(pieces[2:], axis=0))
    second = project_planes(normed[2:], in_x, in_z)
    xs, zs = [first[i] + second[i] for i in range(2)]
    gated, squares = scan_all(spots, xs, zs, dts, early, late, consts, heads)

    squares = squares + permute(squares, over_core)
    squares = squares + permute(squares, over_y)
    scale = lax.rsqrt(squares[:planes].reshape(-1) / (INNER // GROUPS) + 1e-05)

    parts = 2
    part = width // parts
    mine = [
        lax.dynamic_slice_in_dim(scale, ((z_pos - 1 - step) % planes * PLANE + spot) * rows, rows)[:, None]
        for step in range(planes)
    ]
    kept, got_y = [], []
    for index in range(parts):
        away, send, keep = out_part(spots, gated, out_weight, planes, index * part, part)
        got = over(away, over_core)
        send = [
            (send[step].astype(f32) + got[step][:rows].astype(f32)).astype(jnp.bfloat16)
            for step in range(planes)
        ]
        kept.append([(keep[step], got[step][rows:]) for step in range(planes)])
        got_y.append(over(send, over_y))
    travelling = [None] * parts
    totals = [None] * parts
    for step in range(planes):
        for index in range(parts):
            low, high = kept[index][step]
            total = low.astype(f32) + high.astype(f32)
            total = (total + got_y[index][step].astype(f32)) * mine[step]
            if step:
                total = total + travelling[index].astype(f32)
            if step + 1 < planes:
                travelling[index] = permute(total.astype(jnp.bfloat16), ring)
            totals[index] = total
        if step == 0:
            picked, travelling[0] = lax.optimization_barrier((pick(planes - 1, picked), travelling[0]))
    layer_out = (hidden.astype(f32) + jnp.concatenate(totals, axis=1)).astype(jnp.bfloat16)

    filled = jnp.dot(place, layer_out, preferred_element_type=f32).astype(jnp.bfloat16)
    received = lax.all_to_all(
        filled.reshape(count, CAP, width), "tensor", split_axis=0, concat_axis=0, tiled=True
    )
    packed = jnp.concatenate([picked, received.reshape(count * CAP, width)], axis=1)
    return (layer_out, packed)


def solution(mesh):
    planar = mesh.shape["dp"] == 1 and mesh.shape["tensor"] == PLANE * GROUPS
    return jax.shard_map(
        on_device_planes if planar else on_device,
        mesh=mesh,
        in_specs=(
            P(("rep", "dp", "tensor"), None),
            P(),
            P(("dp", "tensor"), None),
            P(("dp", "tensor"), None),
            P(("dp", "tensor"), None),
            P(),
            P("tensor", None),
            P(("dp", "tensor"), None),
            P(("dp", "tensor")),
            P(("dp", "tensor")),
            P(("dp", "tensor")),
            P(("dp", "tensor")),
            P(("dp", "tensor"), None),
            P(("rep", "dp"), None),
            P(("rep", "dp", "tensor"), None),
        ),
        out_specs=(P(("rep", "dp", "tensor"), None), P(("rep", "dp", "tensor"), None)),
        check_vma=False,
    )
```

```python
import functools

import jax
import jax.numpy as jnp
from jax import lax
from jax.experimental import pallas as pl
from jax.experimental.pallas import tpu as pltpu
from jax.sharding import PartitionSpec as P

HEAD_DIM = 64
INNER = 8192
HEADS = 128
STATE = 128
GROUPS = 4
BLOCK = 128
CAP = 2


highest = lax.Precision.HIGHEST


def dot_rows(left, right):
    return lax.dot_general(
        left, right, (((1,), (1,)), ((), ())), preferred_element_type=jnp.float32
    )


def rms_rows(values, scale):
    wide = values.astype(jnp.float32)
    meansq = jnp.mean(wide * wide, axis=-1, keepdims=True)
    return (wide * lax.rsqrt(meansq + 1e-05) * scale.astype(jnp.float32)).astype(jnp.bfloat16)


def causal_conv(signal, kernel, segment):
    length = signal.shape[0]
    taps_count = kernel.shape[1]
    result = jnp.zeros(signal.shape, jnp.float32)
    for offset in range(taps_count):
        steps_back = taps_count - 1 - offset
        shifted = jnp.pad(signal, ((steps_back, 0), (0, 0)))[:length]
        shifted_seg = jnp.pad(segment, (steps_back, 0), constant_values=-1)[:length]
        same = (shifted_seg == segment).astype(jnp.float32)
        result = result + shifted * kernel[:, offset][None, :] * same[:, None]
    return result


def state_scan(inputs, deltas, rates, keys_b, queries_c, skips, segment):
    total, heads_n, dim_p = inputs.shape
    count = total // BLOCK
    order = jnp.arange(BLOCK)

    def advance(carry, block):
        state, previous = carry
        block_x, block_dt, block_b, block_c, block_seg = block
        cumul = jnp.cumsum(-rates[None, :] * block_dt, axis=0)
        allowed = (block_seg[:, None] == block_seg[None, :]) & (order[:, None] >= order[None, :])
        gaps = cumul[:, None, :] - cumul[None, :, :]
        decays = jnp.where(
            allowed[:, :, None], jnp.exp(jnp.where(allowed[:, :, None], gaps, 0.0)), 0.0
        )
        scores = jnp.einsum("ihn,jhn->ijh", block_c, block_b, precision=highest)
        mixing = scores * decays * block_dt[None, :, :]
        output = jnp.einsum("ijh,jhp->ihp", mixing, block_x, precision=highest)
        carried = (block_seg == previous).astype(jnp.float32)
        from_state = jnp.einsum("ihn,hpn->ihp", block_c, state, precision=highest)
        output = output + (carried[:, None] * jnp.exp(cumul))[:, :, None] * from_state
        output = output + skips[None, :, None] * block_x
        final_seg = block_seg[BLOCK - 1]
        ending = (block_seg == final_seg).astype(jnp.float32)
        weights_end = jnp.exp(cumul[BLOCK - 1][None, :] - cumul) * block_dt * ending[:, None]
        keeping = (previous == final_seg).astype(jnp.float32)
        fresh = jnp.einsum("jh,jhp,jhn->hpn", weights_end, block_x, block_b, precision=highest)
        state = keeping * jnp.exp(cumul[BLOCK - 1])[:, None, None] * state + fresh
        return ((state, final_seg), output)

    blocks = (
        inputs.reshape(count, BLOCK, heads_n, dim_p),
        deltas.reshape(count, BLOCK, heads_n),
        keys_b.reshape(count, BLOCK, heads_n, -1),
        queries_c.reshape(count, BLOCK, heads_n, -1),
        segment.reshape(count, BLOCK),
    )
    start = (jnp.zeros((heads_n, dim_p, keys_b.shape[-1]), jnp.float32), jnp.array(-1, jnp.int32))
    carry_end, outputs = lax.scan(advance, start, blocks)
    return outputs.reshape(total, heads_n, dim_p)


def mixer_core(tokens, segment, params, head_ids, ssm_raw, conv_bc):
    proj_x, proj_z, taps_x, proj_dt, bias_dt, rates, skips = params
    row_total = tokens.shape[0]
    heads_here = head_ids.shape[0]
    width_bc = GROUPS * STATE
    x_raw = dot_rows(tokens, proj_x).astype(jnp.bfloat16)
    z_raw = dot_rows(tokens, proj_z).astype(jnp.bfloat16)
    dt_raw = dot_rows(tokens, proj_dt).astype(jnp.bfloat16)
    x_act = jax.nn.silu(causal_conv(x_raw.astype(jnp.float32), taps_x.astype(jnp.float32), segment))
    ssm_act = jax.nn.silu(
        causal_conv(ssm_raw.astype(jnp.float32), conv_bc.astype(jnp.float32), segment)
    )
    b_groups = ssm_act[:, :width_bc].reshape(row_total, GROUPS, STATE)
    c_groups = ssm_act[:, width_bc:].reshape(row_total, GROUPS, STATE)
    select = (head_ids[:, None] // (HEADS // GROUPS) == jnp.arange(GROUPS)[None, :]).astype(
        jnp.float32
    )
    b_heads = jnp.einsum("tgn,hg->thn", b_groups, select, precision=highest)
    c_heads = jnp.einsum("tgn,hg->thn", c_groups, select, precision=highest)
    delta = jax.nn.softplus(dt_raw.astype(jnp.float32) + bias_dt.astype(jnp.float32)[None, :])
    scanned = state_scan(
        x_act.reshape(row_total, heads_here, HEAD_DIM),
        delta,
        rates.astype(jnp.float32),
        b_heads,
        c_heads,
        skips.astype(jnp.float32),
        segment,
    )
    return scanned.reshape(row_total, -1) * jax.nn.silu(z_raw.astype(jnp.float32))


def on_device(
    hidden,
    pre_gain,
    in_x,
    in_z,
    conv_x,
    conv_bc,
    bc_weight,
    dt_weight,
    dt_bias,
    decay_rate,
    skip,
    norm_gain,
    out_weight,
    segment_ids,
    destination,
):
    tensor_count = lax.axis_size("tensor")
    group_count = lax.axis_size("dp")
    shard_count = tensor_count * group_count
    tensor_pos = lax.axis_index("tensor")
    heads_each = in_x.shape[0] // HEAD_DIM
    target = destination[:, 0]
    onehot = (target[:, None] == jnp.arange(shard_count, dtype=jnp.int32)[None, :]).astype(
        jnp.int32
    )
    ranks = jnp.sum((jnp.cumsum(onehot, axis=0) - onehot) * onehot, axis=1)
    slot_ids = target * CAP + ranks
    normed = rms_rows(hidden, pre_gain)
    tokens = lax.all_gather(normed, "tensor", axis=0, tiled=True)
    segment = segment_ids.reshape(-1)
    gathered = (
        lax.all_gather(in_x, "dp", axis=0, tiled=True),
        lax.all_gather(in_z, "dp", axis=0, tiled=True),
        lax.all_gather(conv_x, "dp", axis=0, tiled=True),
        lax.all_gather(dt_weight, "dp", axis=0, tiled=True),
        lax.all_gather(dt_bias, "dp", axis=0, tiled=True),
        lax.all_gather(decay_rate, "dp", axis=0, tiled=True),
        lax.all_gather(skip, "dp", axis=0, tiled=True),
        lax.all_gather(norm_gain, "dp", axis=0, tiled=True),
        lax.all_gather(out_weight, "dp", axis=0, tiled=True),
    )
    params = gathered[:7]
    gain_here = gathered[7]
    proj_out = gathered[8]
    head_ids = jnp.concatenate(
        [
            (member * tensor_count + tensor_pos) * heads_each + jnp.arange(heads_each)
            for member in range(group_count)
        ]
    )
    ssm_part = dot_rows(tokens, bc_weight).astype(jnp.bfloat16)
    ssm_raw = lax.all_gather(ssm_part, "tensor", axis=1, tiled=True)
    gated = mixer_core(tokens, segment, params, head_ids, ssm_raw, conv_bc)
    row_total = gated.shape[0]
    heads_here = head_ids.shape[0]
    group_sel = (head_ids[:, None] // (HEADS // GROUPS) == jnp.arange(GROUPS)[None, :]).astype(
        jnp.float32
    )
    by_head = gated.reshape(row_total, heads_here, HEAD_DIM)
    head_sq = jnp.sum(by_head * by_head, axis=2)
    partial_sq = jnp.dot(head_sq, group_sel, precision=highest)
    total_sq = lax.psum(partial_sq, "tensor")
    head_total = jnp.dot(total_sq, group_sel.T, precision=highest)
    head_scale = lax.rsqrt(head_total / (INNER // GROUPS) + 1e-05)
    scaled = (by_head * head_scale[:, :, None]).reshape(row_total, -1)
    inner = (scaled * gain_here.astype(jnp.float32)[None, :]).astype(jnp.bfloat16)
    mixer = lax.psum_scatter(
        jnp.dot(inner, proj_out, preferred_element_type=jnp.float32),
        "tensor",
        scatter_dimension=0,
        tiled=True,
    )
    layer_out = (hidden.astype(jnp.float32) + mixer).astype(jnp.bfloat16)
    joined = jnp.concatenate([hidden, layer_out], axis=1)
    filled = jnp.zeros((shard_count * CAP, joined.shape[1]), jnp.bfloat16).at[slot_ids].set(joined)
    received = lax.all_to_all(
        filled.reshape(shard_count, CAP, joined.shape[1]),
        ("dp", "tensor"),
        split_axis=0,
        concat_axis=0,
        tiled=True,
    )
    packed = received.reshape(shard_count * CAP, -1)
    return (layer_out, packed)


PLANE = 4
VMEM_LIMIT = 9 * 1024 * 1024
NEG = -1e30


def vmem():
    return pl.BlockSpec(memory_space=pltpu.VMEM)


def smem():
    return pl.BlockSpec(memory_space=pltpu.SMEM)


def near(value):
    return pltpu.with_memory_space_constraint(value, pltpu.VMEM)


def far(value):
    return pltpu.with_memory_space_constraint(value, pltpu.MemorySpace.HBM)


def dot_nt(left, right, precision=None):
    return lax.dot_general(
        left, right, (((1,), (1,)), ((), ())), precision=precision, preferred_element_type=jnp.float32
    )


def norm_kernel(spot_ref, *refs, pieces, held):
    gain_ref, small_ref, *rest = refs[sum(pieces) :]
    weights, (normed_ref, bc_ref, dt_ref) = rest[:held], rest[held : held + 3]
    copies = [
        pltpu.make_async_copy(weight, rest[held + 3 + i], rest[-1].at[i])
        for i, weight in enumerate(weights)
    ]
    for copy in copies:
        copy.start()
    width = gain_ref.shape[1]
    step = 1024
    taken = 0
    rows = sum(ref.shape[0] for ref in refs[: pieces[0]])
    for index, parts in enumerate(pieces):
        below = 0
        for ref in refs[taken : taken + parts]:
            high = ref.shape[0]
            start = pl.multiple_of((spot_ref[1] ^ index) * rows + below, high)
            total = jnp.zeros((high, 128), jnp.float32)
            for col in range(0, width, step):
                wide = ref[:, col : col + step].astype(jnp.float32)
                square = wide * wide
                for lane in range(0, step, 128):
                    total = total + square[:, lane : lane + 128]
            scale = lax.rsqrt(jnp.sum(total, axis=1, keepdims=True) / width + 1e-05)
            for col in range(0, width, step):
                wide = ref[:, col : col + step].astype(jnp.float32)
                normed_ref[pl.ds(start, high), col : col + step] = (
                    wide * scale * gain_ref[:, col : col + step].astype(jnp.float32)
                ).astype(jnp.bfloat16)
            below += high
        taken += parts
    result = dot_nt(normed_ref[...], small_ref[...]).astype(jnp.bfloat16)
    half = bc_ref.shape[1]
    bc_ref[...] = result[:, :half]
    dt_ref[...] = result[:, half:].astype(jnp.float32)
    for copy in copies:
        copy.wait()


def norm_plane(spots, blocks, gain, small, late, weights):
    rows, width = blocks[0][0].shape[0] * PLANE, gain.shape[1]
    flat = [near(part) for block in blocks for part in block]
    return pl.pallas_call(
        functools.partial(
            norm_kernel, pieces=tuple(len(block) for block in blocks), held=len(weights)
        ),
        out_shape=(
            (pltpu.VMEM if late else jax.ShapeDtypeStruct)((rows, width), jnp.bfloat16),
            jax.ShapeDtypeStruct((rows, small.shape[0] - 128), jnp.bfloat16),
            jax.ShapeDtypeStruct((rows, 128), jnp.float32),
            *[pltpu.VMEM(weight.shape, weight.dtype) for weight in weights],
        ),
        in_specs=[smem()]
        + [vmem()] * (len(flat) + 2)
        + [pl.BlockSpec(memory_space=pltpu.MemorySpace.HBM)] * len(weights),
        out_specs=(vmem(),) * (3 + len(weights)),
        scratch_shapes=[pltpu.SemaphoreType.DMA((len(weights),))] if weights else [],
        compiler_params=pltpu.CompilerParams(vmem_limit_bytes=VMEM_LIMIT),
        cost_estimate=pl.CostEstimate(
            flops=1 << 31, bytes_accessed=6 << 20, transcendentals=0
        ),
        name="norm_plane",
    )(spots, *flat, near(gain), near(small), *[far(weight) for weight in weights])


def project_kernel(*refs, planes):
    normed, weights = refs[:planes], refs[planes : planes + 2]
    outs, left = refs[planes + 2 : -1], refs[-1]
    tile = 256
    rows = normed[0].shape[0]
    for index, ref in enumerate(normed):
        left[index * rows : (index + 1) * rows, :] = ref[...]
    for which, weight in enumerate(weights):
        for col in range(0, weight.shape[0], tile):
            result = dot_nt(left[...], weight[col : col + tile, :]).astype(jnp.bfloat16)
            for index in range(planes):
                outs[2 * index + which][:, col : col + tile] = result[index * rows : (index + 1) * rows]


def project_planes(normed, in_x, in_z):
    rows, width = normed[0].shape
    cols = in_x.shape[0]
    count = len(normed)
    outs = pl.pallas_call(
        functools.partial(project_kernel, planes=count),
        out_shape=(jax.ShapeDtypeStruct((rows, cols), jnp.bfloat16),) * (2 * count),
        in_specs=[vmem()] * (count + 2),
        out_specs=(vmem(),) * (2 * count),
        scratch_shapes=[pltpu.VMEM((count * rows, width), jnp.bfloat16)],
        compiler_params=pltpu.CompilerParams(vmem_limit_bytes=VMEM_LIMIT),
        cost_estimate=pl.CostEstimate(
            flops=4 << 30, bytes_accessed=4 << 20, transcendentals=0
        ),
        name="project_planes",
    )(*[near(value) for value in normed], near(in_x), near(in_z))
    return outs[0::2], outs[1::2]


def silu(value):
    return value / (1.0 + jnp.exp(-value))


def scan_kernel(
    spot_ref,
    *refs,
    heads,
    planes,
):
    xs, zs, dts = refs[:planes], refs[planes : 2 * planes], refs[2 * planes : 3 * planes]
    refs = refs[3 * planes :]
    far_pieces = refs[:2]
    (taps_x, taps_bc, masks, bias, marks, keep, head_rows, gain_ref) = refs[2:10]
    weight_ref, gated_ref, square_ref, held_ref = refs[10:14]
    x_all, z_all, dt_all, bc_all, sem = refs[14:]
    held_copy = pltpu.make_async_copy(weight_ref, held_ref, sem)
    held_copy.start()
    z_pos, spot = spot_ref[0], spot_ref[1]
    rows = xs[0].shape[0]
    chans = xs[0].shape[1]
    highest_ = lax.Precision.HIGHEST
    upper = spot >= 2
    x_all[0:8, :] = jnp.zeros((8, chans), jnp.float32)
    bc_all[0:8, :] = jnp.zeros((8, 2 * STATE), jnp.float32)
    for s in range(planes):
        at = pl.multiple_of(lax.rem(z_pos - s + planes, planes) * rows, rows)
        x_all[pl.ds(at + 8, rows), :] = xs[s][...].astype(jnp.float32)
        z_all[pl.ds(at, rows), :] = zs[s][...]
        dt_all[pl.ds(at, rows), :] = dts[s][...]
        one, two = [
            ref[s * rows : (s + 1) * rows, :].astype(jnp.float32) for ref in far_pieces
        ]
        for chip, left, value in (
            (z_pos, 0, jnp.where(upper, two, one)),
            (z_pos + GROUPS, STATE, jnp.where(upper, one, two)),
        ):
            row = lax.rem(lax.div(chip, PLANE // 2) - s + planes, planes) * rows
            row = pl.multiple_of(row, rows)
            bc_all[pl.ds(row + 8, rows), left : left + STATE] = value
    order_i = lax.broadcasted_iota(jnp.int32, (rows, rows), 0)
    order_j = lax.broadcasted_iota(jnp.int32, (rows, rows), 1)
    tri = (order_i >= order_j).astype(jnp.float32)
    lane = lax.broadcasted_iota(jnp.int32, (rows, 128), 1)
    real = lane < heads
    low = lane < HEAD_DIM
    bias_dt, rates = head_rows[0:1, :], head_rows[1:2, :]
    expand = (
        lax.broadcasted_iota(jnp.int32, (128, chans), 0)
        == lax.broadcasted_iota(jnp.int32, (128, chans), 1) // HEAD_DIM
    ).astype(jnp.float32)
    pick_row = lax.broadcasted_iota(jnp.int32, (8, 128), 0)
    lanes_x, lanes_bc = chans // 128, 2 * STATE // 128

    def conv(source, taps, base, count):
        last = taps.shape[0] - 1
        total = source[base + 8 : base + 8 + rows, :] * taps[last : last + 1, :]
        for back in range(1, last + 1):
            same = jnp.concatenate([masks[back - 1, base : base + rows, :]] * count, axis=1)
            total = total + (
                source[base + 8 - back : base + 8 - back + rows, :]
                * taps[last - back : last - back + 1, :]
                * same
            )
        return silu(total)

    state = jnp.zeros((STATE, chans), jnp.float32)
    for p in range(planes):
        base = p * rows
        span = slice(base, base + rows)
        x_act = conv(x_all, taps_x, base, lanes_x)
        bc_act = conv(bc_all, taps_bc, base, lanes_bc).astype(jnp.bfloat16)
        keys, queries = bc_act[:, :STATE], bc_act[:, STATE:]
        raw = dt_all[span, :] + bias_dt
        delta = jnp.maximum(raw, 0.0) + jnp.log1p(jnp.exp(-jnp.abs(raw)))
        delta = jnp.where(real, delta, 0.0)
        cum = jnp.dot(tri, -rates * delta, precision=highest_, preferred_element_type=jnp.float32)
        cum_t = cum.T
        last = cum[rows - 1 : rows, :]
        carried = jnp.where(real, jnp.exp(cum) * marks[0, span, :], 0.0)
        ending = jnp.where(real, jnp.exp(last - cum) * marks[1, span, :] * delta, 0.0)
        decay_end = jnp.where(pick_row == 0, jnp.exp(last) * keep[p : p + 1, :], head_rows[2:3, :])
        decay_end = jnp.where(real[0:8], decay_end, 0.0)
        spread = jnp.dot(
            jnp.concatenate([delta, carried, ending, decay_end], axis=0),
            expand,
            precision=highest_,
            preferred_element_type=jnp.float32,
        )
        delta_x = (spread[:rows] * x_act).astype(jnp.bfloat16)
        end_x = (spread[2 * rows : 3 * rows] * x_act).astype(jnp.bfloat16)
        scores = dot_nt(queries, keys)
        from_state = jnp.dot(queries, state.astype(jnp.bfloat16), preferred_element_type=jnp.float32)
        block_bias = bias[span, :]
        outs = []
        for pair in range(heads // 2):
            both = delta_x[:, pair * 128 : (pair + 1) * 128]
            part = []
            for h in (2 * pair, 2 * pair + 1):
                gap = cum[:, h : h + 1] - cum_t[h : h + 1, :]
                mixing = (jnp.exp(gap + block_bias) * scores).astype(jnp.bfloat16)
                part.append(jnp.dot(mixing, both, preferred_element_type=jnp.float32))
            outs.append(jnp.where(low, part[0], part[1]))
        y = jnp.concatenate(outs, axis=1)
        y = y + spread[rows : 2 * rows] * from_state + spread[3 * rows + 1 : 3 * rows + 2] * x_act
        gated = y * silu(z_all[span, :].astype(jnp.float32))
        square_ref[p : p + 1, :] = dot_nt(
            jnp.ones((8, chans), jnp.float32), gated * gated, precision=highest_
        )[0:1, :]
        gated_ref[span, :] = (gated * gain_ref[...].astype(jnp.float32)).astype(jnp.bfloat16)
        if p + 1 < planes:
            fresh = lax.dot_general(
                keys, end_x, (((0,), (0,)), ((), ())), preferred_element_type=jnp.float32
            )
            state = spread[3 * rows : 3 * rows + 1] * state + fresh
    held_copy.wait()


def pair_kernel(spots, *refs):
    *pieces, out_ref = refs
    count = len(pieces) // 2
    rows, cols = pieces[0].shape
    first = lax.rem(spots[1], 2) == 0
    for i in range(count):
        own, other = pieces[i][...].astype(jnp.float32), pieces[count + i][...].astype(jnp.float32)
        span = slice(i * rows, (i + 1) * rows)
        out_ref[span, :] = jnp.concatenate(
            [jnp.where(first, own, other), jnp.where(first, other, own)], axis=1
        ).astype(jnp.bfloat16)


def pair_pieces(spots, own, other):
    rows, cols = own[0].shape
    return pl.pallas_call(
        pair_kernel,
        out_shape=jax.ShapeDtypeStruct((len(own) * rows, 2 * cols), jnp.bfloat16),
        in_specs=[smem()] + [vmem()] * (2 * len(own)),
        out_specs=vmem(),
        compiler_params=pltpu.CompilerParams(vmem_limit_bytes=VMEM_LIMIT),
        cost_estimate=pl.CostEstimate(flops=1 << 20, bytes_accessed=1 << 20, transcendentals=0),
        name="pair_pieces",
    )(spots, *[near(value) for value in (*own, *other)])


def scan_all(spots, xs, zs, dts, far_pieces, consts, weight, heads):
    planes = len(xs)
    rows, chans = xs[0].shape
    return pl.pallas_call(
        functools.partial(scan_kernel, heads=heads, planes=planes),
        out_shape=(
            jax.ShapeDtypeStruct((planes * rows, chans), jnp.bfloat16),
            jax.ShapeDtypeStruct((8, rows), jnp.float32),
            pltpu.VMEM(weight.shape, weight.dtype),
        ),
        in_specs=[smem()]
        + [vmem()] * (3 * planes + 2 + len(consts))
        + [pl.BlockSpec(memory_space=pltpu.MemorySpace.HBM)],
        out_specs=(vmem(), vmem(), vmem()),
        scratch_shapes=[
            pltpu.VMEM((planes * rows + 8, chans), jnp.float32),
            pltpu.VMEM((planes * rows, chans), jnp.bfloat16),
            pltpu.VMEM((planes * rows, 128), jnp.float32),
            pltpu.VMEM((planes * rows + 8, 2 * STATE), jnp.float32),
            pltpu.SemaphoreType.DMA,
        ],
        compiler_params=pltpu.CompilerParams(vmem_limit_bytes=VMEM_LIMIT),
        cost_estimate=pl.CostEstimate(flops=1 << 30, bytes_accessed=8 << 20, transcendentals=0),
        name="scan_all",
    )(spots, *[near(v) for v in (*xs, *zs, *dts, *far_pieces, *consts)], far(weight))


def out_kernel(spots, gated_ref, weight_ref, *outs, planes, steps):
    rows = gated_ref.shape[0] // planes // PLANE
    level, side = lax.div(spots[1], 2), lax.rem(spots[1], 2)
    parts = []
    for step in steps:
        plane = lax.rem(spots[0] - 1 - step + planes, planes)
        for at_side in (1 - side, side):
            for at_level in (1 - level, level):
                at = pl.multiple_of(((plane * 2 + at_level) * 2 + at_side) * rows, rows)
                parts.append(gated_ref[pl.ds(at, rows), :])
    left = jnp.concatenate(parts, axis=0)
    tile = 1024
    for col in range(0, weight_ref.shape[1], tile):
        result = jnp.dot(
            left, weight_ref[:, col : col + tile], preferred_element_type=jnp.float32
        ).astype(jnp.bfloat16)
        at = 0
        for out in outs:
            out[:, col : col + tile] = result[at : at + out.shape[0]]
            at += out.shape[0]


def out_part(spots, gated, weight, planes, steps):
    width = weight.shape[1]
    rows = gated.shape[0] // planes // PLANE
    shapes = [2 * rows, rows, rows] * len(steps)
    outs = pl.pallas_call(
        functools.partial(out_kernel, planes=planes, steps=steps),
        out_shape=tuple(jax.ShapeDtypeStruct((high, width), jnp.bfloat16) for high in shapes),
        in_specs=[smem(), vmem(), vmem()],
        out_specs=(vmem(),) * len(shapes),
        compiler_params=pltpu.CompilerParams(vmem_limit_bytes=VMEM_LIMIT),
        cost_estimate=pl.CostEstimate(
            flops=len(steps) << 30, bytes_accessed=len(steps) << 21, transcendentals=0
        ),
        name="out_part",
    )(spots, near(gated), near(weight))
    return [outs[i : i + 3] for i in range(0, len(outs), 3)]


def pick_kernel(spots, *refs, pieces, step, planes, chained):
    parts, out_ref = refs[: sum(pieces)], refs[-1]
    width = out_ref.shape[1]
    code = jnp.concatenate([ref[:, width:] for ref in parts], axis=0).astype(jnp.float32)
    total = code.shape[0]
    rows = total // PLANE
    me = spots[0] * PLANE + spots[1]
    match = code == me.astype(jnp.float32)
    row = lax.broadcasted_iota(jnp.int32, (total, total), 0)
    col = lax.broadcasted_iota(jnp.int32, (total, total), 1)
    before = (row > col) & (row // rows == col // rows)
    rank = jnp.dot(
        before.astype(jnp.bfloat16), match.astype(jnp.bfloat16), preferred_element_type=jnp.float32
    )
    plane = lax.rem(spots[0] - step + planes, planes)
    slot = ((plane * PLANE + (spots[1] ^ (row // rows))) * CAP).astype(jnp.float32) + rank
    select = (match & (slot == col.astype(jnp.float32))).astype(jnp.float32)
    select = select.T[: out_ref.shape[0]].astype(jnp.bfloat16)
    tile = 1024
    for at in range(0, width, tile):
        raw = jnp.concatenate([ref[:, at : at + tile] for ref in parts], axis=0)
        result = jnp.dot(select, raw, preferred_element_type=jnp.float32)
        if chained:
            result = result + refs[-2][:, at : at + tile].astype(jnp.float32)
        out_ref[:, at : at + tile] = result.astype(jnp.bfloat16)


def pick_plane(spots, blocks, earlier, slots, width, step, planes):
    flat = [near(part) for block in blocks for part in block]
    chain = [] if earlier is None else [near(earlier)]
    return pl.pallas_call(
        functools.partial(
            pick_kernel,
            pieces=tuple(len(block) for block in blocks),
            step=step,
            planes=planes,
            chained=bool(chain),
        ),
        out_shape=jax.ShapeDtypeStruct((slots, width), jnp.bfloat16),
        in_specs=[smem()] + [vmem()] * (len(flat) + len(chain)),
        out_specs=vmem(),
        compiler_params=pltpu.CompilerParams(vmem_limit_bytes=VMEM_LIMIT),
        cost_estimate=pl.CostEstimate(flops=1 << 30, bytes_accessed=3 << 20, transcendentals=0),
        name="pick_plane",
    )(spots, *flat, *chain)


def marks_kernel(col_ref, row_ref, masks_ref, bias_ref, marks_ref, keep_ref, padded, *, planes):
    total = col_ref.shape[0]
    rows = total // planes
    col = col_ref[...]
    padded[0:8, :] = jnp.full((8, 128), -1.0, jnp.float32)
    padded[8:, :] = col
    for back in range(1, masks_ref.shape[0] + 1):
        masks_ref[back - 1] = (padded[8 - back : 8 - back + total, :] == col).astype(jnp.float32)
    order = lax.broadcasted_iota(jnp.int32, (rows, rows), 0) >= lax.broadcasted_iota(
        jnp.int32, (rows, rows), 1
    )
    keep_ref[...] = jnp.zeros(keep_ref.shape, jnp.float32)
    for p in range(planes):
        span = slice(p * rows, (p + 1) * rows)
        block = col[span]
        bias_ref[span, :] = jnp.where((block == row_ref[p : p + 1, :]) & order, 0.0, NEG)
        previous = padded[p * rows + 7 : p * rows + 8, :]
        final = block[rows - 1 : rows]
        marks_ref[0, span, :] = (block == previous).astype(jnp.float32)
        marks_ref[1, span, :] = (block == final).astype(jnp.float32)
        keep_ref[p : p + 1, :] = (previous == final).astype(jnp.float32)


def scan_constants(
    segment_ids, conv_x, conv_bc, dt_bias, decay_rate, skip, norm_gain, z_pos, planes
):
    f32 = jnp.float32
    heads = dt_bias.shape[0]
    segment = segment_ids.reshape(-1).astype(f32)
    total = segment.shape[0]
    rows = total // planes
    column = jnp.broadcast_to(segment[:, None], (total, 128))
    lines = jnp.pad(segment.reshape(planes, rows), ((0, 8 - planes), (0, 0)))
    back = conv_x.shape[1] - 1
    masks, bias, marks, keep = pl.pallas_call(
        functools.partial(marks_kernel, planes=planes),
        out_shape=(
            jax.ShapeDtypeStruct((back, total, 128), f32),
            jax.ShapeDtypeStruct((total, rows), f32),
            jax.ShapeDtypeStruct((2, total, 128), f32),
            jax.ShapeDtypeStruct((8, 128), f32),
        ),
        in_specs=[vmem(), vmem()],
        out_specs=(vmem(),) * 4,
        scratch_shapes=[pltpu.VMEM((total + 8, 128), f32)],
        compiler_params=pltpu.CompilerParams(vmem_limit_bytes=VMEM_LIMIT),
        cost_estimate=pl.CostEstimate(flops=1 << 20, bytes_accessed=2 << 20, transcendentals=0),
        name="scan_marks",
    )(column, lines)
    head_rows = jnp.pad(
        jnp.stack([dt_bias, decay_rate, skip]).astype(f32), ((0, 5), (0, 128 - heads))
    )
    width_bc = GROUPS * STATE
    taps_bc = jnp.concatenate(
        [
            lax.dynamic_slice_in_dim(conv_bc, z_pos * STATE + start, STATE, axis=0)
            for start in (0, width_bc)
        ],
        axis=0,
    )
    return (
        conv_x.astype(f32).T,
        taps_bc.astype(f32).T,
        masks,
        bias,
        marks,
        keep,
        head_rows,
        norm_gain[None, :],
    )


def on_device_planes(
    hidden,
    pre_gain,
    in_x,
    in_z,
    conv_x,
    conv_bc,
    bc_weight,
    dt_weight,
    dt_bias,
    decay_rate,
    skip,
    norm_gain,
    out_weight,
    segment_ids,
    destination,
):
    count = lax.axis_size("tensor")
    planes = count // PLANE
    me = lax.axis_index("tensor")
    z_pos, spot = me // PLANE, me % PLANE
    rows, width = hidden.shape
    heads = dt_weight.shape[0]
    every = range(count)
    ring = [(t, (t + PLANE) % count) for t in every]
    over_y = [(t, t ^ 2) for t in every]
    over_core = [(t, t ^ 1) for t in every]

    def permute(value, pairs):
        return lax.ppermute(value, "tensor", pairs)

    f32 = jnp.float32
    small = jnp.concatenate(
        [bc_weight, dt_weight, jnp.zeros((128 - heads, width), dt_weight.dtype)], axis=0
    )
    gain_row = pre_gain[None, :]
    spots = jnp.stack([z_pos, spot]).astype(jnp.int32)

    own = jnp.concatenate(
        [hidden, jnp.broadcast_to(destination.astype(jnp.bfloat16), (rows, 128))], axis=1
    )
    half = rows // 2
    straight, crossed = [[own]], []
    straight_core, crossed_core = [], []
    results = []
    picked = None
    peers = []
    spec = (segment_ids, conv_x, conv_bc, dt_bias, decay_rate, skip, norm_gain)

    def send_far(both):
        result = []
        for turn in range(2):
            pairs = []
            for t in every:
                chip, side = t // 2, t % 2
                kind, plane = chip // GROUPS, chip % GROUPS
                pairs.append((t, plane * PLANE + (kind ^ turn) * 2 + side))
            result.append(permute(both, pairs))
        return result

    def over(parts, pairs):
        return [permute(part, pairs) for part in parts]

    def blocks_of(step):
        return [straight[step], straight_core[step], crossed[step], crossed_core[step]]

    def compute(step, *weights):
        return norm_plane(spots, blocks_of(step), gain_row, small, step >= 2, weights)

    def pick(step, earlier):
        return pick_plane(spots, blocks_of(step), earlier, count * CAP, width, step, planes)

    def own_slots(dest):
        target = dest[:, 0]
        onehot = (target[:, None] == jnp.arange(count, dtype=jnp.int32)[None, :]).astype(jnp.int32)
        ranks = jnp.sum((jnp.cumsum(onehot, axis=0) - onehot) * onehot, axis=1)
        slots = target * CAP + ranks
        return (slots[None, :] == jnp.arange(count * CAP)[:, None]).astype(jnp.bfloat16)

    for step in range(planes):
        last = step + 1 == planes
        group = [over(straight[step], over_core)]
        if last:
            group.append(
                [permute(straight[step][0][:half], over_y), permute(crossed[step - 1][0][half:], ring)]
            )
        else:
            group.append(over(straight[step], over_y))
            group.append(over(straight[step], ring))
        if step:
            crossed_core.append(over(crossed[step - 1], over_core))
        extra = {}
        if step == 0:
            extra["spec"] = (spec, destination)
        else:
            extra["result"] = compute(step - 1)
            if step < 3:
                picked = pick(step - 1, picked)
        if step == 1:
            extra["consts"] = scan_constants(*spec, z_pos, planes)
            extra["place"] = own_slots(own_dest)
        if step == 2:
            extra["first"] = project_planes([results[0][0], extra["result"][0]], in_x, in_z)
        if step >= 2:
            extra["peer"] = permute(results[step - 2][1], over_core)
        group, extra, picked = lax.optimization_barrier((group, extra, picked))
        straight_core.append(group[0])
        crossed.append(group[1])
        if not last:
            straight.append(group[2])
        if step:
            results.append(extra["result"])
        else:
            spec, own_dest = extra["spec"]
        if step == 1:
            consts, place = extra["consts"], extra["place"]
        if step == 2:
            first = extra["first"]
        if step >= 2:
            peers.append(extra["peer"])
    crossed_core.append(over(crossed[-1], over_core))
    *result, near_x, near_z = compute(planes - 1, in_x, in_z)
    results.append(result)

    normed, pieces, dts = zip(*results)
    peers += over(pieces[2:], over_core)
    both = pair_pieces(spots, pieces, peers)
    both, normed = lax.optimization_barrier((both, normed[2:]))
    far_pieces = send_far(both)
    second = project_planes(normed, near_x, near_z)
    xs, zs = [first[i] + second[i] for i in range(2)]
    gated, squares, held_out = scan_all(spots, xs, zs, dts, far_pieces, consts, out_weight, heads)

    squares = squares + permute(squares, over_core)
    squares = squares + permute(squares, over_y)
    scale = lax.rsqrt(squares[:planes].reshape(-1) / (INNER // GROUPS) + 1e-05)

    mine = [
        lax.dynamic_slice_in_dim(scale, ((z_pos - 1 - step) % planes * PLANE + spot) * rows, rows)[:, None]
        for step in range(planes)
    ]
    outs = out_part(spots, gated, held_out, planes, (0,))
    got = [permute(outs[0][0], over_core)]
    outs += out_part(spots, gated, held_out, planes, tuple(range(1, planes)))
    got += [permute(away, over_core) for away, _, _ in outs[1:]]
    total = None
    for step in range(planes):
        send = (outs[step][1].astype(f32) + got[step][:rows].astype(f32)).astype(jnp.bfloat16)
        group = [permute(send, over_y)]
        if step:
            group.append(permute(total.astype(jnp.bfloat16), ring))
        if step in (1, 2):
            picked = pick(planes - 3 + step, picked)
        group, got, picked, outs = lax.optimization_barrier((group, got, picked, outs))
        total = outs[step][2].astype(f32) + got[step][rows:].astype(f32)
        total = (total + group[0].astype(f32)) * mine[step]
        if step:
            total = total + group[1].astype(f32)
    layer_out = (hidden.astype(f32) + total).astype(jnp.bfloat16)

    filled = jnp.dot(place, layer_out, preferred_element_type=f32).astype(jnp.bfloat16)
    received = lax.all_to_all(
        filled.reshape(count, CAP, width), "tensor", split_axis=0, concat_axis=0, tiled=True
    )
    packed = jnp.concatenate([picked, received.reshape(count * CAP, width)], axis=1)
    return (layer_out, packed)


def solution(mesh):
    planar = mesh.shape["dp"] == 1 and mesh.shape["tensor"] == PLANE * GROUPS
    return jax.shard_map(
        on_device_planes if planar else on_device,
        mesh=mesh,
        in_specs=(
            P(("rep", "dp", "tensor"), None),
            P(),
            P(("dp", "tensor"), None),
            P(("dp", "tensor"), None),
            P(("dp", "tensor"), None),
            P(),
            P("tensor", None),
            P(("dp", "tensor"), None),
            P(("dp", "tensor")),
            P(("dp", "tensor")),
            P(("dp", "tensor")),
            P(("dp", "tensor")),
            P(("dp", "tensor"), None),
            P(("rep", "dp"), None),
            P(("rep", "dp", "tensor"), None),
        ),
        out_specs=(P(("rep", "dp", "tensor"), None), P(("rep", "dp", "tensor"), None)),
        check_vma=False,
    )
```

```python
import functools

import jax
import jax.numpy as jnp
from jax import lax
from jax.experimental import pallas as pl
from jax.experimental.pallas import tpu as pltpu
from jax.sharding import PartitionSpec as P

HEAD_DIM = 64
INNER = 8192
HEADS = 128
STATE = 128
GROUPS = 4
BLOCK = 128
CAP = 2


highest = lax.Precision.HIGHEST


def dot_rows(left, right):
    return lax.dot_general(
        left, right, (((1,), (1,)), ((), ())), preferred_element_type=jnp.float32
    )


def rms_rows(values, scale):
    wide = values.astype(jnp.float32)
    meansq = jnp.mean(wide * wide, axis=-1, keepdims=True)
    return (wide * lax.rsqrt(meansq + 1e-05) * scale.astype(jnp.float32)).astype(jnp.bfloat16)


def causal_conv(signal, kernel, segment):
    length = signal.shape[0]
    taps_count = kernel.shape[1]
    result = jnp.zeros(signal.shape, jnp.float32)
    for offset in range(taps_count):
        steps_back = taps_count - 1 - offset
        shifted = jnp.pad(signal, ((steps_back, 0), (0, 0)))[:length]
        shifted_seg = jnp.pad(segment, (steps_back, 0), constant_values=-1)[:length]
        same = (shifted_seg == segment).astype(jnp.float32)
        result = result + shifted * kernel[:, offset][None, :] * same[:, None]
    return result


def state_scan(inputs, deltas, rates, keys_b, queries_c, skips, segment):
    total, heads_n, dim_p = inputs.shape
    count = total // BLOCK
    order = jnp.arange(BLOCK)

    def advance(carry, block):
        state, previous = carry
        block_x, block_dt, block_b, block_c, block_seg = block
        cumul = jnp.cumsum(-rates[None, :] * block_dt, axis=0)
        allowed = (block_seg[:, None] == block_seg[None, :]) & (order[:, None] >= order[None, :])
        gaps = cumul[:, None, :] - cumul[None, :, :]
        decays = jnp.where(
            allowed[:, :, None], jnp.exp(jnp.where(allowed[:, :, None], gaps, 0.0)), 0.0
        )
        scores = jnp.einsum("ihn,jhn->ijh", block_c, block_b, precision=highest)
        mixing = scores * decays * block_dt[None, :, :]
        output = jnp.einsum("ijh,jhp->ihp", mixing, block_x, precision=highest)
        carried = (block_seg == previous).astype(jnp.float32)
        from_state = jnp.einsum("ihn,hpn->ihp", block_c, state, precision=highest)
        output = output + (carried[:, None] * jnp.exp(cumul))[:, :, None] * from_state
        output = output + skips[None, :, None] * block_x
        final_seg = block_seg[BLOCK - 1]
        ending = (block_seg == final_seg).astype(jnp.float32)
        weights_end = jnp.exp(cumul[BLOCK - 1][None, :] - cumul) * block_dt * ending[:, None]
        keeping = (previous == final_seg).astype(jnp.float32)
        fresh = jnp.einsum("jh,jhp,jhn->hpn", weights_end, block_x, block_b, precision=highest)
        state = keeping * jnp.exp(cumul[BLOCK - 1])[:, None, None] * state + fresh
        return ((state, final_seg), output)

    blocks = (
        inputs.reshape(count, BLOCK, heads_n, dim_p),
        deltas.reshape(count, BLOCK, heads_n),
        keys_b.reshape(count, BLOCK, heads_n, -1),
        queries_c.reshape(count, BLOCK, heads_n, -1),
        segment.reshape(count, BLOCK),
    )
    start = (jnp.zeros((heads_n, dim_p, keys_b.shape[-1]), jnp.float32), jnp.array(-1, jnp.int32))
    carry_end, outputs = lax.scan(advance, start, blocks)
    return outputs.reshape(total, heads_n, dim_p)


def mixer_core(tokens, segment, params, head_ids, ssm_raw, conv_bc):
    proj_x, proj_z, taps_x, proj_dt, bias_dt, rates, skips = params
    row_total = tokens.shape[0]
    heads_here = head_ids.shape[0]
    width_bc = GROUPS * STATE
    x_raw = dot_rows(tokens, proj_x).astype(jnp.bfloat16)
    z_raw = dot_rows(tokens, proj_z).astype(jnp.bfloat16)
    dt_raw = dot_rows(tokens, proj_dt).astype(jnp.bfloat16)
    x_act = jax.nn.silu(causal_conv(x_raw.astype(jnp.float32), taps_x.astype(jnp.float32), segment))
    ssm_act = jax.nn.silu(
        causal_conv(ssm_raw.astype(jnp.float32), conv_bc.astype(jnp.float32), segment)
    )
    b_groups = ssm_act[:, :width_bc].reshape(row_total, GROUPS, STATE)
    c_groups = ssm_act[:, width_bc:].reshape(row_total, GROUPS, STATE)
    select = (head_ids[:, None] // (HEADS // GROUPS) == jnp.arange(GROUPS)[None, :]).astype(
        jnp.float32
    )
    b_heads = jnp.einsum("tgn,hg->thn", b_groups, select, precision=highest)
    c_heads = jnp.einsum("tgn,hg->thn", c_groups, select, precision=highest)
    delta = jax.nn.softplus(dt_raw.astype(jnp.float32) + bias_dt.astype(jnp.float32)[None, :])
    scanned = state_scan(
        x_act.reshape(row_total, heads_here, HEAD_DIM),
        delta,
        rates.astype(jnp.float32),
        b_heads,
        c_heads,
        skips.astype(jnp.float32),
        segment,
    )
    return scanned.reshape(row_total, -1) * jax.nn.silu(z_raw.astype(jnp.float32))


def on_device(
    hidden,
    pre_gain,
    in_x,
    in_z,
    conv_x,
    conv_bc,
    bc_weight,
    dt_weight,
    dt_bias,
    decay_rate,
    skip,
    norm_gain,
    out_weight,
    segment_ids,
    destination,
):
    tensor_count = lax.axis_size("tensor")
    group_count = lax.axis_size("dp")
    shard_count = tensor_count * group_count
    tensor_pos = lax.axis_index("tensor")
    heads_each = in_x.shape[0] // HEAD_DIM
    target = destination[:, 0]
    onehot = (target[:, None] == jnp.arange(shard_count, dtype=jnp.int32)[None, :]).astype(
        jnp.int32
    )
    ranks = jnp.sum((jnp.cumsum(onehot, axis=0) - onehot) * onehot, axis=1)
    slot_ids = target * CAP + ranks
    normed = rms_rows(hidden, pre_gain)
    tokens = lax.all_gather(normed, "tensor", axis=0, tiled=True)
    segment = segment_ids.reshape(-1)
    gathered = (
        lax.all_gather(in_x, "dp", axis=0, tiled=True),
        lax.all_gather(in_z, "dp", axis=0, tiled=True),
        lax.all_gather(conv_x, "dp", axis=0, tiled=True),
        lax.all_gather(dt_weight, "dp", axis=0, tiled=True),
        lax.all_gather(dt_bias, "dp", axis=0, tiled=True),
        lax.all_gather(decay_rate, "dp", axis=0, tiled=True),
        lax.all_gather(skip, "dp", axis=0, tiled=True),
        lax.all_gather(norm_gain, "dp", axis=0, tiled=True),
        lax.all_gather(out_weight, "dp", axis=0, tiled=True),
    )
    params = gathered[:7]
    gain_here = gathered[7]
    proj_out = gathered[8]
    head_ids = jnp.concatenate(
        [
            (member * tensor_count + tensor_pos) * heads_each + jnp.arange(heads_each)
            for member in range(group_count)
        ]
    )
    ssm_part = dot_rows(tokens, bc_weight).astype(jnp.bfloat16)
    ssm_raw = lax.all_gather(ssm_part, "tensor", axis=1, tiled=True)
    gated = mixer_core(tokens, segment, params, head_ids, ssm_raw, conv_bc)
    row_total = gated.shape[0]
    heads_here = head_ids.shape[0]
    group_sel = (head_ids[:, None] // (HEADS // GROUPS) == jnp.arange(GROUPS)[None, :]).astype(
        jnp.float32
    )
    by_head = gated.reshape(row_total, heads_here, HEAD_DIM)
    head_sq = jnp.sum(by_head * by_head, axis=2)
    partial_sq = jnp.dot(head_sq, group_sel, precision=highest)
    total_sq = lax.psum(partial_sq, "tensor")
    head_total = jnp.dot(total_sq, group_sel.T, precision=highest)
    head_scale = lax.rsqrt(head_total / (INNER // GROUPS) + 1e-05)
    scaled = (by_head * head_scale[:, :, None]).reshape(row_total, -1)
    inner = (scaled * gain_here.astype(jnp.float32)[None, :]).astype(jnp.bfloat16)
    mixer = lax.psum_scatter(
        jnp.dot(inner, proj_out, preferred_element_type=jnp.float32),
        "tensor",
        scatter_dimension=0,
        tiled=True,
    )
    layer_out = (hidden.astype(jnp.float32) + mixer).astype(jnp.bfloat16)
    joined = jnp.concatenate([hidden, layer_out], axis=1)
    filled = jnp.zeros((shard_count * CAP, joined.shape[1]), jnp.bfloat16).at[slot_ids].set(joined)
    received = lax.all_to_all(
        filled.reshape(shard_count, CAP, joined.shape[1]),
        ("dp", "tensor"),
        split_axis=0,
        concat_axis=0,
        tiled=True,
    )
    packed = received.reshape(shard_count * CAP, -1)
    return (layer_out, packed)


PLANE = 4
VMEM_LIMIT = 9 * 1024 * 1024
NEG = -1e30


def vmem():
    return pl.BlockSpec(memory_space=pltpu.VMEM)


def smem():
    return pl.BlockSpec(memory_space=pltpu.SMEM)


def near(value):
    return pltpu.with_memory_space_constraint(value, pltpu.VMEM)


def far(value):
    return pltpu.with_memory_space_constraint(value, pltpu.MemorySpace.HBM)


def dot_nt(left, right, precision=None):
    return lax.dot_general(
        left, right, (((1,), (1,)), ((), ())), precision=precision, preferred_element_type=jnp.float32
    )


def norm_kernel(spot_ref, *refs, pieces, held):
    gain_ref, small_ref, *rest = refs[sum(pieces) :]
    weights, (normed_ref, bc_ref, dt_ref) = rest[:held], rest[held : held + 3]
    copies = [
        pltpu.make_async_copy(weight, rest[held + 3 + i], rest[-1].at[i])
        for i, weight in enumerate(weights)
    ]
    for copy in copies:
        copy.start()
    width = gain_ref.shape[1]
    step = 1024
    taken = 0
    rows = sum(ref.shape[0] for ref in refs[: pieces[0]])
    for index, parts in enumerate(pieces):
        below = 0
        for ref in refs[taken : taken + parts]:
            high = ref.shape[0]
            start = pl.multiple_of((spot_ref[1] ^ index) * rows + below, high)
            total = jnp.zeros((high, 128), jnp.float32)
            for col in range(0, width, step):
                wide = ref[:, col : col + step].astype(jnp.float32)
                square = wide * wide
                for lane in range(0, step, 128):
                    total = total + square[:, lane : lane + 128]
            scale = lax.rsqrt(jnp.sum(total, axis=1, keepdims=True) / width + 1e-05)
            for col in range(0, width, step):
                wide = ref[:, col : col + step].astype(jnp.float32)
                normed_ref[pl.ds(start, high), col : col + step] = (
                    wide * scale * gain_ref[:, col : col + step].astype(jnp.float32)
                ).astype(jnp.bfloat16)
            below += high
        taken += parts
    result = dot_nt(normed_ref[...], small_ref[...]).astype(jnp.bfloat16)
    half = bc_ref.shape[1]
    bc_ref[...] = result[:, :half]
    dt_ref[...] = result[:, half:].astype(jnp.float32)
    for copy in copies:
        copy.wait()


def norm_plane(spots, blocks, gain, small, late, weights):
    rows, width = blocks[0][0].shape[0] * PLANE, gain.shape[1]
    flat = [near(part) for block in blocks for part in block]
    return pl.pallas_call(
        functools.partial(
            norm_kernel, pieces=tuple(len(block) for block in blocks), held=len(weights)
        ),
        out_shape=(
            (pltpu.VMEM if late else jax.ShapeDtypeStruct)((rows, width), jnp.bfloat16),
            jax.ShapeDtypeStruct((rows, small.shape[0] - 128), jnp.bfloat16),
            jax.ShapeDtypeStruct((rows, 128), jnp.float32),
            *[pltpu.VMEM(weight.shape, weight.dtype) for weight in weights],
        ),
        in_specs=[smem()]
        + [vmem()] * (len(flat) + 2)
        + [pl.BlockSpec(memory_space=pltpu.MemorySpace.HBM)] * len(weights),
        out_specs=(vmem(),) * (3 + len(weights)),
        scratch_shapes=[pltpu.SemaphoreType.DMA((len(weights),))] if weights else [],
        compiler_params=pltpu.CompilerParams(vmem_limit_bytes=VMEM_LIMIT),
        cost_estimate=pl.CostEstimate(
            flops=1 << 31, bytes_accessed=6 << 20, transcendentals=0
        ),
        name="norm_plane",
    )(spots, *flat, near(gain), near(small), *[far(weight) for weight in weights])


def project_kernel(*refs, planes):
    normed, weights = refs[:planes], refs[planes : planes + 2]
    outs, left = refs[planes + 2 : -1], refs[-1]
    tile = 256
    rows = normed[0].shape[0]
    for index, ref in enumerate(normed):
        left[index * rows : (index + 1) * rows, :] = ref[...]
    for which, weight in enumerate(weights):
        for col in range(0, weight.shape[0], tile):
            result = dot_nt(left[...], weight[col : col + tile, :]).astype(jnp.bfloat16)
            for index in range(planes):
                outs[2 * index + which][:, col : col + tile] = result[index * rows : (index + 1) * rows]


def project_planes(normed, in_x, in_z):
    rows, width = normed[0].shape
    cols = in_x.shape[0]
    count = len(normed)
    outs = pl.pallas_call(
        functools.partial(project_kernel, planes=count),
        out_shape=(jax.ShapeDtypeStruct((rows, cols), jnp.bfloat16),) * (2 * count),
        in_specs=[vmem()] * (count + 2),
        out_specs=(vmem(),) * (2 * count),
        scratch_shapes=[pltpu.VMEM((count * rows, width), jnp.bfloat16)],
        compiler_params=pltpu.CompilerParams(vmem_limit_bytes=VMEM_LIMIT),
        cost_estimate=pl.CostEstimate(
            flops=4 << 30, bytes_accessed=4 << 20, transcendentals=0
        ),
        name="project_planes",
    )(*[near(value) for value in normed], near(in_x), near(in_z))
    return outs[0::2], outs[1::2]


def silu(value):
    return value / (1.0 + jnp.exp(-value))


def scan_kernel(
    spot_ref,
    *refs,
    heads,
    planes,
):
    xs, zs, dts = refs[:planes], refs[planes : 2 * planes], refs[2 * planes : 3 * planes]
    refs = refs[3 * planes :]
    far_pieces = refs[:2]
    (taps_x, taps_bc, masks, bias, marks, keep, head_rows, gain_ref) = refs[2:10]
    weight_ref, gated_ref, square_ref, held_ref = refs[10:14]
    x_all, z_all, dt_all, bc_all, sem = refs[14:]
    held_copy = pltpu.make_async_copy(weight_ref, held_ref, sem)
    held_copy.start()
    z_pos, spot = spot_ref[0], spot_ref[1]
    rows = xs[0].shape[0]
    chans = xs[0].shape[1]
    highest_ = lax.Precision.HIGHEST
    upper = spot >= 2
    x_all[0:8, :] = jnp.zeros((8, chans), jnp.float32)
    bc_all[0:8, :] = jnp.zeros((8, 2 * STATE), jnp.float32)
    for s in range(planes):
        at = pl.multiple_of(lax.rem(z_pos - s + planes, planes) * rows, rows)
        x_all[pl.ds(at + 8, rows), :] = xs[s][...].astype(jnp.float32)
        z_all[pl.ds(at, rows), :] = zs[s][...]
        dt_all[pl.ds(at, rows), :] = dts[s][...]
        one, two = [
            ref[s * rows : (s + 1) * rows, :].astype(jnp.float32) for ref in far_pieces
        ]
        for chip, left, value in (
            (z_pos, 0, jnp.where(upper, two, one)),
            (z_pos + GROUPS, STATE, jnp.where(upper, one, two)),
        ):
            row = lax.rem(lax.div(chip, PLANE // 2) - s + planes, planes) * rows
            row = pl.multiple_of(row, rows)
            bc_all[pl.ds(row + 8, rows), left : left + STATE] = value
    order_i = lax.broadcasted_iota(jnp.int32, (rows, rows), 0)
    order_j = lax.broadcasted_iota(jnp.int32, (rows, rows), 1)
    tri = (order_i >= order_j).astype(jnp.float32)
    lane = lax.broadcasted_iota(jnp.int32, (rows, 128), 1)
    real = lane < heads
    low = lane < HEAD_DIM
    bias_dt, rates = head_rows[0:1, :], head_rows[1:2, :]
    expand = (
        lax.broadcasted_iota(jnp.int32, (128, chans), 0)
        == lax.broadcasted_iota(jnp.int32, (128, chans), 1) // HEAD_DIM
    ).astype(jnp.float32)
    pick_row = lax.broadcasted_iota(jnp.int32, (8, 128), 0)
    lanes_x, lanes_bc = chans // 128, 2 * STATE // 128

    def conv(source, taps, base, count):
        last = taps.shape[0] - 1
        total = source[base + 8 : base + 8 + rows, :] * taps[last : last + 1, :]
        for back in range(1, last + 1):
            same = jnp.concatenate([masks[back - 1, base : base + rows, :]] * count, axis=1)
            total = total + (
                source[base + 8 - back : base + 8 - back + rows, :]
                * taps[last - back : last - back + 1, :]
                * same
            )
        return silu(total)

    state = jnp.zeros((STATE, chans), jnp.float32)
    for p in range(planes):
        base = p * rows
        span = slice(base, base + rows)
        x_act = conv(x_all, taps_x, base, lanes_x)
        bc_act = conv(bc_all, taps_bc, base, lanes_bc).astype(jnp.bfloat16)
        keys, queries = bc_act[:, :STATE], bc_act[:, STATE:]
        raw = dt_all[span, :] + bias_dt
        delta = jnp.maximum(raw, 0.0) + jnp.log1p(jnp.exp(-jnp.abs(raw)))
        delta = jnp.where(real, delta, 0.0)
        cum = jnp.dot(tri, -rates * delta, precision=highest_, preferred_element_type=jnp.float32)
        cum_t = cum.T
        last = cum[rows - 1 : rows, :]
        carried = jnp.where(real, jnp.exp(cum) * marks[0, span, :], 0.0)
        ending = jnp.where(real, jnp.exp(last - cum) * marks[1, span, :] * delta, 0.0)
        decay_end = jnp.where(pick_row == 0, jnp.exp(last) * keep[p : p + 1, :], head_rows[2:3, :])
        decay_end = jnp.where(real[0:8], decay_end, 0.0)
        spread = jnp.dot(
            jnp.concatenate([delta, carried, ending, decay_end], axis=0),
            expand,
            precision=highest_,
            preferred_element_type=jnp.float32,
        )
        delta_x = (spread[:rows] * x_act).astype(jnp.bfloat16)
        end_x = (spread[2 * rows : 3 * rows] * x_act).astype(jnp.bfloat16)
        scores = dot_nt(queries, keys)
        from_state = jnp.dot(queries, state.astype(jnp.bfloat16), preferred_element_type=jnp.float32)
        block_bias = bias[span, :]
        outs = []
        for pair in range(heads // 2):
            both = delta_x[:, pair * 128 : (pair + 1) * 128]
            part = []
            for h in (2 * pair, 2 * pair + 1):
                gap = cum[:, h : h + 1] - cum_t[h : h + 1, :]
                mixing = (jnp.exp(gap + block_bias) * scores).astype(jnp.bfloat16)
                part.append(jnp.dot(mixing, both, preferred_element_type=jnp.float32))
            outs.append(jnp.where(low, part[0], part[1]))
        y = jnp.concatenate(outs, axis=1)
        y = y + spread[rows : 2 * rows] * from_state + spread[3 * rows + 1 : 3 * rows + 2] * x_act
        gated = y * silu(z_all[span, :].astype(jnp.float32))
        square_ref[p : p + 1, :] = dot_nt(
            jnp.ones((8, chans), jnp.float32), gated * gated, precision=highest_
        )[0:1, :]
        gated_ref[span, :] = (gated * gain_ref[...].astype(jnp.float32)).astype(jnp.bfloat16)
        if p + 1 < planes:
            fresh = lax.dot_general(
                keys, end_x, (((0,), (0,)), ((), ())), preferred_element_type=jnp.float32
            )
            state = spread[3 * rows : 3 * rows + 1] * state + fresh
    held_copy.wait()


def pair_kernel(spots, *refs):
    *pieces, out_ref = refs
    count = len(pieces) // 2
    rows, cols = pieces[0].shape
    first = lax.rem(spots[1], 2) == 0
    for i in range(count):
        own, other = pieces[i][...].astype(jnp.float32), pieces[count + i][...].astype(jnp.float32)
        span = slice(i * rows, (i + 1) * rows)
        out_ref[span, :] = jnp.concatenate(
            [jnp.where(first, own, other), jnp.where(first, other, own)], axis=1
        ).astype(jnp.bfloat16)


def pair_pieces(spots, own, other):
    rows, cols = own[0].shape
    return pl.pallas_call(
        pair_kernel,
        out_shape=jax.ShapeDtypeStruct((len(own) * rows, 2 * cols), jnp.bfloat16),
        in_specs=[smem()] + [vmem()] * (2 * len(own)),
        out_specs=vmem(),
        compiler_params=pltpu.CompilerParams(vmem_limit_bytes=VMEM_LIMIT),
        cost_estimate=pl.CostEstimate(flops=1 << 20, bytes_accessed=1 << 20, transcendentals=0),
        name="pair_pieces",
    )(spots, *[near(value) for value in (*own, *other)])


def scan_all(spots, xs, zs, dts, far_pieces, consts, weight, heads):
    planes = len(xs)
    rows, chans = xs[0].shape
    return pl.pallas_call(
        functools.partial(scan_kernel, heads=heads, planes=planes),
        out_shape=(
            jax.ShapeDtypeStruct((planes * rows, chans), jnp.bfloat16),
            jax.ShapeDtypeStruct((8, rows), jnp.float32),
            pltpu.VMEM(weight.shape, weight.dtype),
        ),
        in_specs=[smem()]
        + [vmem()] * (3 * planes + 2 + len(consts))
        + [pl.BlockSpec(memory_space=pltpu.MemorySpace.HBM)],
        out_specs=(vmem(), vmem(), vmem()),
        scratch_shapes=[
            pltpu.VMEM((planes * rows + 8, chans), jnp.float32),
            pltpu.VMEM((planes * rows, chans), jnp.bfloat16),
            pltpu.VMEM((planes * rows, 128), jnp.float32),
            pltpu.VMEM((planes * rows + 8, 2 * STATE), jnp.float32),
            pltpu.SemaphoreType.DMA,
        ],
        compiler_params=pltpu.CompilerParams(vmem_limit_bytes=VMEM_LIMIT),
        cost_estimate=pl.CostEstimate(flops=1 << 30, bytes_accessed=8 << 20, transcendentals=0),
        name="scan_all",
    )(spots, *[near(v) for v in (*xs, *zs, *dts, *far_pieces, *consts)], far(weight))


def out_kernel(spots, gated_ref, weight_ref, *outs, planes, steps):
    rows = gated_ref.shape[0] // planes // PLANE
    level, side = lax.div(spots[1], 2), lax.rem(spots[1], 2)
    parts = []
    for step in steps:
        plane = lax.rem(spots[0] - 1 - step + planes, planes)
        for at_side in (1 - side, side):
            for at_level in (1 - level, level):
                at = pl.multiple_of(((plane * 2 + at_level) * 2 + at_side) * rows, rows)
                parts.append(gated_ref[pl.ds(at, rows), :])
    left = jnp.concatenate(parts, axis=0)
    tile = outs[0].shape[1]
    col = pl.multiple_of(pl.program_id(0) * tile, tile)
    result = jnp.dot(
        left, weight_ref[:, pl.ds(col, tile)], preferred_element_type=jnp.float32
    ).astype(jnp.bfloat16)
    at = 0
    for out in outs:
        out[...] = result[at : at + out.shape[0]]
        at += out.shape[0]


def out_part(spots, gated, weight, planes, steps):
    width = weight.shape[1]
    rows = gated.shape[0] // planes // PLANE
    shapes = [2 * rows, rows, rows] * len(steps)
    tile = 1024
    outs = pl.pallas_call(
        functools.partial(out_kernel, planes=planes, steps=steps),
        grid=(width // tile,),
        out_shape=tuple(pltpu.MemorySpace.HBM((high, width), jnp.bfloat16) for high in shapes),
        in_specs=[smem(), vmem(), vmem()],
        out_specs=tuple(pl.BlockSpec((high, tile), lambda i: (0, i)) for high in shapes),
        compiler_params=pltpu.CompilerParams(vmem_limit_bytes=VMEM_LIMIT),
        cost_estimate=pl.CostEstimate(
            flops=len(steps) << 30, bytes_accessed=len(steps) << 21, transcendentals=0
        ),
        name="out_part",
    )(spots, near(gated), near(weight))
    return [outs[i : i + 3] for i in range(0, len(outs), 3)]


def pick_kernel(spots, *refs, pieces, step, planes, chained):
    parts, out_ref = refs[: sum(pieces)], refs[-1]
    width = out_ref.shape[1]
    code = jnp.concatenate([ref[:, width:] for ref in parts], axis=0).astype(jnp.float32)
    total = code.shape[0]
    rows = total // PLANE
    me = spots[0] * PLANE + spots[1]
    match = code == me.astype(jnp.float32)
    row = lax.broadcasted_iota(jnp.int32, (total, total), 0)
    col = lax.broadcasted_iota(jnp.int32, (total, total), 1)
    before = (row > col) & (row // rows == col // rows)
    rank = jnp.dot(
        before.astype(jnp.bfloat16), match.astype(jnp.bfloat16), preferred_element_type=jnp.float32
    )
    plane = lax.rem(spots[0] - step + planes, planes)
    slot = ((plane * PLANE + (spots[1] ^ (row // rows))) * CAP).astype(jnp.float32) + rank
    select = (match & (slot == col.astype(jnp.float32))).astype(jnp.float32)
    select = select.T[: out_ref.shape[0]].astype(jnp.bfloat16)
    tile = 1024
    for at in range(0, width, tile):
        raw = jnp.concatenate([ref[:, at : at + tile] for ref in parts], axis=0)
        result = jnp.dot(select, raw, preferred_element_type=jnp.float32)
        if chained:
            result = result + refs[-2][:, at : at + tile].astype(jnp.float32)
        out_ref[:, at : at + tile] = result.astype(jnp.bfloat16)


def pick_plane(spots, blocks, earlier, slots, width, step, planes):
    flat = [near(part) for block in blocks for part in block]
    chain = [] if earlier is None else [near(earlier)]
    return pl.pallas_call(
        functools.partial(
            pick_kernel,
            pieces=tuple(len(block) for block in blocks),
            step=step,
            planes=planes,
            chained=bool(chain),
        ),
        out_shape=jax.ShapeDtypeStruct((slots, width), jnp.bfloat16),
        in_specs=[smem()] + [vmem()] * (len(flat) + len(chain)),
        out_specs=vmem(),
        compiler_params=pltpu.CompilerParams(vmem_limit_bytes=VMEM_LIMIT),
        cost_estimate=pl.CostEstimate(flops=1 << 30, bytes_accessed=3 << 20, transcendentals=0),
        name="pick_plane",
    )(spots, *flat, *chain)


def marks_kernel(col_ref, row_ref, masks_ref, bias_ref, marks_ref, keep_ref, padded, *, planes):
    total = col_ref.shape[0]
    rows = total // planes
    col = col_ref[...]
    padded[0:8, :] = jnp.full((8, 128), -1.0, jnp.float32)
    padded[8:, :] = col
    for back in range(1, masks_ref.shape[0] + 1):
        masks_ref[back - 1] = (padded[8 - back : 8 - back + total, :] == col).astype(jnp.float32)
    order = lax.broadcasted_iota(jnp.int32, (rows, rows), 0) >= lax.broadcasted_iota(
        jnp.int32, (rows, rows), 1
    )
    keep_ref[...] = jnp.zeros(keep_ref.shape, jnp.float32)
    for p in range(planes):
        span = slice(p * rows, (p + 1) * rows)
        block = col[span]
        bias_ref[span, :] = jnp.where((block == row_ref[p : p + 1, :]) & order, 0.0, NEG)
        previous = padded[p * rows + 7 : p * rows + 8, :]
        final = block[rows - 1 : rows]
        marks_ref[0, span, :] = (block == previous).astype(jnp.float32)
        marks_ref[1, span, :] = (block == final).astype(jnp.float32)
        keep_ref[p : p + 1, :] = (previous == final).astype(jnp.float32)


def scan_constants(
    segment_ids, conv_x, conv_bc, dt_bias, decay_rate, skip, norm_gain, z_pos, planes
):
    f32 = jnp.float32
    heads = dt_bias.shape[0]
    segment = segment_ids.reshape(-1).astype(f32)
    total = segment.shape[0]
    rows = total // planes
    column = jnp.broadcast_to(segment[:, None], (total, 128))
    lines = jnp.pad(segment.reshape(planes, rows), ((0, 8 - planes), (0, 0)))
    back = conv_x.shape[1] - 1
    masks, bias, marks, keep = pl.pallas_call(
        functools.partial(marks_kernel, planes=planes),
        out_shape=(
            jax.ShapeDtypeStruct((back, total, 128), f32),
            jax.ShapeDtypeStruct((total, rows), f32),
            jax.ShapeDtypeStruct((2, total, 128), f32),
            jax.ShapeDtypeStruct((8, 128), f32),
        ),
        in_specs=[vmem(), vmem()],
        out_specs=(vmem(),) * 4,
        scratch_shapes=[pltpu.VMEM((total + 8, 128), f32)],
        compiler_params=pltpu.CompilerParams(vmem_limit_bytes=VMEM_LIMIT),
        cost_estimate=pl.CostEstimate(flops=1 << 20, bytes_accessed=2 << 20, transcendentals=0),
        name="scan_marks",
    )(column, lines)
    head_rows = jnp.pad(
        jnp.stack([dt_bias, decay_rate, skip]).astype(f32), ((0, 5), (0, 128 - heads))
    )
    width_bc = GROUPS * STATE
    taps_bc = jnp.concatenate(
        [
            lax.dynamic_slice_in_dim(conv_bc, z_pos * STATE + start, STATE, axis=0)
            for start in (0, width_bc)
        ],
        axis=0,
    )
    return (
        conv_x.astype(f32).T,
        taps_bc.astype(f32).T,
        masks,
        bias,
        marks,
        keep,
        head_rows,
        norm_gain[None, :],
    )


def on_device_planes(
    hidden,
    pre_gain,
    in_x,
    in_z,
    conv_x,
    conv_bc,
    bc_weight,
    dt_weight,
    dt_bias,
    decay_rate,
    skip,
    norm_gain,
    out_weight,
    segment_ids,
    destination,
):
    count = lax.axis_size("tensor")
    planes = count // PLANE
    me = lax.axis_index("tensor")
    z_pos, spot = me // PLANE, me % PLANE
    rows, width = hidden.shape
    heads = dt_weight.shape[0]
    every = range(count)
    ring = [(t, (t + PLANE) % count) for t in every]
    over_y = [(t, t ^ 2) for t in every]
    over_core = [(t, t ^ 1) for t in every]

    def permute(value, pairs):
        return lax.ppermute(value, "tensor", pairs)

    f32 = jnp.float32
    small = jnp.concatenate(
        [bc_weight, dt_weight, jnp.zeros((128 - heads, width), dt_weight.dtype)], axis=0
    )
    gain_row = pre_gain[None, :]
    spots = jnp.stack([z_pos, spot]).astype(jnp.int32)

    own = jnp.concatenate(
        [hidden, jnp.broadcast_to(destination.astype(jnp.bfloat16), (rows, 128))], axis=1
    )
    half = rows // 2
    straight, crossed = [[own]], []
    straight_core, crossed_core = [], []
    results = []
    picked = None
    peers = []
    spec = (segment_ids, conv_x, conv_bc, dt_bias, decay_rate, skip, norm_gain)

    def send_far(both):
        result = []
        for turn in range(2):
            pairs = []
            for t in every:
                chip, side = t // 2, t % 2
                kind, plane = chip // GROUPS, chip % GROUPS
                pairs.append((t, plane * PLANE + (kind ^ turn) * 2 + side))
            result.append(permute(both, pairs))
        return result

    def over(parts, pairs):
        return [permute(part, pairs) for part in parts]

    def blocks_of(step):
        return [straight[step], straight_core[step], crossed[step], crossed_core[step]]

    def compute(step, *weights):
        return norm_plane(spots, blocks_of(step), gain_row, small, step >= 2, weights)

    def pick(step, earlier):
        return pick_plane(spots, blocks_of(step), earlier, count * CAP, width, step, planes)

    def own_slots(dest):
        target = dest[:, 0]
        onehot = (target[:, None] == jnp.arange(count, dtype=jnp.int32)[None, :]).astype(jnp.int32)
        ranks = jnp.sum((jnp.cumsum(onehot, axis=0) - onehot) * onehot, axis=1)
        slots = target * CAP + ranks
        return (slots[None, :] == jnp.arange(count * CAP)[:, None]).astype(jnp.bfloat16)

    for step in range(planes):
        last = step + 1 == planes
        group = [over(straight[step], over_core)]
        if last:
            group.append(
                [permute(straight[step][0][:half], over_y), permute(crossed[step - 1][0][half:], ring)]
            )
        else:
            group.append(over(straight[step], over_y))
            group.append(over(straight[step], ring))
        if step:
            crossed_core.append(over(crossed[step - 1], over_core))
        extra = {}
        if step == 0:
            extra["spec"] = (spec, destination)
        else:
            extra["result"] = compute(step - 1, *([in_x] if last else []))
            picked = pick(step - 1, picked)
        if step == 1:
            extra["consts"] = scan_constants(*spec, z_pos, planes)
            extra["place"] = own_slots(own_dest)
        if step == 2:
            extra["first"] = project_planes([results[0][0], extra["result"][0]], in_x, in_z)
        if step >= 2:
            extra["peer"] = permute(results[step - 2][1], over_core)
        group, extra, picked = lax.optimization_barrier((group, extra, picked))
        straight_core.append(group[0])
        crossed.append(group[1])
        if not last:
            straight.append(group[2])
        if step:
            result = extra["result"]
            results.append(result[:3])
            near_x = result[3] if last else None
        else:
            spec, own_dest = extra["spec"]
        if step == 1:
            consts, place = extra["consts"], extra["place"]
        if step == 2:
            first = extra["first"]
        if step >= 2:
            peers.append(extra["peer"])
    crossed_core.append(over(crossed[-1], over_core))
    *result, near_z = compute(planes - 1, in_z)
    results.append(result)

    normed, pieces, dts = zip(*results)
    peers += over(pieces[2:], over_core)
    both = pair_pieces(spots, pieces, peers)
    both, normed = lax.optimization_barrier((both, normed[2:]))
    far_pieces = send_far(both)
    second = project_planes(normed, near_x, near_z)
    far_pieces, picked = lax.optimization_barrier((far_pieces, pick(planes - 1, picked)))
    xs, zs = [first[i] + second[i] for i in range(2)]
    gated, squares, held_out = scan_all(spots, xs, zs, dts, far_pieces, consts, out_weight, heads)

    squares = squares + permute(squares, over_core)
    squares = squares + permute(squares, over_y)
    scale = lax.rsqrt(squares[:planes].reshape(-1) / (INNER // GROUPS) + 1e-05)

    def scale_of(step, at_spot):
        start = ((z_pos - 1 - step) % planes * PLANE + at_spot) * rows
        return lax.dynamic_slice_in_dim(scale, start, rows)[:, None]

    mine = [scale_of(step, spot) for step in range(planes)]
    theirs = [scale_of(step, spot ^ 2) for step in range(planes)]
    outs = out_part(spots, gated, held_out, planes, tuple(range(planes)))
    got = [permute(away, over_core) for away, _, _ in outs]

    def send_of(step):
        return outs[step][1].astype(f32) + got[step][:rows].astype(f32)

    send = send_of(0)
    aside = permute((send[half:] * theirs[0][half:]).astype(jnp.bfloat16), ring)
    send = send[:half].astype(jnp.bfloat16)
    total = None
    for step in range(planes):
        group = [permute(send, over_y)]
        if step:
            group.append(permute(total.astype(jnp.bfloat16), ring))
        else:
            group.append(aside)
        group = lax.optimization_barrier(group)
        if step + 1 < planes:
            send = send_of(step + 1) * theirs[step + 1]
            if step == 0:
                send = jnp.concatenate([send[:half], send[half:] + group[1].astype(f32)], axis=0)
            send = send.astype(jnp.bfloat16)
        total = outs[step][2].astype(f32) + got[step][rows:].astype(f32)
        if step:
            total = total * mine[step] + group[0].astype(f32) + group[1].astype(f32)
        else:
            total = (
                jnp.concatenate([total[:half] + group[0].astype(f32), total[half:]], axis=0) * mine[0]
            )
    layer_out = (hidden.astype(f32) + total).astype(jnp.bfloat16)

    filled = jnp.dot(place, layer_out, preferred_element_type=f32).astype(jnp.bfloat16)
    received = lax.all_to_all(
        filled.reshape(count, CAP, width), "tensor", split_axis=0, concat_axis=0, tiled=True
    )
    packed = jnp.concatenate([picked, received.reshape(count * CAP, width)], axis=1)
    return (layer_out, packed)


def solution(mesh):
    planar = mesh.shape["dp"] == 1 and mesh.shape["tensor"] == PLANE * GROUPS
    return jax.shard_map(
        on_device_planes if planar else on_device,
        mesh=mesh,
        in_specs=(
            P(("rep", "dp", "tensor"), None),
            P(),
            P(("dp", "tensor"), None),
            P(("dp", "tensor"), None),
            P(("dp", "tensor"), None),
            P(),
            P("tensor", None),
            P(("dp", "tensor"), None),
            P(("dp", "tensor")),
            P(("dp", "tensor")),
            P(("dp", "tensor")),
            P(("dp", "tensor")),
            P(("dp", "tensor"), None),
            P(("rep", "dp"), None),
            P(("rep", "dp", "tensor"), None),
        ),
        out_specs=(P(("rep", "dp", "tensor"), None), P(("rep", "dp", "tensor"), None)),
        check_vma=False,
    )
```

```python
import functools

import jax
import jax.numpy as jnp
from jax import lax
from jax.experimental import pallas as pl
from jax.experimental.pallas import tpu as pltpu
from jax.sharding import PartitionSpec as P

HEAD_DIM = 64
INNER = 8192
HEADS = 128
STATE = 128
GROUPS = 4
BLOCK = 128
CAP = 2


highest = lax.Precision.HIGHEST


def dot_rows(left, right):
    return lax.dot_general(
        left, right, (((1,), (1,)), ((), ())), preferred_element_type=jnp.float32
    )


def rms_rows(values, scale):
    wide = values.astype(jnp.float32)
    meansq = jnp.mean(wide * wide, axis=-1, keepdims=True)
    return (wide * lax.rsqrt(meansq + 1e-05) * scale.astype(jnp.float32)).astype(jnp.bfloat16)


def causal_conv(signal, kernel, segment):
    length = signal.shape[0]
    taps_count = kernel.shape[1]
    result = jnp.zeros(signal.shape, jnp.float32)
    for offset in range(taps_count):
        steps_back = taps_count - 1 - offset
        shifted = jnp.pad(signal, ((steps_back, 0), (0, 0)))[:length]
        shifted_seg = jnp.pad(segment, (steps_back, 0), constant_values=-1)[:length]
        same = (shifted_seg == segment).astype(jnp.float32)
        result = result + shifted * kernel[:, offset][None, :] * same[:, None]
    return result


def state_scan(inputs, deltas, rates, keys_b, queries_c, skips, segment):
    total, heads_n, dim_p = inputs.shape
    count = total // BLOCK
    order = jnp.arange(BLOCK)

    def advance(carry, block):
        state, previous = carry
        block_x, block_dt, block_b, block_c, block_seg = block
        cumul = jnp.cumsum(-rates[None, :] * block_dt, axis=0)
        allowed = (block_seg[:, None] == block_seg[None, :]) & (order[:, None] >= order[None, :])
        gaps = cumul[:, None, :] - cumul[None, :, :]
        decays = jnp.where(
            allowed[:, :, None], jnp.exp(jnp.where(allowed[:, :, None], gaps, 0.0)), 0.0
        )
        scores = jnp.einsum("ihn,jhn->ijh", block_c, block_b, precision=highest)
        mixing = scores * decays * block_dt[None, :, :]
        output = jnp.einsum("ijh,jhp->ihp", mixing, block_x, precision=highest)
        carried = (block_seg == previous).astype(jnp.float32)
        from_state = jnp.einsum("ihn,hpn->ihp", block_c, state, precision=highest)
        output = output + (carried[:, None] * jnp.exp(cumul))[:, :, None] * from_state
        output = output + skips[None, :, None] * block_x
        final_seg = block_seg[BLOCK - 1]
        ending = (block_seg == final_seg).astype(jnp.float32)
        weights_end = jnp.exp(cumul[BLOCK - 1][None, :] - cumul) * block_dt * ending[:, None]
        keeping = (previous == final_seg).astype(jnp.float32)
        fresh = jnp.einsum("jh,jhp,jhn->hpn", weights_end, block_x, block_b, precision=highest)
        state = keeping * jnp.exp(cumul[BLOCK - 1])[:, None, None] * state + fresh
        return ((state, final_seg), output)

    blocks = (
        inputs.reshape(count, BLOCK, heads_n, dim_p),
        deltas.reshape(count, BLOCK, heads_n),
        keys_b.reshape(count, BLOCK, heads_n, -1),
        queries_c.reshape(count, BLOCK, heads_n, -1),
        segment.reshape(count, BLOCK),
    )
    start = (jnp.zeros((heads_n, dim_p, keys_b.shape[-1]), jnp.float32), jnp.array(-1, jnp.int32))
    carry_end, outputs = lax.scan(advance, start, blocks)
    return outputs.reshape(total, heads_n, dim_p)


def mixer_core(tokens, segment, params, head_ids, ssm_raw, conv_bc):
    proj_x, proj_z, taps_x, proj_dt, bias_dt, rates, skips = params
    row_total = tokens.shape[0]
    heads_here = head_ids.shape[0]
    width_bc = GROUPS * STATE
    x_raw = dot_rows(tokens, proj_x).astype(jnp.bfloat16)
    z_raw = dot_rows(tokens, proj_z).astype(jnp.bfloat16)
    dt_raw = dot_rows(tokens, proj_dt).astype(jnp.bfloat16)
    x_act = jax.nn.silu(causal_conv(x_raw.astype(jnp.float32), taps_x.astype(jnp.float32), segment))
    ssm_act = jax.nn.silu(
        causal_conv(ssm_raw.astype(jnp.float32), conv_bc.astype(jnp.float32), segment)
    )
    b_groups = ssm_act[:, :width_bc].reshape(row_total, GROUPS, STATE)
    c_groups = ssm_act[:, width_bc:].reshape(row_total, GROUPS, STATE)
    select = (head_ids[:, None] // (HEADS // GROUPS) == jnp.arange(GROUPS)[None, :]).astype(
        jnp.float32
    )
    b_heads = jnp.einsum("tgn,hg->thn", b_groups, select, precision=highest)
    c_heads = jnp.einsum("tgn,hg->thn", c_groups, select, precision=highest)
    delta = jax.nn.softplus(dt_raw.astype(jnp.float32) + bias_dt.astype(jnp.float32)[None, :])
    scanned = state_scan(
        x_act.reshape(row_total, heads_here, HEAD_DIM),
        delta,
        rates.astype(jnp.float32),
        b_heads,
        c_heads,
        skips.astype(jnp.float32),
        segment,
    )
    return scanned.reshape(row_total, -1) * jax.nn.silu(z_raw.astype(jnp.float32))


def on_device(
    hidden,
    pre_gain,
    in_x,
    in_z,
    conv_x,
    conv_bc,
    bc_weight,
    dt_weight,
    dt_bias,
    decay_rate,
    skip,
    norm_gain,
    out_weight,
    segment_ids,
    destination,
):
    tensor_count = lax.axis_size("tensor")
    group_count = lax.axis_size("dp")
    shard_count = tensor_count * group_count
    tensor_pos = lax.axis_index("tensor")
    heads_each = in_x.shape[0] // HEAD_DIM
    target = destination[:, 0]
    onehot = (target[:, None] == jnp.arange(shard_count, dtype=jnp.int32)[None, :]).astype(
        jnp.int32
    )
    ranks = jnp.sum((jnp.cumsum(onehot, axis=0) - onehot) * onehot, axis=1)
    slot_ids = target * CAP + ranks
    normed = rms_rows(hidden, pre_gain)
    tokens = lax.all_gather(normed, "tensor", axis=0, tiled=True)
    segment = segment_ids.reshape(-1)
    gathered = (
        lax.all_gather(in_x, "dp", axis=0, tiled=True),
        lax.all_gather(in_z, "dp", axis=0, tiled=True),
        lax.all_gather(conv_x, "dp", axis=0, tiled=True),
        lax.all_gather(dt_weight, "dp", axis=0, tiled=True),
        lax.all_gather(dt_bias, "dp", axis=0, tiled=True),
        lax.all_gather(decay_rate, "dp", axis=0, tiled=True),
        lax.all_gather(skip, "dp", axis=0, tiled=True),
        lax.all_gather(norm_gain, "dp", axis=0, tiled=True),
        lax.all_gather(out_weight, "dp", axis=0, tiled=True),
    )
    params = gathered[:7]
    gain_here = gathered[7]
    proj_out = gathered[8]
    head_ids = jnp.concatenate(
        [
            (member * tensor_count + tensor_pos) * heads_each + jnp.arange(heads_each)
            for member in range(group_count)
        ]
    )
    ssm_part = dot_rows(tokens, bc_weight).astype(jnp.bfloat16)
    ssm_raw = lax.all_gather(ssm_part, "tensor", axis=1, tiled=True)
    gated = mixer_core(tokens, segment, params, head_ids, ssm_raw, conv_bc)
    row_total = gated.shape[0]
    heads_here = head_ids.shape[0]
    group_sel = (head_ids[:, None] // (HEADS // GROUPS) == jnp.arange(GROUPS)[None, :]).astype(
        jnp.float32
    )
    by_head = gated.reshape(row_total, heads_here, HEAD_DIM)
    head_sq = jnp.sum(by_head * by_head, axis=2)
    partial_sq = jnp.dot(head_sq, group_sel, precision=highest)
    total_sq = lax.psum(partial_sq, "tensor")
    head_total = jnp.dot(total_sq, group_sel.T, precision=highest)
    head_scale = lax.rsqrt(head_total / (INNER // GROUPS) + 1e-05)
    scaled = (by_head * head_scale[:, :, None]).reshape(row_total, -1)
    inner = (scaled * gain_here.astype(jnp.float32)[None, :]).astype(jnp.bfloat16)
    mixer = lax.psum_scatter(
        jnp.dot(inner, proj_out, preferred_element_type=jnp.float32),
        "tensor",
        scatter_dimension=0,
        tiled=True,
    )
    layer_out = (hidden.astype(jnp.float32) + mixer).astype(jnp.bfloat16)
    joined = jnp.concatenate([hidden, layer_out], axis=1)
    filled = jnp.zeros((shard_count * CAP, joined.shape[1]), jnp.bfloat16).at[slot_ids].set(joined)
    received = lax.all_to_all(
        filled.reshape(shard_count, CAP, joined.shape[1]),
        ("dp", "tensor"),
        split_axis=0,
        concat_axis=0,
        tiled=True,
    )
    packed = received.reshape(shard_count * CAP, -1)
    return (layer_out, packed)


PLANE = 4
VMEM_LIMIT = 9 * 1024 * 1024
NEG = -1e30


def vmem():
    return pl.BlockSpec(memory_space=pltpu.VMEM)


def smem():
    return pl.BlockSpec(memory_space=pltpu.SMEM)


def near(value):
    return pltpu.with_memory_space_constraint(value, pltpu.VMEM)


def far(value):
    return pltpu.with_memory_space_constraint(value, pltpu.MemorySpace.HBM)


def dot_nt(left, right, precision=None):
    return lax.dot_general(
        left, right, (((1,), (1,)), ((), ())), precision=precision, preferred_element_type=jnp.float32
    )


def norm_kernel(spot_ref, *refs, pieces, held):
    gain_ref, small_ref, *rest = refs[sum(pieces) :]
    weights, (normed_ref, bc_ref, dt_ref) = rest[:held], rest[held : held + 3]
    copies = [
        pltpu.make_async_copy(weight, rest[held + 3 + i], rest[-1].at[i])
        for i, weight in enumerate(weights)
    ]
    for copy in copies:
        copy.start()
    width = gain_ref.shape[1]
    step = 1024
    taken = 0
    rows = sum(ref.shape[0] for ref in refs[: pieces[0]])
    for index, parts in enumerate(pieces):
        below = 0
        for ref in refs[taken : taken + parts]:
            high = ref.shape[0]
            start = pl.multiple_of((spot_ref[1] ^ index) * rows + below, high)
            total = jnp.zeros((high, 128), jnp.float32)
            for col in range(0, width, step):
                wide = ref[:, col : col + step].astype(jnp.float32)
                square = wide * wide
                for lane in range(0, step, 128):
                    total = total + square[:, lane : lane + 128]
            scale = lax.rsqrt(jnp.sum(total, axis=1, keepdims=True) / width + 1e-05)
            for col in range(0, width, step):
                wide = ref[:, col : col + step].astype(jnp.float32)
                normed_ref[pl.ds(start, high), col : col + step] = (
                    wide * scale * gain_ref[:, col : col + step].astype(jnp.float32)
                ).astype(jnp.bfloat16)
            below += high
        taken += parts
    result = dot_nt(normed_ref[...], small_ref[...]).astype(jnp.bfloat16)
    half = bc_ref.shape[1]
    bc_ref[...] = result[:, :half]
    dt_ref[...] = result[:, half:].astype(jnp.float32)
    for copy in copies:
        copy.wait()


def norm_plane(spots, blocks, gain, small, late, weights):
    rows, width = sum(part.shape[0] for part in blocks[0]) * PLANE, gain.shape[1]
    flat = [near(part) for block in blocks for part in block]
    return pl.pallas_call(
        functools.partial(
            norm_kernel, pieces=tuple(len(block) for block in blocks), held=len(weights)
        ),
        out_shape=(
            (pltpu.VMEM if late else jax.ShapeDtypeStruct)((rows, width), jnp.bfloat16),
            jax.ShapeDtypeStruct((rows, small.shape[0] - 128), jnp.bfloat16),
            jax.ShapeDtypeStruct((rows, 128), jnp.float32),
            *[pltpu.VMEM(weight.shape, weight.dtype) for weight in weights],
        ),
        in_specs=[smem()]
        + [vmem()] * (len(flat) + 2)
        + [pl.BlockSpec(memory_space=pltpu.MemorySpace.HBM)] * len(weights),
        out_specs=(vmem(),) * (3 + len(weights)),
        scratch_shapes=[pltpu.SemaphoreType.DMA((len(weights),))] if weights else [],
        compiler_params=pltpu.CompilerParams(vmem_limit_bytes=VMEM_LIMIT),
        cost_estimate=pl.CostEstimate(
            flops=1 << 31, bytes_accessed=6 << 20, transcendentals=0
        ),
        name="norm_plane",
    )(spots, *flat, near(gain), near(small), *[far(weight) for weight in weights])


def project_kernel(*refs, planes):
    normed, weights = refs[:planes], refs[planes : planes + 2]
    outs, left = refs[planes + 2 : -1], refs[-1]
    tile = 256
    rows = normed[0].shape[0]
    for index, ref in enumerate(normed):
        left[index * rows : (index + 1) * rows, :] = ref[...]
    for which, weight in enumerate(weights):
        for col in range(0, weight.shape[0], tile):
            result = dot_nt(left[...], weight[col : col + tile, :]).astype(jnp.bfloat16)
            for index in range(planes):
                outs[2 * index + which][:, col : col + tile] = result[index * rows : (index + 1) * rows]


def project_planes(normed, in_x, in_z):
    rows, width = normed[0].shape
    cols = in_x.shape[0]
    count = len(normed)
    outs = pl.pallas_call(
        functools.partial(project_kernel, planes=count),
        out_shape=(jax.ShapeDtypeStruct((rows, cols), jnp.bfloat16),) * (2 * count),
        in_specs=[vmem()] * (count + 2),
        out_specs=(vmem(),) * (2 * count),
        scratch_shapes=[pltpu.VMEM((count * rows, width), jnp.bfloat16)],
        compiler_params=pltpu.CompilerParams(vmem_limit_bytes=VMEM_LIMIT),
        cost_estimate=pl.CostEstimate(
            flops=4 << 30, bytes_accessed=4 << 20, transcendentals=0
        ),
        name="project_planes",
    )(*[near(value) for value in normed], near(in_x), near(in_z))
    return outs[0::2], outs[1::2]


def silu(value):
    return value / (1.0 + jnp.exp(-value))


def scan_kernel(
    spot_ref,
    *refs,
    heads,
    planes,
):
    xs, zs, dts = refs[:planes], refs[planes : 2 * planes], refs[2 * planes : 3 * planes]
    refs = refs[3 * planes :]
    far_pieces = refs[:2]
    (taps_x, taps_bc, masks, bias, marks, keep, head_rows, gain_ref) = refs[2:10]
    weight_ref, gated_ref, square_ref, held_ref = refs[10:14]
    x_all, z_all, dt_all, bc_all, sem = refs[14:]
    held_copy = pltpu.make_async_copy(weight_ref, held_ref, sem)
    held_copy.start()
    z_pos, spot = spot_ref[0], spot_ref[1]
    rows = xs[0].shape[0]
    chans = xs[0].shape[1]
    highest_ = lax.Precision.HIGHEST
    upper = spot >= 2
    x_all[0:8, :] = jnp.zeros((8, chans), jnp.float32)
    bc_all[0:8, :] = jnp.zeros((8, 2 * STATE), jnp.float32)
    for s in range(planes):
        at = pl.multiple_of(lax.rem(z_pos - s + planes, planes) * rows, rows)
        x_all[pl.ds(at + 8, rows), :] = xs[s][...].astype(jnp.float32)
        z_all[pl.ds(at, rows), :] = zs[s][...]
        dt_all[pl.ds(at, rows), :] = dts[s][...]
        one, two = [
            ref[s * rows : (s + 1) * rows, :].astype(jnp.float32) for ref in far_pieces
        ]
        for chip, left, value in (
            (z_pos, 0, jnp.where(upper, two, one)),
            (z_pos + GROUPS, STATE, jnp.where(upper, one, two)),
        ):
            row = lax.rem(lax.div(chip, PLANE // 2) - s + planes, planes) * rows
            row = pl.multiple_of(row, rows)
            bc_all[pl.ds(row + 8, rows), left : left + STATE] = value
    order_i = lax.broadcasted_iota(jnp.int32, (rows, rows), 0)
    order_j = lax.broadcasted_iota(jnp.int32, (rows, rows), 1)
    tri = (order_i >= order_j).astype(jnp.float32)
    lane = lax.broadcasted_iota(jnp.int32, (rows, 128), 1)
    real = lane < heads
    low = lane < HEAD_DIM
    bias_dt, rates = head_rows[0:1, :], head_rows[1:2, :]
    expand = (
        lax.broadcasted_iota(jnp.int32, (128, chans), 0)
        == lax.broadcasted_iota(jnp.int32, (128, chans), 1) // HEAD_DIM
    ).astype(jnp.float32)
    pick_row = lax.broadcasted_iota(jnp.int32, (8, 128), 0)
    lanes_x, lanes_bc = chans // 128, 2 * STATE // 128

    def conv(source, taps, base, count):
        last = taps.shape[0] - 1
        total = source[base + 8 : base + 8 + rows, :] * taps[last : last + 1, :]
        for back in range(1, last + 1):
            same = jnp.concatenate([masks[back - 1, base : base + rows, :]] * count, axis=1)
            total = total + (
                source[base + 8 - back : base + 8 - back + rows, :]
                * taps[last - back : last - back + 1, :]
                * same
            )
        return silu(total)

    state = jnp.zeros((STATE, chans), jnp.float32)
    for p in range(planes):
        base = p * rows
        span = slice(base, base + rows)
        x_act = conv(x_all, taps_x, base, lanes_x)
        bc_act = conv(bc_all, taps_bc, base, lanes_bc).astype(jnp.bfloat16)
        keys, queries = bc_act[:, :STATE], bc_act[:, STATE:]
        raw = dt_all[span, :] + bias_dt
        delta = jnp.maximum(raw, 0.0) + jnp.log1p(jnp.exp(-jnp.abs(raw)))
        delta = jnp.where(real, delta, 0.0)
        cum = jnp.dot(tri, -rates * delta, precision=highest_, preferred_element_type=jnp.float32)
        cum_t = cum.T
        last = cum[rows - 1 : rows, :]
        carried = jnp.where(real, jnp.exp(cum) * marks[0, span, :], 0.0)
        ending = jnp.where(real, jnp.exp(last - cum) * marks[1, span, :] * delta, 0.0)
        decay_end = jnp.where(pick_row == 0, jnp.exp(last) * keep[p : p + 1, :], head_rows[2:3, :])
        decay_end = jnp.where(real[0:8], decay_end, 0.0)
        spread = jnp.dot(
            jnp.concatenate([delta, carried, ending, decay_end], axis=0),
            expand,
            precision=highest_,
            preferred_element_type=jnp.float32,
        )
        delta_x = (spread[:rows] * x_act).astype(jnp.bfloat16)
        end_x = (spread[2 * rows : 3 * rows] * x_act).astype(jnp.bfloat16)
        scores = dot_nt(queries, keys)
        from_state = jnp.dot(queries, state.astype(jnp.bfloat16), preferred_element_type=jnp.float32)
        block_bias = bias[span, :]
        outs = []
        for pair in range(heads // 2):
            both = delta_x[:, pair * 128 : (pair + 1) * 128]
            part = []
            for h in (2 * pair, 2 * pair + 1):
                gap = cum[:, h : h + 1] - cum_t[h : h + 1, :]
                mixing = (jnp.exp(gap + block_bias) * scores).astype(jnp.bfloat16)
                part.append(jnp.dot(mixing, both, preferred_element_type=jnp.float32))
            outs.append(jnp.where(low, part[0], part[1]))
        y = jnp.concatenate(outs, axis=1)
        y = y + spread[rows : 2 * rows] * from_state + spread[3 * rows + 1 : 3 * rows + 2] * x_act
        gated = y * silu(z_all[span, :].astype(jnp.float32))
        square_ref[p : p + 1, :] = dot_nt(
            jnp.ones((8, chans), jnp.float32), gated * gated, precision=highest_
        )[0:1, :]
        gated_ref[span, :] = (gated * gain_ref[...].astype(jnp.float32)).astype(jnp.bfloat16)
        if p + 1 < planes:
            fresh = lax.dot_general(
                keys, end_x, (((0,), (0,)), ((), ())), preferred_element_type=jnp.float32
            )
            state = spread[3 * rows : 3 * rows + 1] * state + fresh
    held_copy.wait()


def pair_kernel(spots, *refs):
    *pieces, out_ref = refs
    count = len(pieces) // 2
    rows, cols = pieces[0].shape
    first = lax.rem(spots[1], 2) == 0
    for i in range(count):
        own, other = pieces[i][...].astype(jnp.float32), pieces[count + i][...].astype(jnp.float32)
        span = slice(i * rows, (i + 1) * rows)
        out_ref[span, :] = jnp.concatenate(
            [jnp.where(first, own, other), jnp.where(first, other, own)], axis=1
        ).astype(jnp.bfloat16)


def pair_pieces(spots, own, other):
    rows, cols = own[0].shape
    return pl.pallas_call(
        pair_kernel,
        out_shape=jax.ShapeDtypeStruct((len(own) * rows, 2 * cols), jnp.bfloat16),
        in_specs=[smem()] + [vmem()] * (2 * len(own)),
        out_specs=vmem(),
        compiler_params=pltpu.CompilerParams(vmem_limit_bytes=VMEM_LIMIT),
        cost_estimate=pl.CostEstimate(flops=1 << 20, bytes_accessed=1 << 20, transcendentals=0),
        name="pair_pieces",
    )(spots, *[near(value) for value in (*own, *other)])


def scan_all(spots, xs, zs, dts, far_pieces, consts, weight, heads):
    planes = len(xs)
    rows, chans = xs[0].shape
    return pl.pallas_call(
        functools.partial(scan_kernel, heads=heads, planes=planes),
        out_shape=(
            jax.ShapeDtypeStruct((planes * rows, chans), jnp.bfloat16),
            jax.ShapeDtypeStruct((8, rows), jnp.float32),
            pltpu.VMEM(weight.shape, weight.dtype),
        ),
        in_specs=[smem()]
        + [vmem()] * (3 * planes + 2 + len(consts))
        + [pl.BlockSpec(memory_space=pltpu.MemorySpace.HBM)],
        out_specs=(vmem(), vmem(), vmem()),
        scratch_shapes=[
            pltpu.VMEM((planes * rows + 8, chans), jnp.float32),
            pltpu.VMEM((planes * rows, chans), jnp.bfloat16),
            pltpu.VMEM((planes * rows, 128), jnp.float32),
            pltpu.VMEM((planes * rows + 8, 2 * STATE), jnp.float32),
            pltpu.SemaphoreType.DMA,
        ],
        compiler_params=pltpu.CompilerParams(vmem_limit_bytes=VMEM_LIMIT),
        cost_estimate=pl.CostEstimate(flops=1 << 30, bytes_accessed=8 << 20, transcendentals=0),
        name="scan_all",
    )(spots, *[near(v) for v in (*xs, *zs, *dts, *far_pieces, *consts)], far(weight))


def out_kernel(spots, gated_ref, weight_ref, *outs, planes, steps):
    rows = gated_ref.shape[0] // planes // PLANE
    level, side = lax.div(spots[1], 2), lax.rem(spots[1], 2)
    parts = []
    for step in steps:
        plane = lax.rem(spots[0] - 1 - step + planes, planes)
        for at_side in (1 - side, side):
            for at_level in (1 - level, level):
                at = pl.multiple_of(((plane * 2 + at_level) * 2 + at_side) * rows, rows)
                parts.append(gated_ref[pl.ds(at, rows), :])
    left = jnp.concatenate(parts, axis=0)
    tile = outs[0].shape[1]
    col = pl.multiple_of(pl.program_id(0) * tile, tile)
    result = jnp.dot(
        left, weight_ref[:, pl.ds(col, tile)], preferred_element_type=jnp.float32
    ).astype(jnp.bfloat16)
    at = 0
    for out in outs:
        out[...] = result[at : at + out.shape[0]]
        at += out.shape[0]


def out_part(spots, gated, weight, planes, steps):
    width = weight.shape[1]
    rows = gated.shape[0] // planes // PLANE
    shapes = [2 * rows, rows, rows] * len(steps)
    tile = 1024
    outs = pl.pallas_call(
        functools.partial(out_kernel, planes=planes, steps=steps),
        grid=(width // tile,),
        out_shape=tuple(pltpu.MemorySpace.HBM((high, width), jnp.bfloat16) for high in shapes),
        in_specs=[smem(), vmem(), vmem()],
        out_specs=tuple(pl.BlockSpec((high, tile), lambda i: (0, i)) for high in shapes),
        compiler_params=pltpu.CompilerParams(vmem_limit_bytes=VMEM_LIMIT),
        cost_estimate=pl.CostEstimate(
            flops=len(steps) << 30, bytes_accessed=len(steps) << 21, transcendentals=0
        ),
        name="out_part",
    )(spots, near(gated), near(weight))
    return [outs[i : i + 3] for i in range(0, len(outs), 3)]


def pick_kernel(spots, *refs, pieces, step, planes, chained):
    parts, out_ref = refs[: sum(pieces)], refs[-1]
    width = out_ref.shape[1]
    code = jnp.concatenate([ref[:, width:] for ref in parts], axis=0).astype(jnp.float32)
    total = code.shape[0]
    rows = total // PLANE
    me = spots[0] * PLANE + spots[1]
    match = code == me.astype(jnp.float32)
    row = lax.broadcasted_iota(jnp.int32, (total, total), 0)
    col = lax.broadcasted_iota(jnp.int32, (total, total), 1)
    before = (row > col) & (row // rows == col // rows)
    rank = jnp.dot(
        before.astype(jnp.bfloat16), match.astype(jnp.bfloat16), preferred_element_type=jnp.float32
    )
    plane = lax.rem(spots[0] - step + planes, planes)
    slot = ((plane * PLANE + (spots[1] ^ (row // rows))) * CAP).astype(jnp.float32) + rank
    select = (match & (slot == col.astype(jnp.float32))).astype(jnp.float32)
    select = select.T[: out_ref.shape[0]].astype(jnp.bfloat16)
    tile = 1024
    for at in range(0, width, tile):
        raw = jnp.concatenate([ref[:, at : at + tile] for ref in parts], axis=0)
        result = jnp.dot(select, raw, preferred_element_type=jnp.float32)
        if chained:
            result = result + refs[-2][:, at : at + tile].astype(jnp.float32)
        out_ref[:, at : at + tile] = result.astype(jnp.bfloat16)


def pick_plane(spots, blocks, earlier, slots, width, step, planes):
    flat = [near(part) for block in blocks for part in block]
    chain = [] if earlier is None else [near(earlier)]
    return pl.pallas_call(
        functools.partial(
            pick_kernel,
            pieces=tuple(len(block) for block in blocks),
            step=step,
            planes=planes,
            chained=bool(chain),
        ),
        out_shape=jax.ShapeDtypeStruct((slots, width), jnp.bfloat16),
        in_specs=[smem()] + [vmem()] * (len(flat) + len(chain)),
        out_specs=vmem(),
        compiler_params=pltpu.CompilerParams(vmem_limit_bytes=VMEM_LIMIT),
        cost_estimate=pl.CostEstimate(flops=1 << 30, bytes_accessed=3 << 20, transcendentals=0),
        name="pick_plane",
    )(spots, *flat, *chain)


def marks_kernel(col_ref, row_ref, masks_ref, bias_ref, marks_ref, keep_ref, padded, *, planes):
    total = col_ref.shape[0]
    rows = total // planes
    col = col_ref[...]
    padded[0:8, :] = jnp.full((8, 128), -1.0, jnp.float32)
    padded[8:, :] = col
    for back in range(1, masks_ref.shape[0] + 1):
        masks_ref[back - 1] = (padded[8 - back : 8 - back + total, :] == col).astype(jnp.float32)
    order = lax.broadcasted_iota(jnp.int32, (rows, rows), 0) >= lax.broadcasted_iota(
        jnp.int32, (rows, rows), 1
    )
    keep_ref[...] = jnp.zeros(keep_ref.shape, jnp.float32)
    for p in range(planes):
        span = slice(p * rows, (p + 1) * rows)
        block = col[span]
        bias_ref[span, :] = jnp.where((block == row_ref[p : p + 1, :]) & order, 0.0, NEG)
        previous = padded[p * rows + 7 : p * rows + 8, :]
        final = block[rows - 1 : rows]
        marks_ref[0, span, :] = (block == previous).astype(jnp.float32)
        marks_ref[1, span, :] = (block == final).astype(jnp.float32)
        keep_ref[p : p + 1, :] = (previous == final).astype(jnp.float32)


def scan_constants(
    segment_ids, conv_x, conv_bc, dt_bias, decay_rate, skip, norm_gain, z_pos, planes
):
    f32 = jnp.float32
    heads = dt_bias.shape[0]
    segment = segment_ids.reshape(-1).astype(f32)
    total = segment.shape[0]
    rows = total // planes
    column = jnp.broadcast_to(segment[:, None], (total, 128))
    lines = jnp.pad(segment.reshape(planes, rows), ((0, 8 - planes), (0, 0)))
    back = conv_x.shape[1] - 1
    masks, bias, marks, keep = pl.pallas_call(
        functools.partial(marks_kernel, planes=planes),
        out_shape=(
            jax.ShapeDtypeStruct((back, total, 128), f32),
            jax.ShapeDtypeStruct((total, rows), f32),
            jax.ShapeDtypeStruct((2, total, 128), f32),
            jax.ShapeDtypeStruct((8, 128), f32),
        ),
        in_specs=[vmem(), vmem()],
        out_specs=(vmem(),) * 4,
        scratch_shapes=[pltpu.VMEM((total + 8, 128), f32)],
        compiler_params=pltpu.CompilerParams(vmem_limit_bytes=VMEM_LIMIT),
        cost_estimate=pl.CostEstimate(flops=1 << 20, bytes_accessed=2 << 20, transcendentals=0),
        name="scan_marks",
    )(column, lines)
    head_rows = jnp.pad(
        jnp.stack([dt_bias, decay_rate, skip]).astype(f32), ((0, 5), (0, 128 - heads))
    )
    width_bc = GROUPS * STATE
    taps_bc = jnp.concatenate(
        [
            lax.dynamic_slice_in_dim(conv_bc, z_pos * STATE + start, STATE, axis=0)
            for start in (0, width_bc)
        ],
        axis=0,
    )
    return (
        conv_x.astype(f32).T,
        taps_bc.astype(f32).T,
        masks,
        bias,
        marks,
        keep,
        head_rows,
        norm_gain[None, :],
    )


def on_device_planes(
    hidden,
    pre_gain,
    in_x,
    in_z,
    conv_x,
    conv_bc,
    bc_weight,
    dt_weight,
    dt_bias,
    decay_rate,
    skip,
    norm_gain,
    out_weight,
    segment_ids,
    destination,
):
    count = lax.axis_size("tensor")
    planes = count // PLANE
    me = lax.axis_index("tensor")
    z_pos, spot = me // PLANE, me % PLANE
    rows, width = hidden.shape
    heads = dt_weight.shape[0]
    every = range(count)
    ring = [(t, (t + PLANE) % count) for t in every]
    over_y = [(t, t ^ 2) for t in every]
    over_core = [(t, t ^ 1) for t in every]

    def permute(value, pairs):
        return lax.ppermute(value, "tensor", pairs)

    f32 = jnp.float32
    small = jnp.concatenate(
        [bc_weight, dt_weight, jnp.zeros((128 - heads, width), dt_weight.dtype)], axis=0
    )
    gain_row = pre_gain[None, :]
    spots = jnp.stack([z_pos, spot]).astype(jnp.int32)

    half = rows // 2
    own = [
        jnp.concatenate(
            [hidden[at : at + half], jnp.broadcast_to(destination[at : at + half].astype(jnp.bfloat16), (half, 128))],
            axis=1,
        )
        for at in (0, half)
    ]
    straight, crossed = [own], []
    straight_core, crossed_core = [], []
    results = []
    picked = None
    peers = []
    spec = (segment_ids, conv_x, conv_bc, dt_bias, decay_rate, skip, norm_gain)

    def send_far(both):
        result = []
        for turn in range(2):
            pairs = []
            for t in every:
                chip, side = t // 2, t % 2
                kind, plane = chip // GROUPS, chip % GROUPS
                pairs.append((t, plane * PLANE + (kind ^ turn) * 2 + side))
            result.append(permute(both, pairs))
        return result

    def over(parts, pairs):
        return [permute(part, pairs) for part in parts]

    def blocks_of(step):
        return [straight[step], straight_core[step], crossed[step], crossed_core[step]]

    def compute(step, *weights):
        return norm_plane(spots, blocks_of(step), gain_row, small, step >= 2, weights)

    def pick(step, earlier):
        return pick_plane(spots, blocks_of(step), earlier, count * CAP, width, step, planes)

    def own_slots(dest):
        target = dest[:, 0]
        onehot = (target[:, None] == jnp.arange(count, dtype=jnp.int32)[None, :]).astype(jnp.int32)
        ranks = jnp.sum((jnp.cumsum(onehot, axis=0) - onehot) * onehot, axis=1)
        slots = target * CAP + ranks
        return (slots[None, :] == jnp.arange(count * CAP)[:, None]).astype(jnp.bfloat16)

    for step in range(planes):
        last = step + 1 == planes
        if step:
            crossed_core.append(over(crossed[step - 1], over_core))
        extra = {}
        if step == 0:
            extra["spec"] = (spec, destination)
        else:
            extra["result"] = compute(step - 1, *([in_x] if last else []))
            picked = pick(step - 1, picked)
        if step == 1:
            extra["consts"] = scan_constants(*spec, z_pos, planes)
            extra["place"] = own_slots(own_dest)
        if step == 2:
            extra["first"] = project_planes([results[0][0], extra["result"][0]], in_x, in_z)
        if step >= 2:
            extra["peer"] = permute(results[step - 2][1], over_core)
        moved = []
        for index, piece in enumerate(straight[step]):
            if last:
                group = [permute(crossed[step - 1][1], ring) if index else permute(piece, over_y)]
            else:
                group = [permute(piece, over_y), permute(piece, ring)]
            group.append(permute(piece, over_core))
            if index:
                group, extra, picked = lax.optimization_barrier((group, extra, picked))
            else:
                group = lax.optimization_barrier(group)
            moved.append(group)
        straight_core.append([group[-1] for group in moved])
        crossed.append([group[0] for group in moved])
        if not last:
            straight.append([group[1] for group in moved])
        if step:
            result = extra["result"]
            results.append(result[:3])
            near_x = result[3] if last else None
        else:
            spec, own_dest = extra["spec"]
        if step == 1:
            consts, place = extra["consts"], extra["place"]
        if step == 2:
            first = extra["first"]
        if step >= 2:
            peers.append(extra["peer"])
    crossed_core.append(over(crossed[-1], over_core))
    *result, near_z = compute(planes - 1, in_z)
    results.append(result)

    normed, pieces, dts = zip(*results)
    peers += over(pieces[2:], over_core)
    both = pair_pieces(spots, pieces, peers)
    both, normed = lax.optimization_barrier((both, normed[2:]))
    far_pieces = send_far(both)
    second = project_planes(normed, near_x, near_z)
    far_pieces, picked = lax.optimization_barrier((far_pieces, pick(planes - 1, picked)))
    xs, zs = [first[i] + second[i] for i in range(2)]
    gated, squares, held_out = scan_all(spots, xs, zs, dts, far_pieces, consts, out_weight, heads)

    squares = squares + permute(squares, over_core)
    squares = squares + permute(squares, over_y)
    scale = lax.rsqrt(squares[:planes].reshape(-1) / (INNER // GROUPS) + 1e-05)

    def scale_of(step, at_spot):
        start = ((z_pos - 1 - step) % planes * PLANE + at_spot) * rows
        return lax.dynamic_slice_in_dim(scale, start, rows)[:, None]

    mine = [scale_of(step, spot) for step in range(planes)]
    theirs = [scale_of(step, spot ^ 2) for step in range(planes)]
    outs = out_part(spots, gated, held_out, planes, tuple(range(planes)))
    got = [permute(away, over_core) for away, _, _ in outs]

    def send_of(step):
        return outs[step][1].astype(f32) + got[step][:rows].astype(f32)

    send = send_of(0)
    aside = permute((send[half:] * theirs[0][half:]).astype(jnp.bfloat16), ring)
    send = send[:half].astype(jnp.bfloat16)
    total = None
    for step in range(planes):
        group = [permute(send, over_y)]
        if step:
            group.append(permute(total.astype(jnp.bfloat16), ring))
        else:
            group.append(aside)
        group = lax.optimization_barrier(group)
        if step + 1 < planes:
            send = send_of(step + 1) * theirs[step + 1]
            if step == 0:
                send = jnp.concatenate([send[:half], send[half:] + group[1].astype(f32)], axis=0)
            send = send.astype(jnp.bfloat16)
        total = outs[step][2].astype(f32) + got[step][rows:].astype(f32)
        if step:
            total = total * mine[step] + group[0].astype(f32) + group[1].astype(f32)
        else:
            total = (
                jnp.concatenate([total[:half] + group[0].astype(f32), total[half:]], axis=0) * mine[0]
            )
    layer_out = (hidden.astype(f32) + total).astype(jnp.bfloat16)

    filled = jnp.dot(place, layer_out, preferred_element_type=f32).astype(jnp.bfloat16)
    received = lax.all_to_all(
        filled.reshape(count, CAP, width), "tensor", split_axis=0, concat_axis=0, tiled=True
    )
    packed = jnp.concatenate([picked, received.reshape(count * CAP, width)], axis=1)
    return (layer_out, packed)


def solution(mesh):
    planar = mesh.shape["dp"] == 1 and mesh.shape["tensor"] == PLANE * GROUPS
    return jax.shard_map(
        on_device_planes if planar else on_device,
        mesh=mesh,
        in_specs=(
            P(("rep", "dp", "tensor"), None),
            P(),
            P(("dp", "tensor"), None),
            P(("dp", "tensor"), None),
            P(("dp", "tensor"), None),
            P(),
            P("tensor", None),
            P(("dp", "tensor"), None),
            P(("dp", "tensor")),
            P(("dp", "tensor")),
            P(("dp", "tensor")),
            P(("dp", "tensor")),
            P(("dp", "tensor"), None),
            P(("rep", "dp"), None),
            P(("rep", "dp", "tensor"), None),
        ),
        out_specs=(P(("rep", "dp", "tensor"), None), P(("rep", "dp", "tensor"), None)),
        check_vma=False,
    )
```

```python
import functools

import jax
import jax.numpy as jnp
from jax import lax
from jax.experimental import pallas as pl
from jax.experimental.pallas import tpu as pltpu
from jax.sharding import PartitionSpec as P

HEAD_DIM = 64
INNER = 8192
HEADS = 128
STATE = 128
GROUPS = 4
BLOCK = 128
CAP = 2


highest = lax.Precision.HIGHEST


def dot_rows(left, right):
    return lax.dot_general(
        left, right, (((1,), (1,)), ((), ())), preferred_element_type=jnp.float32
    )


def rms_rows(values, scale):
    wide = values.astype(jnp.float32)
    meansq = jnp.mean(wide * wide, axis=-1, keepdims=True)
    return (wide * lax.rsqrt(meansq + 1e-05) * scale.astype(jnp.float32)).astype(jnp.bfloat16)


def causal_conv(signal, kernel, segment):
    length = signal.shape[0]
    taps_count = kernel.shape[1]
    result = jnp.zeros(signal.shape, jnp.float32)
    for offset in range(taps_count):
        steps_back = taps_count - 1 - offset
        shifted = jnp.pad(signal, ((steps_back, 0), (0, 0)))[:length]
        shifted_seg = jnp.pad(segment, (steps_back, 0), constant_values=-1)[:length]
        same = (shifted_seg == segment).astype(jnp.float32)
        result = result + shifted * kernel[:, offset][None, :] * same[:, None]
    return result


def state_scan(inputs, deltas, rates, keys_b, queries_c, skips, segment):
    total, heads_n, dim_p = inputs.shape
    count = total // BLOCK
    order = jnp.arange(BLOCK)

    def advance(carry, block):
        state, previous = carry
        block_x, block_dt, block_b, block_c, block_seg = block
        cumul = jnp.cumsum(-rates[None, :] * block_dt, axis=0)
        allowed = (block_seg[:, None] == block_seg[None, :]) & (order[:, None] >= order[None, :])
        gaps = cumul[:, None, :] - cumul[None, :, :]
        decays = jnp.where(
            allowed[:, :, None], jnp.exp(jnp.where(allowed[:, :, None], gaps, 0.0)), 0.0
        )
        scores = jnp.einsum("ihn,jhn->ijh", block_c, block_b, precision=highest)
        mixing = scores * decays * block_dt[None, :, :]
        output = jnp.einsum("ijh,jhp->ihp", mixing, block_x, precision=highest)
        carried = (block_seg == previous).astype(jnp.float32)
        from_state = jnp.einsum("ihn,hpn->ihp", block_c, state, precision=highest)
        output = output + (carried[:, None] * jnp.exp(cumul))[:, :, None] * from_state
        output = output + skips[None, :, None] * block_x
        final_seg = block_seg[BLOCK - 1]
        ending = (block_seg == final_seg).astype(jnp.float32)
        weights_end = jnp.exp(cumul[BLOCK - 1][None, :] - cumul) * block_dt * ending[:, None]
        keeping = (previous == final_seg).astype(jnp.float32)
        fresh = jnp.einsum("jh,jhp,jhn->hpn", weights_end, block_x, block_b, precision=highest)
        state = keeping * jnp.exp(cumul[BLOCK - 1])[:, None, None] * state + fresh
        return ((state, final_seg), output)

    blocks = (
        inputs.reshape(count, BLOCK, heads_n, dim_p),
        deltas.reshape(count, BLOCK, heads_n),
        keys_b.reshape(count, BLOCK, heads_n, -1),
        queries_c.reshape(count, BLOCK, heads_n, -1),
        segment.reshape(count, BLOCK),
    )
    start = (jnp.zeros((heads_n, dim_p, keys_b.shape[-1]), jnp.float32), jnp.array(-1, jnp.int32))
    carry_end, outputs = lax.scan(advance, start, blocks)
    return outputs.reshape(total, heads_n, dim_p)


def mixer_core(tokens, segment, params, head_ids, ssm_raw, conv_bc):
    proj_x, proj_z, taps_x, proj_dt, bias_dt, rates, skips = params
    row_total = tokens.shape[0]
    heads_here = head_ids.shape[0]
    width_bc = GROUPS * STATE
    x_raw = dot_rows(tokens, proj_x).astype(jnp.bfloat16)
    z_raw = dot_rows(tokens, proj_z).astype(jnp.bfloat16)
    dt_raw = dot_rows(tokens, proj_dt).astype(jnp.bfloat16)
    x_act = jax.nn.silu(causal_conv(x_raw.astype(jnp.float32), taps_x.astype(jnp.float32), segment))
    ssm_act = jax.nn.silu(
        causal_conv(ssm_raw.astype(jnp.float32), conv_bc.astype(jnp.float32), segment)
    )
    b_groups = ssm_act[:, :width_bc].reshape(row_total, GROUPS, STATE)
    c_groups = ssm_act[:, width_bc:].reshape(row_total, GROUPS, STATE)
    select = (head_ids[:, None] // (HEADS // GROUPS) == jnp.arange(GROUPS)[None, :]).astype(
        jnp.float32
    )
    b_heads = jnp.einsum("tgn,hg->thn", b_groups, select, precision=highest)
    c_heads = jnp.einsum("tgn,hg->thn", c_groups, select, precision=highest)
    delta = jax.nn.softplus(dt_raw.astype(jnp.float32) + bias_dt.astype(jnp.float32)[None, :])
    scanned = state_scan(
        x_act.reshape(row_total, heads_here, HEAD_DIM),
        delta,
        rates.astype(jnp.float32),
        b_heads,
        c_heads,
        skips.astype(jnp.float32),
        segment,
    )
    return scanned.reshape(row_total, -1) * jax.nn.silu(z_raw.astype(jnp.float32))


def on_device(
    hidden,
    pre_gain,
    in_x,
    in_z,
    conv_x,
    conv_bc,
    bc_weight,
    dt_weight,
    dt_bias,
    decay_rate,
    skip,
    norm_gain,
    out_weight,
    segment_ids,
    destination,
):
    tensor_count = lax.axis_size("tensor")
    group_count = lax.axis_size("dp")
    shard_count = tensor_count * group_count
    tensor_pos = lax.axis_index("tensor")
    heads_each = in_x.shape[0] // HEAD_DIM
    target = destination[:, 0]
    onehot = (target[:, None] == jnp.arange(shard_count, dtype=jnp.int32)[None, :]).astype(
        jnp.int32
    )
    ranks = jnp.sum((jnp.cumsum(onehot, axis=0) - onehot) * onehot, axis=1)
    slot_ids = target * CAP + ranks
    normed = rms_rows(hidden, pre_gain)
    tokens = lax.all_gather(normed, "tensor", axis=0, tiled=True)
    segment = segment_ids.reshape(-1)
    gathered = (
        lax.all_gather(in_x, "dp", axis=0, tiled=True),
        lax.all_gather(in_z, "dp", axis=0, tiled=True),
        lax.all_gather(conv_x, "dp", axis=0, tiled=True),
        lax.all_gather(dt_weight, "dp", axis=0, tiled=True),
        lax.all_gather(dt_bias, "dp", axis=0, tiled=True),
        lax.all_gather(decay_rate, "dp", axis=0, tiled=True),
        lax.all_gather(skip, "dp", axis=0, tiled=True),
        lax.all_gather(norm_gain, "dp", axis=0, tiled=True),
        lax.all_gather(out_weight, "dp", axis=0, tiled=True),
    )
    params = gathered[:7]
    gain_here = gathered[7]
    proj_out = gathered[8]
    head_ids = jnp.concatenate(
        [
            (member * tensor_count + tensor_pos) * heads_each + jnp.arange(heads_each)
            for member in range(group_count)
        ]
    )
    ssm_part = dot_rows(tokens, bc_weight).astype(jnp.bfloat16)
    ssm_raw = lax.all_gather(ssm_part, "tensor", axis=1, tiled=True)
    gated = mixer_core(tokens, segment, params, head_ids, ssm_raw, conv_bc)
    row_total = gated.shape[0]
    heads_here = head_ids.shape[0]
    group_sel = (head_ids[:, None] // (HEADS // GROUPS) == jnp.arange(GROUPS)[None, :]).astype(
        jnp.float32
    )
    by_head = gated.reshape(row_total, heads_here, HEAD_DIM)
    head_sq = jnp.sum(by_head * by_head, axis=2)
    partial_sq = jnp.dot(head_sq, group_sel, precision=highest)
    total_sq = lax.psum(partial_sq, "tensor")
    head_total = jnp.dot(total_sq, group_sel.T, precision=highest)
    head_scale = lax.rsqrt(head_total / (INNER // GROUPS) + 1e-05)
    scaled = (by_head * head_scale[:, :, None]).reshape(row_total, -1)
    inner = (scaled * gain_here.astype(jnp.float32)[None, :]).astype(jnp.bfloat16)
    mixer = lax.psum_scatter(
        jnp.dot(inner, proj_out, preferred_element_type=jnp.float32),
        "tensor",
        scatter_dimension=0,
        tiled=True,
    )
    layer_out = (hidden.astype(jnp.float32) + mixer).astype(jnp.bfloat16)
    joined = jnp.concatenate([hidden, layer_out], axis=1)
    filled = jnp.zeros((shard_count * CAP, joined.shape[1]), jnp.bfloat16).at[slot_ids].set(joined)
    received = lax.all_to_all(
        filled.reshape(shard_count, CAP, joined.shape[1]),
        ("dp", "tensor"),
        split_axis=0,
        concat_axis=0,
        tiled=True,
    )
    packed = received.reshape(shard_count * CAP, -1)
    return (layer_out, packed)


PLANE = 4
VMEM_LIMIT = 9 * 1024 * 1024
NEG = -1e30


def vmem():
    return pl.BlockSpec(memory_space=pltpu.VMEM)


def smem():
    return pl.BlockSpec(memory_space=pltpu.SMEM)


def near(value):
    return pltpu.with_memory_space_constraint(value, pltpu.VMEM)


def far(value):
    return pltpu.with_memory_space_constraint(value, pltpu.MemorySpace.HBM)


def dot_nt(left, right, precision=None):
    return lax.dot_general(
        left, right, (((1,), (1,)), ((), ())), precision=precision, preferred_element_type=jnp.float32
    )


def norm_kernel(spot_ref, *refs, pieces, held):
    gain_ref, small_ref, *rest = refs[sum(pieces) :]
    weights, (normed_ref, bc_ref, dt_ref) = rest[:held], rest[held : held + 3]
    copies = [
        pltpu.make_async_copy(weight, rest[held + 3 + i], rest[-1].at[i])
        for i, weight in enumerate(weights)
    ]
    for copy in copies:
        copy.start()
    width = gain_ref.shape[1]
    step = 1024
    taken = 0
    rows = sum(ref.shape[0] for ref in refs[: pieces[0]])
    for index, parts in enumerate(pieces):
        below = 0
        for ref in refs[taken : taken + parts]:
            high = ref.shape[0]
            start = pl.multiple_of((spot_ref[1] ^ index) * rows + below, high)
            total = jnp.zeros((high, 128), jnp.float32)
            for col in range(0, width, step):
                wide = ref[:, col : col + step].astype(jnp.float32)
                square = wide * wide
                for lane in range(0, step, 128):
                    total = total + square[:, lane : lane + 128]
            scale = lax.rsqrt(jnp.sum(total, axis=1, keepdims=True) / width + 1e-05)
            for col in range(0, width, step):
                wide = ref[:, col : col + step].astype(jnp.float32)
                normed_ref[pl.ds(start, high), col : col + step] = (
                    wide * scale * gain_ref[:, col : col + step].astype(jnp.float32)
                ).astype(jnp.bfloat16)
            below += high
        taken += parts
    result = dot_nt(normed_ref[...], small_ref[...]).astype(jnp.bfloat16)
    half = bc_ref.shape[1]
    bc_ref[...] = result[:, :half]
    dt_ref[...] = result[:, half:].astype(jnp.float32)
    for copy in copies:
        copy.wait()


def norm_plane(spots, blocks, gain, small, late, weights):
    rows, width = sum(part.shape[0] for part in blocks[0]) * PLANE, gain.shape[1]
    flat = [near(part) for block in blocks for part in block]
    return pl.pallas_call(
        functools.partial(
            norm_kernel, pieces=tuple(len(block) for block in blocks), held=len(weights)
        ),
        out_shape=(
            (pltpu.VMEM if late else jax.ShapeDtypeStruct)((rows, width), jnp.bfloat16),
            jax.ShapeDtypeStruct((rows, small.shape[0] - 128), jnp.bfloat16),
            jax.ShapeDtypeStruct((rows, 128), jnp.float32),
            *[pltpu.VMEM(weight.shape, weight.dtype) for weight in weights],
        ),
        in_specs=[smem()]
        + [vmem()] * (len(flat) + 2)
        + [pl.BlockSpec(memory_space=pltpu.MemorySpace.HBM)] * len(weights),
        out_specs=(vmem(),) * (3 + len(weights)),
        scratch_shapes=[pltpu.SemaphoreType.DMA((len(weights),))] if weights else [],
        compiler_params=pltpu.CompilerParams(vmem_limit_bytes=VMEM_LIMIT),
        cost_estimate=pl.CostEstimate(
            flops=1 << 31, bytes_accessed=6 << 20, transcendentals=0
        ),
        name="norm_plane",
    )(spots, *flat, near(gain), near(small), *[far(weight) for weight in weights])


def project_kernel(*refs, planes):
    normed, weights = refs[:planes], refs[planes : planes + 2]
    outs, left = refs[planes + 2 : -1], refs[-1]
    tile = 256
    rows = normed[0].shape[0]
    for index, ref in enumerate(normed):
        left[index * rows : (index + 1) * rows, :] = ref[...]
    for which, weight in enumerate(weights):
        for col in range(0, weight.shape[0], tile):
            result = dot_nt(left[...], weight[col : col + tile, :]).astype(jnp.bfloat16)
            for index in range(planes):
                outs[2 * index + which][:, col : col + tile] = result[index * rows : (index + 1) * rows]


def project_planes(normed, in_x, in_z):
    rows, width = normed[0].shape
    cols = in_x.shape[0]
    count = len(normed)
    outs = pl.pallas_call(
        functools.partial(project_kernel, planes=count),
        out_shape=(jax.ShapeDtypeStruct((rows, cols), jnp.bfloat16),) * (2 * count),
        in_specs=[vmem()] * (count + 2),
        out_specs=(vmem(),) * (2 * count),
        scratch_shapes=[pltpu.VMEM((count * rows, width), jnp.bfloat16)],
        compiler_params=pltpu.CompilerParams(vmem_limit_bytes=VMEM_LIMIT),
        cost_estimate=pl.CostEstimate(
            flops=4 << 30, bytes_accessed=4 << 20, transcendentals=0
        ),
        name="project_planes",
    )(*[near(value) for value in normed], near(in_x), near(in_z))
    return outs[0::2], outs[1::2]


def silu(value):
    return value / (1.0 + jnp.exp(-value))


def scan_kernel(
    spot_ref,
    *refs,
    heads,
    planes,
):
    xs, zs, dts = refs[:planes], refs[planes : 2 * planes], refs[2 * planes : 3 * planes]
    refs = refs[3 * planes :]
    far_pieces = refs[:2]
    (taps_x, taps_bc, masks, bias, marks, keep, head_rows, gain_ref) = refs[2:10]
    weight_ref, gated_ref, square_ref, held_ref = refs[10:14]
    x_all, z_all, dt_all, bc_all, sem = refs[14:]
    held_copy = pltpu.make_async_copy(weight_ref, held_ref, sem)
    held_copy.start()
    z_pos, spot = spot_ref[0], spot_ref[1]
    rows = xs[0].shape[0]
    chans = xs[0].shape[1]
    highest_ = lax.Precision.HIGHEST
    upper = spot >= 2
    x_all[0:8, :] = jnp.zeros((8, chans), jnp.float32)
    bc_all[0:8, :] = jnp.zeros((8, 2 * STATE), jnp.float32)
    for s in range(planes):
        at = pl.multiple_of(lax.rem(z_pos - s + planes, planes) * rows, rows)
        x_all[pl.ds(at + 8, rows), :] = xs[s][...].astype(jnp.float32)
        z_all[pl.ds(at, rows), :] = zs[s][...]
        dt_all[pl.ds(at, rows), :] = dts[s][...]
        one, two = [
            ref[s * rows : (s + 1) * rows, :].astype(jnp.float32) for ref in far_pieces
        ]
        for chip, left, value in (
            (z_pos, 0, jnp.where(upper, two, one)),
            (z_pos + GROUPS, STATE, jnp.where(upper, one, two)),
        ):
            row = lax.rem(lax.div(chip, PLANE // 2) - s + planes, planes) * rows
            row = pl.multiple_of(row, rows)
            bc_all[pl.ds(row + 8, rows), left : left + STATE] = value
    order_i = lax.broadcasted_iota(jnp.int32, (rows, rows), 0)
    order_j = lax.broadcasted_iota(jnp.int32, (rows, rows), 1)
    tri = (order_i >= order_j).astype(jnp.float32)
    lane = lax.broadcasted_iota(jnp.int32, (rows, 128), 1)
    real = lane < heads
    low = lane < HEAD_DIM
    bias_dt, rates = head_rows[0:1, :], head_rows[1:2, :]
    expand = (
        lax.broadcasted_iota(jnp.int32, (128, chans), 0)
        == lax.broadcasted_iota(jnp.int32, (128, chans), 1) // HEAD_DIM
    ).astype(jnp.float32)
    pick_row = lax.broadcasted_iota(jnp.int32, (8, 128), 0)
    lanes_x, lanes_bc = chans // 128, 2 * STATE // 128

    def conv(source, taps, base, count):
        last = taps.shape[0] - 1
        total = source[base + 8 : base + 8 + rows, :] * taps[last : last + 1, :]
        for back in range(1, last + 1):
            same = jnp.concatenate([masks[back - 1, base : base + rows, :]] * count, axis=1)
            total = total + (
                source[base + 8 - back : base + 8 - back + rows, :]
                * taps[last - back : last - back + 1, :]
                * same
            )
        return silu(total)

    state = jnp.zeros((STATE, chans), jnp.float32)
    for p in range(planes):
        base = p * rows
        span = slice(base, base + rows)
        x_act = conv(x_all, taps_x, base, lanes_x)
        bc_act = conv(bc_all, taps_bc, base, lanes_bc).astype(jnp.bfloat16)
        keys, queries = bc_act[:, :STATE], bc_act[:, STATE:]
        raw = dt_all[span, :] + bias_dt
        delta = jnp.maximum(raw, 0.0) + jnp.log1p(jnp.exp(-jnp.abs(raw)))
        delta = jnp.where(real, delta, 0.0)
        cum = jnp.dot(tri, -rates * delta, precision=highest_, preferred_element_type=jnp.float32)
        cum_t = cum.T
        last = cum[rows - 1 : rows, :]
        carried = jnp.where(real, jnp.exp(cum) * marks[0, span, :], 0.0)
        ending = jnp.where(real, jnp.exp(last - cum) * marks[1, span, :] * delta, 0.0)
        decay_end = jnp.where(pick_row == 0, jnp.exp(last) * keep[p : p + 1, :], head_rows[2:3, :])
        decay_end = jnp.where(real[0:8], decay_end, 0.0)
        spread = jnp.dot(
            jnp.concatenate([delta, carried, ending, decay_end], axis=0),
            expand,
            precision=highest_,
            preferred_element_type=jnp.float32,
        )
        delta_x = (spread[:rows] * x_act).astype(jnp.bfloat16)
        end_x = (spread[2 * rows : 3 * rows] * x_act).astype(jnp.bfloat16)
        scores = dot_nt(queries, keys)
        from_state = jnp.dot(queries, state.astype(jnp.bfloat16), preferred_element_type=jnp.float32)
        block_bias = bias[span, :]
        outs = []
        for pair in range(heads // 2):
            both = delta_x[:, pair * 128 : (pair + 1) * 128]
            part = []
            for h in (2 * pair, 2 * pair + 1):
                gap = cum[:, h : h + 1] - cum_t[h : h + 1, :]
                mixing = (jnp.exp(gap + block_bias) * scores).astype(jnp.bfloat16)
                part.append(jnp.dot(mixing, both, preferred_element_type=jnp.float32))
            outs.append(jnp.where(low, part[0], part[1]))
        y = jnp.concatenate(outs, axis=1)
        y = y + spread[rows : 2 * rows] * from_state + spread[3 * rows + 1 : 3 * rows + 2] * x_act
        gated = y * silu(z_all[span, :].astype(jnp.float32))
        square_ref[p : p + 1, :] = dot_nt(
            jnp.ones((8, chans), jnp.float32), gated * gated, precision=highest_
        )[0:1, :]
        gated_ref[span, :] = (gated * gain_ref[...].astype(jnp.float32)).astype(jnp.bfloat16)
        if p + 1 < planes:
            fresh = lax.dot_general(
                keys, end_x, (((0,), (0,)), ((), ())), preferred_element_type=jnp.float32
            )
            state = spread[3 * rows : 3 * rows + 1] * state + fresh
    held_copy.wait()


def pair_kernel(spots, *refs):
    *pieces, out_ref = refs
    count = len(pieces) // 2
    rows, cols = pieces[0].shape
    first = lax.rem(spots[1], 2) == 0
    for i in range(count):
        own, other = pieces[i][...].astype(jnp.float32), pieces[count + i][...].astype(jnp.float32)
        span = slice(i * rows, (i + 1) * rows)
        out_ref[span, :] = jnp.concatenate(
            [jnp.where(first, own, other), jnp.where(first, other, own)], axis=1
        ).astype(jnp.bfloat16)


def pair_pieces(spots, own, other):
    rows, cols = own[0].shape
    return pl.pallas_call(
        pair_kernel,
        out_shape=jax.ShapeDtypeStruct((len(own) * rows, 2 * cols), jnp.bfloat16),
        in_specs=[smem()] + [vmem()] * (2 * len(own)),
        out_specs=vmem(),
        compiler_params=pltpu.CompilerParams(vmem_limit_bytes=VMEM_LIMIT),
        cost_estimate=pl.CostEstimate(flops=1 << 20, bytes_accessed=1 << 20, transcendentals=0),
        name="pair_pieces",
    )(spots, *[near(value) for value in (*own, *other)])


def scan_all(spots, xs, zs, dts, far_pieces, consts, weight, heads):
    planes = len(xs)
    rows, chans = xs[0].shape
    return pl.pallas_call(
        functools.partial(scan_kernel, heads=heads, planes=planes),
        out_shape=(
            jax.ShapeDtypeStruct((planes * rows, chans), jnp.bfloat16),
            jax.ShapeDtypeStruct((8, rows), jnp.float32),
            pltpu.VMEM(weight.shape, weight.dtype),
        ),
        in_specs=[smem()]
        + [vmem()] * (3 * planes + 2 + len(consts))
        + [pl.BlockSpec(memory_space=pltpu.MemorySpace.HBM)],
        out_specs=(vmem(), vmem(), vmem()),
        scratch_shapes=[
            pltpu.VMEM((planes * rows + 8, chans), jnp.float32),
            pltpu.VMEM((planes * rows, chans), jnp.bfloat16),
            pltpu.VMEM((planes * rows, 128), jnp.float32),
            pltpu.VMEM((planes * rows + 8, 2 * STATE), jnp.float32),
            pltpu.SemaphoreType.DMA,
        ],
        compiler_params=pltpu.CompilerParams(vmem_limit_bytes=VMEM_LIMIT),
        cost_estimate=pl.CostEstimate(flops=1 << 30, bytes_accessed=8 << 20, transcendentals=0),
        name="scan_all",
    )(spots, *[near(v) for v in (*xs, *zs, *dts, *far_pieces, *consts)], far(weight))


def out_kernel(spots, gated_ref, weight_ref, *outs, planes, steps):
    rows = gated_ref.shape[0] // planes // PLANE
    level, side = lax.div(spots[1], 2), lax.rem(spots[1], 2)
    parts = []
    for step in steps:
        plane = lax.rem(spots[0] - 1 - step + planes, planes)
        for at_side in (1 - side, side):
            for at_level in (1 - level, level):
                at = pl.multiple_of(((plane * 2 + at_level) * 2 + at_side) * rows, rows)
                parts.append(gated_ref[pl.ds(at, rows), :])
    left = jnp.concatenate(parts, axis=0)
    tile = outs[0].shape[1]
    col = pl.multiple_of(pl.program_id(0) * tile, tile)
    result = jnp.dot(
        left, weight_ref[:, pl.ds(col, tile)], preferred_element_type=jnp.float32
    ).astype(jnp.bfloat16)
    at = 0
    for out in outs:
        out[...] = result[at : at + out.shape[0]]
        at += out.shape[0]


def out_part(spots, gated, weight, planes, steps):
    width = weight.shape[1]
    rows = gated.shape[0] // planes // PLANE
    shapes = [2 * rows, rows, rows] * len(steps)
    tile = 1024
    outs = pl.pallas_call(
        functools.partial(out_kernel, planes=planes, steps=steps),
        grid=(width // tile,),
        out_shape=tuple(pltpu.MemorySpace.HBM((high, width), jnp.bfloat16) for high in shapes),
        in_specs=[smem(), vmem(), vmem()],
        out_specs=tuple(pl.BlockSpec((high, tile), lambda i: (0, i)) for high in shapes),
        compiler_params=pltpu.CompilerParams(vmem_limit_bytes=VMEM_LIMIT),
        cost_estimate=pl.CostEstimate(
            flops=len(steps) << 30, bytes_accessed=len(steps) << 21, transcendentals=0
        ),
        name="out_part",
    )(spots, near(gated), near(weight))
    return [outs[i : i + 3] for i in range(0, len(outs), 3)]


def pick_kernel(spots, *refs, pieces, step, planes, chained):
    parts, out_ref = refs[: sum(pieces)], refs[-1]
    width = out_ref.shape[1]
    code = jnp.concatenate([ref[:, width:] for ref in parts], axis=0).astype(jnp.float32)
    total = code.shape[0]
    rows = total // PLANE
    me = spots[0] * PLANE + spots[1]
    match = code == me.astype(jnp.float32)
    row = lax.broadcasted_iota(jnp.int32, (total, total), 0)
    col = lax.broadcasted_iota(jnp.int32, (total, total), 1)
    before = (row > col) & (row // rows == col // rows)
    rank = jnp.dot(
        before.astype(jnp.bfloat16), match.astype(jnp.bfloat16), preferred_element_type=jnp.float32
    )
    plane = lax.rem(spots[0] - step + planes, planes)
    slot = ((plane * PLANE + (spots[1] ^ (row // rows))) * CAP).astype(jnp.float32) + rank
    select = (match & (slot == col.astype(jnp.float32))).astype(jnp.float32)
    select = select.T[: out_ref.shape[0]].astype(jnp.bfloat16)
    tile = 1024
    for at in range(0, width, tile):
        raw = jnp.concatenate([ref[:, at : at + tile] for ref in parts], axis=0)
        result = jnp.dot(select, raw, preferred_element_type=jnp.float32)
        if chained:
            result = result + refs[-2][:, at : at + tile].astype(jnp.float32)
        out_ref[:, at : at + tile] = result.astype(jnp.bfloat16)


def pick_plane(spots, blocks, earlier, slots, width, step, planes):
    flat = [near(part) for block in blocks for part in block]
    chain = [] if earlier is None else [near(earlier)]
    return pl.pallas_call(
        functools.partial(
            pick_kernel,
            pieces=tuple(len(block) for block in blocks),
            step=step,
            planes=planes,
            chained=bool(chain),
        ),
        out_shape=jax.ShapeDtypeStruct((slots, width), jnp.bfloat16),
        in_specs=[smem()] + [vmem()] * (len(flat) + len(chain)),
        out_specs=vmem(),
        compiler_params=pltpu.CompilerParams(vmem_limit_bytes=VMEM_LIMIT),
        cost_estimate=pl.CostEstimate(flops=1 << 30, bytes_accessed=3 << 20, transcendentals=0),
        name="pick_plane",
    )(spots, *flat, *chain)


def marks_kernel(col_ref, row_ref, masks_ref, bias_ref, marks_ref, keep_ref, padded, *, planes):
    total = col_ref.shape[0]
    rows = total // planes
    col = col_ref[...]
    padded[0:8, :] = jnp.full((8, 128), -1.0, jnp.float32)
    padded[8:, :] = col
    for back in range(1, masks_ref.shape[0] + 1):
        masks_ref[back - 1] = (padded[8 - back : 8 - back + total, :] == col).astype(jnp.float32)
    order = lax.broadcasted_iota(jnp.int32, (rows, rows), 0) >= lax.broadcasted_iota(
        jnp.int32, (rows, rows), 1
    )
    keep_ref[...] = jnp.zeros(keep_ref.shape, jnp.float32)
    for p in range(planes):
        span = slice(p * rows, (p + 1) * rows)
        block = col[span]
        bias_ref[span, :] = jnp.where((block == row_ref[p : p + 1, :]) & order, 0.0, NEG)
        previous = padded[p * rows + 7 : p * rows + 8, :]
        final = block[rows - 1 : rows]
        marks_ref[0, span, :] = (block == previous).astype(jnp.float32)
        marks_ref[1, span, :] = (block == final).astype(jnp.float32)
        keep_ref[p : p + 1, :] = (previous == final).astype(jnp.float32)


def scan_constants(
    segment_ids, conv_x, conv_bc, dt_bias, decay_rate, skip, norm_gain, z_pos, planes
):
    f32 = jnp.float32
    heads = dt_bias.shape[0]
    segment = segment_ids.reshape(-1).astype(f32)
    total = segment.shape[0]
    rows = total // planes
    column = jnp.broadcast_to(segment[:, None], (total, 128))
    lines = jnp.pad(segment.reshape(planes, rows), ((0, 8 - planes), (0, 0)))
    back = conv_x.shape[1] - 1
    masks, bias, marks, keep = pl.pallas_call(
        functools.partial(marks_kernel, planes=planes),
        out_shape=(
            jax.ShapeDtypeStruct((back, total, 128), f32),
            jax.ShapeDtypeStruct((total, rows), f32),
            jax.ShapeDtypeStruct((2, total, 128), f32),
            jax.ShapeDtypeStruct((8, 128), f32),
        ),
        in_specs=[vmem(), vmem()],
        out_specs=(vmem(),) * 4,
        scratch_shapes=[pltpu.VMEM((total + 8, 128), f32)],
        compiler_params=pltpu.CompilerParams(vmem_limit_bytes=VMEM_LIMIT),
        cost_estimate=pl.CostEstimate(flops=1 << 20, bytes_accessed=2 << 20, transcendentals=0),
        name="scan_marks",
    )(column, lines)
    head_rows = jnp.pad(
        jnp.stack([dt_bias, decay_rate, skip]).astype(f32), ((0, 5), (0, 128 - heads))
    )
    width_bc = GROUPS * STATE
    taps_bc = jnp.concatenate(
        [
            lax.dynamic_slice_in_dim(conv_bc, z_pos * STATE + start, STATE, axis=0)
            for start in (0, width_bc)
        ],
        axis=0,
    )
    return (
        conv_x.astype(f32).T,
        taps_bc.astype(f32).T,
        masks,
        bias,
        marks,
        keep,
        head_rows,
        norm_gain[None, :],
    )


def on_device_planes(
    hidden,
    pre_gain,
    in_x,
    in_z,
    conv_x,
    conv_bc,
    bc_weight,
    dt_weight,
    dt_bias,
    decay_rate,
    skip,
    norm_gain,
    out_weight,
    segment_ids,
    destination,
):
    count = lax.axis_size("tensor")
    planes = count // PLANE
    me = lax.axis_index("tensor")
    z_pos, spot = me // PLANE, me % PLANE
    rows, width = hidden.shape
    heads = dt_weight.shape[0]
    every = range(count)
    ring = [(t, (t + PLANE) % count) for t in every]
    over_y = [(t, t ^ 2) for t in every]
    over_core = [(t, t ^ 1) for t in every]

    def permute(value, pairs):
        return lax.ppermute(value, "tensor", pairs)

    f32 = jnp.float32
    small = jnp.concatenate(
        [bc_weight, dt_weight, jnp.zeros((128 - heads, width), dt_weight.dtype)], axis=0
    )
    gain_row = pre_gain[None, :]
    spots = jnp.stack([z_pos, spot]).astype(jnp.int32)

    half = rows // 2
    own = [
        jnp.concatenate(
            [hidden[at : at + half], jnp.broadcast_to(destination[at : at + half].astype(jnp.bfloat16), (half, 128))],
            axis=1,
        )
        for at in (0, half)
    ]
    straight, crossed = [own], []
    straight_core, crossed_core = [], []
    results = []
    picked = None
    peers = []
    spec = (segment_ids, conv_x, conv_bc, dt_bias, decay_rate, skip, norm_gain)

    def send_far(both):
        result = []
        for turn in range(2):
            pairs = []
            for t in every:
                chip, side = t // 2, t % 2
                kind, plane = chip // GROUPS, chip % GROUPS
                pairs.append((t, plane * PLANE + (kind ^ turn) * 2 + side))
            result.append(permute(both, pairs))
        return result

    def over(parts, pairs):
        return [permute(part, pairs) for part in parts]

    def blocks_of(step):
        return [straight[step], straight_core[step], crossed[step], crossed_core[step]]

    def compute(step, *weights):
        return norm_plane(spots, blocks_of(step), gain_row, small, step >= 2, weights)

    def pick(step, earlier):
        return pick_plane(spots, blocks_of(step), earlier, count * CAP, width, step, planes)

    def own_slots(dest):
        target = dest[:, 0]
        onehot = (target[:, None] == jnp.arange(count, dtype=jnp.int32)[None, :]).astype(jnp.int32)
        ranks = jnp.sum((jnp.cumsum(onehot, axis=0) - onehot) * onehot, axis=1)
        slots = target * CAP + ranks
        return (slots[None, :] == jnp.arange(count * CAP)[:, None]).astype(jnp.bfloat16)

    for step in range(planes):
        last = step + 1 == planes
        if step:
            crossed_core.append(over(crossed[step - 1], over_core))
        extra = {}
        if step == 0:
            extra["spec"] = (spec, destination)
        else:
            extra["result"] = compute(step - 1, *([in_x] if last else []))
            picked = pick(step - 1, picked)
        if step == 1:
            extra["consts"] = scan_constants(*spec, z_pos, planes)
            extra["place"] = own_slots(own_dest)
        if step == 2:
            extra["first"] = project_planes([results[0][0], extra["result"][0]], in_x, in_z)
        if step >= 2:
            extra["peer"] = permute(results[step - 2][1], over_core)
        moved = []
        for index, piece in enumerate(straight[step]):
            if last:
                group = [permute(crossed[step - 1][1], ring) if index else permute(piece, over_y)]
            else:
                group = [permute(piece, over_y), permute(piece, ring)]
            group.append(permute(piece, over_core))
            if index:
                group, extra, picked = lax.optimization_barrier((group, extra, picked))
            else:
                group = lax.optimization_barrier(group)
            moved.append(group)
        straight_core.append([group[-1] for group in moved])
        crossed.append([group[0] for group in moved])
        if not last:
            straight.append([group[1] for group in moved])
        if step:
            result = extra["result"]
            results.append(result[:3])
            near_x = result[3] if last else None
        else:
            spec, own_dest = extra["spec"]
        if step == 1:
            consts, place = extra["consts"], extra["place"]
        if step == 2:
            first = extra["first"]
        if step >= 2:
            peers.append(extra["peer"])
    crossed_core.append(over(crossed[-1], over_core))
    *result, near_z = compute(planes - 1, in_z)
    results.append(result)

    normed, pieces, dts = zip(*results)
    peers += over(pieces[2:], over_core)
    both = pair_pieces(spots, pieces, peers)
    both, normed, picked = lax.optimization_barrier((both, normed[2:], picked))
    far_pieces = send_far(both)
    second = project_planes(normed, near_x, near_z)
    far_pieces, picked = lax.optimization_barrier((far_pieces, pick(planes - 1, picked)))
    xs, zs = [first[i] + second[i] for i in range(2)]
    gated, squares, held_out = scan_all(spots, xs, zs, dts, far_pieces, consts, out_weight, heads)

    squares = squares + permute(squares, over_core)
    squares = squares + permute(squares, over_y)
    scale = lax.rsqrt(squares[:planes].reshape(-1) / (INNER // GROUPS) + 1e-05)

    def scale_of(step, at_spot):
        start = ((z_pos - 1 - step) % planes * PLANE + at_spot) * rows
        return lax.dynamic_slice_in_dim(scale, start, rows)[:, None]

    mine = [scale_of(step, spot) for step in range(planes)]
    theirs = [scale_of(step, spot ^ 2) for step in range(planes)]
    outs = out_part(spots, gated, held_out, planes, tuple(range(planes)))
    got = [permute(away, over_core) for away, _, _ in outs]

    def send_of(step):
        return outs[step][1].astype(f32) + got[step][:rows].astype(f32)

    send = send_of(0)
    aside = permute((send[half:] * theirs[0][half:]).astype(jnp.bfloat16), ring)
    send = send[:half].astype(jnp.bfloat16)
    total = None
    for step in range(planes):
        group = [permute(send, over_y)]
        if step:
            group.append(permute(total.astype(jnp.bfloat16), ring))
        else:
            group.append(aside)
        group = lax.optimization_barrier(group)
        if step + 1 < planes:
            send = send_of(step + 1) * theirs[step + 1]
            if step == 0:
                send = jnp.concatenate([send[:half], send[half:] + group[1].astype(f32)], axis=0)
            send = send.astype(jnp.bfloat16)
        total = outs[step][2].astype(f32) + got[step][rows:].astype(f32)
        if step:
            total = total * mine[step] + group[0].astype(f32) + group[1].astype(f32)
        else:
            total = (
                jnp.concatenate([total[:half] + group[0].astype(f32), total[half:]], axis=0) * mine[0]
            )
    layer_out = (hidden.astype(f32) + total).astype(jnp.bfloat16)

    filled = jnp.dot(place, layer_out, preferred_element_type=f32).astype(jnp.bfloat16)
    received = lax.all_to_all(
        filled.reshape(count, CAP, width), "tensor", split_axis=0, concat_axis=0, tiled=True
    )
    packed = jnp.concatenate([picked, received.reshape(count * CAP, width)], axis=1)
    return (layer_out, packed)


def solution(mesh):
    planar = mesh.shape["dp"] == 1 and mesh.shape["tensor"] == PLANE * GROUPS
    return jax.shard_map(
        on_device_planes if planar else on_device,
        mesh=mesh,
        in_specs=(
            P(("rep", "dp", "tensor"), None),
            P(),
            P(("dp", "tensor"), None),
            P(("dp", "tensor"), None),
            P(("dp", "tensor"), None),
            P(),
            P("tensor", None),
            P(("dp", "tensor"), None),
            P(("dp", "tensor")),
            P(("dp", "tensor")),
            P(("dp", "tensor")),
            P(("dp", "tensor")),
            P(("dp", "tensor"), None),
            P(("rep", "dp"), None),
            P(("rep", "dp", "tensor"), None),
        ),
        out_specs=(P(("rep", "dp", "tensor"), None), P(("rep", "dp", "tensor"), None)),
        check_vma=False,
    )
```
